32 devices in a mesh: dp: 8 (over y, x, core), tensor: 4 (over z).
Axes of the slice: x: 2, y: 2, z: 4, core: 2. Of those that a mesh axis runs over, the one named last changes fastest.
Arguments:
- inputs: bfloat16 [256, 4096], P(('dp', 'tensor')), may hold values from -6 to 6
- block_values: bfloat16 [4, 40, 64, 64], P('tensor', 'dp'), may hold values from -0.1875 to 0.1875
- block_slot: int32 [4, 40], P('tensor', 'dp'), may hold values from -1 to 895, as said below
- grad_out: bfloat16 [256, 3584], P('dp', 'tensor'), may hold values from -6 to 6
Outputs:
- outputs: bfloat16 [256, 3584], P('dp', 'tensor')
- grad_in: bfloat16 [256, 4096], P(('dp', 'tensor'))
The draws below stay inside these ranges and needn't reach their ends.
Inputs may be any that keep to these rules, and one draw needn't show every extreme that they name: `block_slot`: A tensor shard's slots hold distinct block positions row * 14 + col, or -1 for an empty slot; empty slots come after all filled ones; a shard fills at least 13 of its 40 slots, in every draw some shard fills all of them and some shard leaves a slot empty.
All inputs are finite; a program needn't handle non-finite values.
Results may differ from the reference program's by a relative error of at most 0.022.
Values may be sent and summed in bfloat16 or wider, within the bound.
No kernel may reach another device: no remote copies, remote signals or barrier semaphores. Data moves between devices by JAX's collectives and lax.ppermute only.
A program may use at most 128 MiB of HBM per device.

```python
import jax
import jax.numpy as jnp
from jax import lax

BLK = 64
D = 4096
FS = 896
FF = 3584
TOKENS = 256
CAP = 40
DBLK = 64
FBLK = 14
POSITIONS = 896
N_TENSOR = 4


def draw_block_slot(key, part):
    key_perm, key_count, key_full = jax.random.split(key, 3)
    shard_keys = jax.random.split(key_perm, N_TENSOR)
    chosen = jax.vmap(lambda k: jax.random.permutation(k, POSITIONS)[:CAP])(shard_keys).astype(jnp.int32)
    full_shard = jax.random.randint(key_full, (), 0, N_TENSOR)
    last_key = jax.random.fold_in(key_full, 7)
    others = jax.random.permutation(last_key, POSITIONS - 1)[:CAP - 1].astype(jnp.int32)
    full_row = jnp.concatenate([others, jnp.full((1,), POSITIONS - 1, jnp.int32)])
    shard_ids = jnp.arange(N_TENSOR)
    chosen = jnp.where((shard_ids == full_shard)[:, None], full_row[None, :], chosen)
    counts = jax.random.randint(key_count, (N_TENSOR,), CAP // 3, CAP + 1)
    counts = jnp.where(shard_ids == full_shard, CAP, counts)
    counts = jnp.where(shard_ids == (full_shard + 1) % N_TENSOR, CAP // 3, counts)
    filled = jnp.arange(CAP)[None, :] < counts[:, None]
    return jnp.where(filled, chosen, -1).astype(jnp.int32)


def shard_levels(rng, extent, pieces, smallest, largest):
    level = 1.0
    for position, blocks in pieces:
        heights = jax.random.uniform(jax.random.fold_in(jax.random.fold_in(rng, 6), position), (blocks,), jnp.float32, smallest / len(pieces), largest / len(pieces))
        level = level * jnp.repeat(jnp.exp(heights), extent[position] // blocks).reshape((-1,) + (1,) * (len(extent) - 1 - position))
    return level


def bell_draw(rng, extent, deviation, limit, cuts=(), held_as=jnp.bfloat16):
    values = deviation * jax.random.normal(rng, extent, jnp.float32)
    if cuts:
        values = values * shard_levels(rng, extent, cuts, -0.22, 0.18)
    return jnp.clip(values, -limit, limit).astype(held_as)


def setup_inputs(seed: int = 0) -> dict:
    arg_keys = jax.random.split(jax.random.key(seed), 5)
    inputs = bell_draw(arg_keys[0], (TOKENS, D), 1.0, 6.0, ((0, 32),))
    block_values = bell_draw(arg_keys[1], (N_TENSOR, CAP, BLK, BLK), (D // 4) ** -0.5, 0.1875, ((0, 4), (1, 8)))
    block_slot = draw_block_slot(jax.random.fold_in(arg_keys[4], 71), 0)
    grad_out = bell_draw(arg_keys[3], (TOKENS, FF), 1.0, 6.0, ((0, 8), (1, 4)))
    return dict(inputs=inputs, block_values=block_values, block_slot=block_slot, grad_out=grad_out)


def shard_weight(values, slots):
    target = jnp.where(slots >= 0, slots, POSITIONS).astype(jnp.int32)
    dense_blocks = jnp.zeros((POSITIONS + 1, BLK, BLK), jnp.bfloat16).at[target].set(values)
    dense_blocks = dense_blocks[:POSITIONS].reshape(DBLK, FBLK, BLK, BLK)
    return dense_blocks.transpose(0, 2, 1, 3).reshape(D, FS)


def reference(inputs, block_values, block_slot, grad_out):
    shards = [shard_weight(block_values[t], block_slot[t]) for t in range(N_TENSOR)]
    weight = jnp.concatenate(shards, axis=1)
    outputs = jnp.dot(inputs, weight, preferred_element_type=jnp.float32).astype(jnp.bfloat16)
    total = jnp.zeros((TOKENS, D), jnp.float32)
    for t in range(N_TENSOR):
        cotangent = grad_out[:, t * FS:(t + 1) * FS]
        partial_value = jnp.dot(cotangent, shards[t].T, preferred_element_type=jnp.float32).astype(jnp.bfloat16)
        partial_value = lax.optimization_barrier(partial_value)
        total = total + partial_value.astype(jnp.float32)
    return outputs, total.astype(jnp.bfloat16)
```

```python
import functools

import jax
import jax.numpy as jnp
from jax import lax
from jax.experimental import pallas as pl
from jax.experimental.pallas import tpu as pltpu
from jax.sharding import PartitionSpec as P

VMEM = pl.BlockSpec(memory_space=pltpu.VMEM)
SMEM = pl.BlockSpec(memory_space=pltpu.SMEM)
LIMIT = 48 * 1024 * 1024


def pack_kernel(count, row_count, col_count, slots, values, packed):
    side = values.shape[2]
    pairs = packed.shape[0]
    lane = lax.broadcasted_iota(jnp.int32, (side, side), 1)
    line = lax.broadcasted_iota(jnp.int32, (side, side), 0)
    head = jnp.zeros((side, side), jnp.float32)
    for j in range(count):
        p = slots[0, j]
        row = jnp.where(p >= 0, p // col_count, row_count)
        col = jnp.where(p >= 0, p % col_count, col_count)
        here = jnp.where(line == 0, row, col).astype(jnp.float32)
        head = jnp.where(lane == j, here, head)
    head = head.astype(jnp.bfloat16)
    for k in range(pairs):
        left = values[0, k]
        right = values[0, k + pairs] if k + pairs < count else head
        packed[k] = jnp.concatenate([left, right], axis=1)


def load_ids(gathered, ids_vmem, ids, sem):
    side = gathered.shape[2]
    head = gathered[:, gathered.shape[1] - 1, 0:16, :].astype(jnp.float32).astype(jnp.int32)
    ids_vmem[...] = head[:, 0:8, :]
    copy = pltpu.make_async_copy(ids_vmem, ids, sem)
    copy.start()
    return copy


def over(n, body):
    if n <= 8:
        for d in range(n):
            body(d)
    else:
        def step(d, carry):
            body(d)
            return carry
        lax.fori_loop(0, n, step, 0)


def backward_kernel(count, n_tensor, gathered, cot, *rest):
    outs = rest[:n_tensor]
    ids_vmem, ids, cot_left, cot_right, prod, acc, sem = rest[n_tensor:]
    n_dp, pairs, side, _ = gathered.shape
    col_count = cot_left.shape[0] - 1
    row_count = acc.shape[0] - 1
    copy = load_ids(gathered, ids_vmem, ids, sem)
    acc[...] = jnp.zeros_like(acc)
    zero = jnp.zeros((cot.shape[0], side), jnp.bfloat16)
    for c in range(col_count):
        part = cot[:, c * side:(c + 1) * side]
        cot_left[c] = jnp.concatenate([part, zero], axis=1)
        cot_right[c] = jnp.concatenate([zero, part], axis=1)
    both = jnp.concatenate([zero, zero], axis=1)
    cot_left[col_count] = both
    cot_right[col_count] = both
    copy.wait()
    rows = cot.shape[0]

    def multiply(d):
        for k in range(pairs):
            left = cot_left[ids[d, 1, side + k]]
            if k + pairs < count:
                right = cot_right[ids[d, 1, side + k + pairs]]
            else:
                right = both
            lhs = jnp.concatenate([left, right], axis=0)
            prod[d * pairs + k] = lax.dot_general(
                lhs, gathered[d, k], (((1,), (1,)), ((), ())), preferred_element_type=jnp.float32
            )

    def add(d):
        for k in range(pairs):
            acc[ids[d, 0, side + k]] += prod[d * pairs + k, 0:rows, :]
            if k + pairs < count:
                acc[ids[d, 0, side + k + pairs]] += prod[d * pairs + k, rows:2 * rows, :]

    over(n_dp, multiply)
    over(n_dp, add)
    me = lax.axis_index("tensor")
    share = rows // n_tensor
    for k in range(n_tensor):
        start = pl.multiple_of(lax.rem(me + k, n_tensor) * share, share)
        for r in range(0, row_count, 2):
            pair = jnp.concatenate(
                [acc[r, pl.ds(start, share), :], acc[r + 1, pl.ds(start, share), :]], axis=1
            )
            outs[k][:, r * side:(r + 2) * side] = pair.astype(jnp.bfloat16)


def forward_kernel(count, n_tensor, gathered, *rest):
    tokens = rest[:n_tensor]
    out = rest[n_tensor]
    ids_vmem, ids, blocks, prod, acc, stage, sem = rest[n_tensor + 1:]
    n_dp, pairs, side, _ = gathered.shape
    row_count = blocks.shape[0] - 1
    col_count = acc.shape[0] - 1
    rows = blocks.shape[1]
    share = rows // n_tensor
    copy = load_ids(gathered, ids_vmem, ids, sem)
    acc[...] = jnp.zeros_like(acc)
    for r in range(row_count):
        parts = [tokens[k][:, r * side:(r + 1) * side].astype(jnp.float32) for k in range(n_tensor)]
        blocks[r] = jnp.concatenate(parts, axis=0).astype(jnp.bfloat16)
    blocks[row_count] = jnp.zeros((rows, side), jnp.bfloat16)
    copy.wait()

    def multiply(d):
        for k in range(pairs):
            left = blocks[ids[d, 0, side + k]]
            right = blocks[ids[d, 0, side + k + pairs]] if k + pairs < count else jnp.zeros_like(left)
            lhs = jnp.concatenate([left, right], axis=0)
            prod[d * pairs + k] = jnp.dot(lhs, gathered[d, k], preferred_element_type=jnp.float32)

    lane = lax.broadcasted_iota(jnp.int32, (rows, 2 * side), 1)

    def add(d):
        for k in range(pairs):
            acc[ids[d, 1, side + k]] += jnp.where(lane < side, prod[d * pairs + k, 0:rows, :], 0.0)
            if k + pairs < count:
                acc[ids[d, 1, side + k + pairs]] += jnp.where(
                    lane >= side, prod[d * pairs + k, rows:2 * rows, :], 0.0
                )

    over(n_dp, multiply)
    over(n_dp, add)
    me = lax.axis_index("tensor")
    for k in range(n_tensor):
        start = pl.multiple_of(lax.rem(me - k + n_tensor, n_tensor) * share, share)
        for c in range(0, col_count, 2):
            sums = []
            for i in (c, c + 1):
                value = acc[i, k * share:(k + 1) * share, :]
                sums.append(value[:, :side] + value[:, side:])
            stage[pl.ds(start, share), c * side:(c + 2) * side] = jnp.concatenate(sums, axis=1)
    out[...] = stage[...].astype(jnp.bfloat16)


def on_device(n_dp, n_tensor, inputs, block_values, block_slot, grad_out):
    share, width = inputs.shape
    rows, hidden = grad_out.shape
    _, count, side, _ = block_values.shape
    row_count, col_count = width // side, hidden // side
    pairs = count // 2 + 1
    bf16, f32, i32 = jnp.bfloat16, jnp.float32, jnp.int32

    def shift(value, k):
        return lax.ppermute(value, "tensor", [(i, (i + k) % n_tensor) for i in range(n_tensor)])

    tokens = [inputs] + [shift(inputs, k) for k in range(1, n_tensor)]
    packed = pl.pallas_call(
        functools.partial(pack_kernel, count, row_count, col_count),
        out_shape=jax.ShapeDtypeStruct((pairs, side, 2 * side), bf16),
        in_specs=[SMEM, VMEM],
        out_specs=VMEM,
    )(block_slot, block_values)
    gathered = lax.all_gather(packed, "dp", axis=0, tiled=False)
    total = n_dp * pairs
    ids = [
        pltpu.VMEM((n_dp, 8, 2 * side), i32),
        pltpu.SMEM((n_dp, 8, 2 * side), i32),
    ]
    partial_sums = pl.pallas_call(
        functools.partial(backward_kernel, count, n_tensor),
        out_shape=[jax.ShapeDtypeStruct((share, width), bf16)] * n_tensor,
        in_specs=[VMEM] * 2,
        out_specs=[VMEM] * n_tensor,
        scratch_shapes=ids + [
            pltpu.VMEM((col_count + 1, rows, 2 * side), bf16),
            pltpu.VMEM((col_count + 1, rows, 2 * side), bf16),
            pltpu.VMEM((total, 2 * rows, side), f32),
            pltpu.VMEM((row_count + 1, rows, side), f32),
            pltpu.SemaphoreType.DMA,
        ],
        compiler_params=pltpu.CompilerParams(vmem_limit_bytes=LIMIT),
    )(gathered, grad_out)
    arrived = [partial_sums[0]] + [shift(partial_sums[k], k) for k in range(1, n_tensor)]
    outputs = pl.pallas_call(
        functools.partial(forward_kernel, count, n_tensor),
        out_shape=jax.ShapeDtypeStruct((rows, hidden), bf16),
        in_specs=[VMEM] * (1 + n_tensor),
        out_specs=VMEM,
        scratch_shapes=ids + [
            pltpu.VMEM((row_count + 1, rows, side), bf16),
            pltpu.VMEM((total, 2 * rows, 2 * side), f32),
            pltpu.VMEM((col_count + 1, rows, 2 * side), f32),
            pltpu.VMEM((rows, hidden), f32),
            pltpu.SemaphoreType.DMA,
        ],
        compiler_params=pltpu.CompilerParams(vmem_limit_bytes=LIMIT),
    )(gathered, *tokens)
    total_grad = arrived[0].astype(f32)
    for value in arrived[1:]:
        total_grad = total_grad + value.astype(f32)
    return (outputs, total_grad.astype(bf16))


def solution(mesh):
    placed = (
        P(("dp", "tensor"), None),
        P("tensor", "dp", None, None),
        P("tensor", "dp"),
        P("dp", "tensor"),
    )
    return jax.shard_map(
        functools.partial(on_device, mesh.shape["dp"], mesh.shape["tensor"]),
        mesh=mesh,
        in_specs=placed,
        out_specs=(P("dp", "tensor"), P(("dp", "tensor"), None)),
        check_vma=False,
    )
```

```python
import functools

import jax
import jax.numpy as jnp
from jax import lax
from jax.experimental import pallas as pl
from jax.experimental.pallas import tpu as pltpu
from jax.sharding import PartitionSpec as P

VMEM = pl.BlockSpec(memory_space=pltpu.VMEM)
SMEM = pl.BlockSpec(memory_space=pltpu.SMEM)
LIMIT = 48 * 1024 * 1024


def pack_kernel(count, row_count, col_count, slots, values, packed):
    side = values.shape[2]
    copies, pairs = packed.shape[:2]
    lane = lax.broadcasted_iota(jnp.int32, (side, side), 1)
    line = lax.broadcasted_iota(jnp.int32, (side, side), 0)
    head = jnp.zeros((side, side), jnp.float32)
    for j in range(count):
        p = slots[0, j]
        row = jnp.where(p >= 0, p // col_count, row_count)
        col = jnp.where(p >= 0, p % col_count, col_count)
        here = jnp.where(line == 0, row, col).astype(jnp.float32)
        head = jnp.where(lane == j, here, head)
    head = head.astype(jnp.bfloat16)
    for k in range(pairs):
        left = values[0, k]
        right = values[0, k + pairs] if k + pairs < count else head
        tile = jnp.concatenate([left, right], axis=1)
        for i in range(copies):
            packed[i, k] = tile


def load_ids(gathered, ids_vmem, ids, sem):
    side = gathered.shape[2]
    head = gathered[:, gathered.shape[1] - 1, 0:16, :].astype(jnp.float32).astype(jnp.int32)
    ids_vmem[...] = head[:, 0:8, :]
    copy = pltpu.make_async_copy(ids_vmem, ids, sem)
    copy.start()
    return copy


def over(n, body):
    if n <= 8:
        for d in range(n):
            body(d)
    else:
        def step(d, carry):
            body(d)
            return carry
        lax.fori_loop(0, n, step, 0)


def backward_kernel(count, n_tensor, gathered, cot, *rest):
    out, ids_vmem, ids, cot_left, cot_right, prod, acc, sem = rest
    n_dp, pairs, side, _ = gathered.shape
    col_count = cot_left.shape[0] - 1
    row_count = acc.shape[0] - 1
    copy = load_ids(gathered, ids_vmem, ids, sem)
    acc[...] = jnp.zeros_like(acc)
    zero = jnp.zeros((cot.shape[0], side), jnp.bfloat16)
    for c in range(col_count):
        part = cot[:, c * side:(c + 1) * side]
        cot_left[c] = jnp.concatenate([part, zero], axis=1)
        cot_right[c] = jnp.concatenate([zero, part], axis=1)
    both = jnp.concatenate([zero, zero], axis=1)
    cot_left[col_count] = both
    cot_right[col_count] = both
    copy.wait()
    rows = cot.shape[0]

    def multiply(d):
        for k in range(pairs):
            left = cot_left[ids[d, 1, side + k]]
            if k + pairs < count:
                right = cot_right[ids[d, 1, side + k + pairs]]
            else:
                right = both
            lhs = jnp.concatenate([left, right], axis=0)
            prod[d * pairs + k] = lax.dot_general(
                lhs, gathered[d, k], (((1,), (1,)), ((), ())), preferred_element_type=jnp.float32
            )

    def add(d):
        for k in range(pairs):
            acc[ids[d, 0, side + k]] += prod[d * pairs + k, 0:rows, :]
            if k + pairs < count:
                acc[ids[d, 0, side + k + pairs]] += prod[d * pairs + k, rows:2 * rows, :]

    over(n_dp, multiply)
    over(n_dp, add)
    share = rows // n_tensor
    for r in range(0, row_count, 2):
        pair = jnp.concatenate([acc[r], acc[r + 1]], axis=1)
        for k in range(n_tensor):
            part = pair[k * share:(k + 1) * share].astype(jnp.bfloat16)
            out[k, :, r * side:(r + 2) * side] = part


def forward_kernel(count, n_tensor, gathered, *rest):
    tokens = rest[:n_tensor]
    out = rest[n_tensor]
    ids_vmem, ids, blocks, prod, acc, stage, sem = rest[n_tensor + 1:]
    n_dp, pairs, side, _ = gathered.shape
    row_count = blocks.shape[0] - 1
    col_count = acc.shape[0] - 1
    rows = blocks.shape[1]
    share = rows // n_tensor
    copy = load_ids(gathered, ids_vmem, ids, sem)
    acc[...] = jnp.zeros_like(acc)
    for r in range(row_count):
        parts = [tokens[k][:, r * side:(r + 1) * side].astype(jnp.float32) for k in range(n_tensor)]
        blocks[r] = jnp.concatenate(parts, axis=0).astype(jnp.bfloat16)
    blocks[row_count] = jnp.zeros((rows, side), jnp.bfloat16)
    copy.wait()

    def multiply(d):
        for k in range(pairs):
            left = blocks[ids[d, 0, side + k]]
            right = blocks[ids[d, 0, side + k + pairs]] if k + pairs < count else jnp.zeros_like(left)
            lhs = jnp.concatenate([left, right], axis=0)
            prod[d * pairs + k] = jnp.dot(lhs, gathered[d, k], preferred_element_type=jnp.float32)

    lane = lax.broadcasted_iota(jnp.int32, (rows, 2 * side), 1)

    def add(d):
        for k in range(pairs):
            acc[ids[d, 1, side + k]] += jnp.where(lane < side, prod[d * pairs + k, 0:rows, :], 0.0)
            if k + pairs < count:
                acc[ids[d, 1, side + k + pairs]] += jnp.where(
                    lane >= side, prod[d * pairs + k, rows:2 * rows, :], 0.0
                )

    over(n_dp, multiply)
    over(n_dp, add)
    me = lax.axis_index("tensor")
    for k in range(n_tensor):
        start = pl.multiple_of(lax.rem(me - k + n_tensor, n_tensor) * share, share)
        for c in range(0, col_count, 2):
            sums = []
            for i in (c, c + 1):
                value = acc[i, k * share:(k + 1) * share, :]
                sums.append(value[:, :side] + value[:, side:])
            stage[pl.ds(start, share), c * side:(c + 2) * side] = jnp.concatenate(sums, axis=1)
    out[...] = stage[...].astype(jnp.bfloat16)


def on_device(n_dp, n_tensor, inputs, block_values, block_slot, grad_out):
    share, width = inputs.shape
    rows, hidden = grad_out.shape
    _, count, side, _ = block_values.shape
    row_count, col_count = width // side, hidden // side
    pairs = count // 2 + 1
    bf16, f32, i32 = jnp.bfloat16, jnp.float32, jnp.int32

    def shift(value, k):
        return lax.ppermute(value, "tensor", [(i, (i + k) % n_tensor) for i in range(n_tensor)])

    tokens = [inputs] + [shift(inputs, k) for k in range(1, n_tensor)]
    packed = pl.pallas_call(
        functools.partial(pack_kernel, count, row_count, col_count),
        out_shape=jax.ShapeDtypeStruct((n_dp, pairs, side, 2 * side), bf16),
        in_specs=[SMEM, VMEM],
        out_specs=VMEM,
    )(block_slot, block_values)
    gathered = lax.all_to_all(packed, "dp", 0, 0, tiled=True)
    total = n_dp * pairs
    ids = [
        pltpu.VMEM((n_dp, 8, 2 * side), i32),
        pltpu.SMEM((n_dp, 8, 2 * side), i32),
    ]
    partial_sums = pl.pallas_call(
        functools.partial(backward_kernel, count, n_tensor),
        out_shape=jax.ShapeDtypeStruct((n_tensor, share, width), bf16),
        in_specs=[VMEM] * 2,
        out_specs=VMEM,
        scratch_shapes=ids + [
            pltpu.VMEM((col_count + 1, rows, 2 * side), bf16),
            pltpu.VMEM((col_count + 1, rows, 2 * side), bf16),
            pltpu.VMEM((total, 2 * rows, side), f32),
            pltpu.VMEM((row_count + 1, rows, side), f32),
            pltpu.SemaphoreType.DMA,
        ],
        compiler_params=pltpu.CompilerParams(vmem_limit_bytes=LIMIT),
    )(gathered, grad_out)
    arrived = lax.all_to_all(partial_sums, "tensor", 0, 0, tiled=True)
    outputs = pl.pallas_call(
        functools.partial(forward_kernel, count, n_tensor),
        out_shape=jax.ShapeDtypeStruct((rows, hidden), bf16),
        in_specs=[VMEM] * (1 + n_tensor),
        out_specs=VMEM,
        scratch_shapes=ids + [
            pltpu.VMEM((row_count + 1, rows, side), bf16),
            pltpu.VMEM((total, 2 * rows, 2 * side), f32),
            pltpu.VMEM((col_count + 1, rows, 2 * side), f32),
            pltpu.VMEM((rows, hidden), f32),
            pltpu.SemaphoreType.DMA,
        ],
        compiler_params=pltpu.CompilerParams(vmem_limit_bytes=LIMIT),
    )(gathered, *tokens)
    total_grad = arrived[0].astype(f32)
    for k in range(1, n_tensor):
        total_grad = total_grad + arrived[k].astype(f32)
    return (outputs, total_grad.astype(bf16))


def solution(mesh):
    placed = (
        P(("dp", "tensor"), None),
        P("tensor", "dp", None, None),
        P("tensor", "dp"),
        P("dp", "tensor"),
    )
    return jax.shard_map(
        functools.partial(on_device, mesh.shape["dp"], mesh.shape["tensor"]),
        mesh=mesh,
        in_specs=placed,
        out_specs=(P("dp", "tensor"), P(("dp", "tensor"), None)),
        check_vma=False,
    )
```

```python
import functools

import jax
import jax.numpy as jnp
from jax import lax
from jax.experimental import pallas as pl
from jax.experimental.pallas import tpu as pltpu
from jax.sharding import PartitionSpec as P

VMEM = pl.BlockSpec(memory_space=pltpu.VMEM)
SMEM = pl.BlockSpec(memory_space=pltpu.SMEM)
LIMIT = 48 * 1024 * 1024


def pack_kernel(count, row_count, col_count, slots, values, packed):
    side = values.shape[2]
    pairs = packed.shape[1]
    lane = lax.broadcasted_iota(jnp.int32, (side, side), 1)
    line = lax.broadcasted_iota(jnp.int32, (side, side), 0)
    head = jnp.zeros((side, side), jnp.float32)
    for j in range(count):
        p = slots[0, j]
        row = jnp.where(p >= 0, p // col_count, row_count)
        col = jnp.where(p >= 0, p % col_count, col_count)
        here = jnp.where(line == 0, row, col).astype(jnp.float32)
        head = jnp.where(lane == j, here, head)
    head = head.astype(jnp.bfloat16)
    for k in range(pairs):
        left = values[0, k]
        right = values[0, k + pairs] if k + pairs < count else head
        packed[0, k] = jnp.concatenate([left, right], axis=1)


def load_ids(gathered, ids_vmem, ids, sem):
    start = 0
    for part in gathered:
        n, pairs = part.shape[:2]
        head = part[:, pairs - 1, 0:16, :].astype(jnp.float32).astype(jnp.int32)
        ids_vmem[start:start + n] = head[:, 0:8, :]
        start += n
    copy = pltpu.make_async_copy(ids_vmem, ids, sem)
    copy.start()
    return copy


def over(gathered, body):
    start = 0
    for part in gathered:
        n = part.shape[0]
        if n <= 8:
            for d in range(n):
                body(part, d, start + d)
        else:
            def step(d, carry, part=part, start=start):
                body(part, d, start + d)
                return carry
            lax.fori_loop(0, n, step, 0)
        start += n


def backward_kernel(count, n_parts, n_tensor, *refs):
    gathered, cot, outs = refs[:n_parts], refs[n_parts], refs[n_parts + 1:n_parts + 1 + n_tensor]
    ids_vmem, ids, cot_left, cot_right, prod, acc, sem = refs[n_parts + 1 + n_tensor:]
    pairs, side = gathered[0].shape[1:3]
    col_count = cot_left.shape[0] - 1
    row_count = acc.shape[0] - 1
    rows = cot.shape[0]
    copy = load_ids(gathered, ids_vmem, ids, sem)
    acc[...] = jnp.zeros_like(acc)
    zero = jnp.zeros((rows, side), jnp.bfloat16)
    for c in range(col_count):
        part = cot[:, c * side:(c + 1) * side]
        cot_left[c] = jnp.concatenate([part, zero], axis=1)
        cot_right[c] = jnp.concatenate([zero, part], axis=1)
    both = jnp.concatenate([zero, zero], axis=1)
    cot_left[col_count] = both
    cot_right[col_count] = both
    copy.wait()

    def multiply(part, d, i):
        for k in range(pairs):
            left = cot_left[ids[i, 1, side + k]]
            right = cot_right[ids[i, 1, side + k + pairs]] if k + pairs < count else both
            lhs = jnp.concatenate([left, right], axis=0)
            prod[i * pairs + k] = lax.dot_general(
                lhs, part[d, k], (((1,), (1,)), ((), ())), preferred_element_type=jnp.float32
            )

    def add(part, d, i):
        for k in range(pairs):
            acc[ids[i, 0, side + k]] += prod[i * pairs + k, 0:rows, :]
            if k + pairs < count:
                acc[ids[i, 0, side + k + pairs]] += prod[i * pairs + k, rows:2 * rows, :]

    over(gathered, multiply)
    over(gathered, add)
    me = lax.axis_index("tensor")
    share = rows // n_tensor
    for k in range(n_tensor):
        start = pl.multiple_of(lax.bitwise_xor(me, k) * share, share)
        for r in range(0, row_count, 2):
            pair = jnp.concatenate(
                [acc[r, pl.ds(start, share), :], acc[r + 1, pl.ds(start, share), :]], axis=1
            )
            outs[k][:, r * side:(r + 2) * side] = pair.astype(jnp.bfloat16)


def forward_kernel(count, n_parts, n_tensor, *refs):
    gathered, tokens = refs[:n_parts], refs[n_parts:n_parts + n_tensor]
    out, ids_vmem, ids, blocks, prod, acc, stage, sem = refs[n_parts + n_tensor:]
    pairs, side = gathered[0].shape[1:3]
    row_count = blocks.shape[0] - 1
    col_count = acc.shape[0] - 1
    rows = blocks.shape[1]
    share = rows // n_tensor
    copy = load_ids(gathered, ids_vmem, ids, sem)
    acc[...] = jnp.zeros_like(acc)
    for r in range(row_count):
        parts = [tokens[k][:, r * side:(r + 1) * side].astype(jnp.float32) for k in range(n_tensor)]
        blocks[r] = jnp.concatenate(parts, axis=0).astype(jnp.bfloat16)
    blocks[row_count] = jnp.zeros((rows, side), jnp.bfloat16)
    copy.wait()

    def multiply(part, d, i):
        for k in range(pairs):
            left = blocks[ids[i, 0, side + k]]
            right = blocks[ids[i, 0, side + k + pairs]] if k + pairs < count else jnp.zeros_like(left)
            lhs = jnp.concatenate([left, right], axis=0)
            prod[i * pairs + k] = jnp.dot(lhs, part[d, k], preferred_element_type=jnp.float32)

    lane = lax.broadcasted_iota(jnp.int32, (rows, 2 * side), 1)

    def add(part, d, i):
        for k in range(pairs):
            acc[ids[i, 1, side + k]] += jnp.where(lane < side, prod[i * pairs + k, 0:rows, :], 0.0)
            if k + pairs < count:
                acc[ids[i, 1, side + k + pairs]] += jnp.where(
                    lane >= side, prod[i * pairs + k, rows:2 * rows, :], 0.0
                )

    over(gathered, multiply)
    over(gathered, add)
    me = lax.axis_index("tensor")
    for k in range(n_tensor):
        start = pl.multiple_of(lax.bitwise_xor(me, k) * share, share)
        for c in range(0, col_count, 2):
            sums = []
            for i in (c, c + 1):
                value = acc[i, k * share:(k + 1) * share, :]
                sums.append(value[:, :side] + value[:, side:])
            stage[pl.ds(start, share), c * side:(c + 2) * side] = jnp.concatenate(sums, axis=1)
    out[...] = stage[...].astype(jnp.bfloat16)


def swap(value, axis, n, k):
    return lax.ppermute(value, axis, [(i, i ^ k) for i in range(n)])


def gather_parts(packed, n_dp):
    if n_dp > 8 or n_dp & (n_dp - 1):
        return [lax.all_gather(packed, "dp", axis=0, tiled=True)]
    same_core = [packed] + [swap(packed, "dp", n_dp, k) for k in range(n_dp - 2, 0, -2)]
    return same_core + [swap(part, "dp", n_dp, 1) for part in same_core]


def on_device(n_dp, n_tensor, inputs, block_values, block_slot, grad_out):
    share, width = inputs.shape
    rows, hidden = grad_out.shape
    _, count, side, _ = block_values.shape
    row_count, col_count = width // side, hidden // side
    pairs = count // 2 + 1
    bf16, f32, i32 = jnp.bfloat16, jnp.float32, jnp.int32
    far_first = range(n_tensor - 1, 0, -1)

    packed = pl.pallas_call(
        functools.partial(pack_kernel, count, row_count, col_count),
        out_shape=jax.ShapeDtypeStruct((1, pairs, side, 2 * side), bf16),
        in_specs=[SMEM, VMEM],
        out_specs=VMEM,
    )(block_slot, block_values)
    gathered = gather_parts(packed, n_dp)
    moved = {k: swap(inputs, "tensor", n_tensor, k) for k in far_first}
    tokens = [inputs] + [moved[k] for k in range(1, n_tensor)]
    n_parts = len(gathered)
    total = n_dp * pairs
    ids = [
        pltpu.VMEM((n_dp, 8, 2 * side), i32),
        pltpu.SMEM((n_dp, 8, 2 * side), i32),
    ]
    partial_sums = pl.pallas_call(
        functools.partial(backward_kernel, count, n_parts, n_tensor),
        out_shape=[jax.ShapeDtypeStruct((share, width), bf16)] * n_tensor,
        in_specs=[VMEM] * (n_parts + 1),
        out_specs=[VMEM] * n_tensor,
        scratch_shapes=ids + [
            pltpu.VMEM((col_count + 1, rows, 2 * side), bf16),
            pltpu.VMEM((col_count + 1, rows, 2 * side), bf16),
            pltpu.VMEM((total, 2 * rows, side), f32),
            pltpu.VMEM((row_count + 1, rows, side), f32),
            pltpu.SemaphoreType.DMA,
        ],
        compiler_params=pltpu.CompilerParams(vmem_limit_bytes=LIMIT),
    )(*gathered, grad_out)
    arrived = [partial_sums[0]] + [swap(partial_sums[k], "tensor", n_tensor, k) for k in far_first]
    outputs = pl.pallas_call(
        functools.partial(forward_kernel, count, n_parts, n_tensor),
        out_shape=jax.ShapeDtypeStruct((rows, hidden), bf16),
        in_specs=[VMEM] * (n_parts + n_tensor),
        out_specs=VMEM,
        scratch_shapes=ids + [
            pltpu.VMEM((row_count + 1, rows, side), bf16),
            pltpu.VMEM((total, 2 * rows, 2 * side), f32),
            pltpu.VMEM((col_count + 1, rows, 2 * side), f32),
            pltpu.VMEM((rows, hidden), f32),
            pltpu.SemaphoreType.DMA,
        ],
        compiler_params=pltpu.CompilerParams(vmem_limit_bytes=LIMIT),
    )(*gathered, *tokens)
    total_grad = arrived[0].astype(f32)
    for value in arrived[1:]:
        total_grad = total_grad + value.astype(f32)
    return (outputs, total_grad.astype(bf16))


def solution(mesh):
    placed = (
        P(("dp", "tensor"), None),
        P("tensor", "dp", None, None),
        P("tensor", "dp"),
        P("dp", "tensor"),
    )
    return jax.shard_map(
        functools.partial(on_device, mesh.shape["dp"], mesh.shape["tensor"]),
        mesh=mesh,
        in_specs=placed,
        out_specs=(P("dp", "tensor"), P(("dp", "tensor"), None)),
        check_vma=False,
    )
```

```python
import functools

import jax
import jax.numpy as jnp
from jax import lax
from jax.experimental import pallas as pl
from jax.experimental.pallas import tpu as pltpu
from jax.sharding import PartitionSpec as P

VMEM = pl.BlockSpec(memory_space=pltpu.VMEM)
SMEM = pl.BlockSpec(memory_space=pltpu.SMEM)
MIB = 1024 * 1024


def pack_kernel(count, row_count, col_count, slots, values, packed):
    side = values.shape[2]
    pairs = packed.shape[1]
    lane = lax.broadcasted_iota(jnp.int32, (side, side), 1)
    line = lax.broadcasted_iota(jnp.int32, (side, side), 0)
    head = jnp.zeros((side, side), jnp.float32)
    for j in range(count):
        p = slots[0, j]
        row = jnp.where(p >= 0, p // col_count, row_count)
        col = jnp.where(p >= 0, p % col_count, col_count)
        here = jnp.where(line == 0, row, col).astype(jnp.float32)
        head = jnp.where(lane == j, here, head)
    head = head.astype(jnp.bfloat16)
    for k in range(pairs):
        left = values[0, k]
        right = values[0, k + pairs] if k + pairs < count else head
        packed[0, k] = jnp.concatenate([left, right], axis=1)


def load_ids(gathered, ids_vmem, ids, sem):
    start = 0
    for part in gathered:
        n, pairs = part.shape[:2]
        head = part[:, pairs - 1, 0:16, :].astype(jnp.float32).astype(jnp.int32)
        ids_vmem[start:start + n] = head[:, 0:8, :]
        start += n
    copy = pltpu.make_async_copy(ids_vmem, ids, sem)
    copy.start()
    return copy


def over(gathered, body):
    start = 0
    for part in gathered:
        n = part.shape[0]
        if n <= 8:
            for d in range(n):
                body(part, d, start + d)
        else:
            def step(d, carry, part=part, start=start):
                body(part, d, start + d)
                return carry
            lax.fori_loop(0, n, step, 0)
        start += n


def backward_kernel(count, n_parts, n_tensor, *refs):
    gathered, cot = refs[:n_parts], refs[n_parts]
    out, ids_vmem, ids, cot_left, cot_right, prod, acc, sem = refs[n_parts + 1:]
    pairs, side = gathered[0].shape[1:3]
    col_count = cot_left.shape[0] - 1
    row_count = acc.shape[0] - 1
    rows = cot.shape[0]
    copy = load_ids(gathered, ids_vmem, ids, sem)
    acc[...] = jnp.zeros_like(acc)
    zero = jnp.zeros((rows, side), jnp.bfloat16)
    for c in range(col_count):
        part = cot[:, c * side:(c + 1) * side]
        cot_left[c] = jnp.concatenate([part, zero], axis=1)
        cot_right[c] = jnp.concatenate([zero, part], axis=1)
    both = jnp.concatenate([zero, zero], axis=1)
    cot_left[col_count] = both
    cot_right[col_count] = both
    copy.wait()

    def multiply(part, d, i):
        for k in range(pairs):
            left = cot_left[ids[i, 1, side + k]]
            right = cot_right[ids[i, 1, side + k + pairs]] if k + pairs < count else both
            lhs = jnp.concatenate([left, right], axis=0)
            prod[i * pairs + k] = lax.dot_general(
                lhs, part[d, k], (((1,), (1,)), ((), ())), preferred_element_type=jnp.float32
            )

    def add(part, d, i):
        for k in range(pairs):
            acc[ids[i, 0, side + k]] += prod[i * pairs + k, 0:rows, :]
            if k + pairs < count:
                acc[ids[i, 0, side + k + pairs]] += prod[i * pairs + k, rows:2 * rows, :]

    over(gathered, multiply)
    over(gathered, add)
    share = rows // n_tensor
    for r in range(0, row_count, 2):
        pair = jnp.concatenate([acc[r], acc[r + 1]], axis=1)
        for k in range(n_tensor):
            out[k, :, r * side:(r + 2) * side] = pair[k * share:(k + 1) * share].astype(jnp.bfloat16)


def forward_kernel(count, n_parts, n_tensor, *refs):
    gathered, tokens = refs[:n_parts], refs[n_parts:n_parts + n_tensor]
    out, ids_vmem, ids, blocks, prod, acc, stage, sem = refs[n_parts + n_tensor:]
    pairs, side = gathered[0].shape[1:3]
    row_count = blocks.shape[0] - 1
    col_count = acc.shape[0] - 1
    rows = blocks.shape[1]
    share = rows // n_tensor
    copy = load_ids(gathered, ids_vmem, ids, sem)
    acc[...] = jnp.zeros_like(acc)
    for r in range(row_count):
        parts = [tokens[k][:, r * side:(r + 1) * side].astype(jnp.float32) for k in range(n_tensor)]
        blocks[r] = jnp.concatenate(parts, axis=0).astype(jnp.bfloat16)
    blocks[row_count] = jnp.zeros((rows, side), jnp.bfloat16)
    copy.wait()

    def multiply(part, d, i):
        for k in range(pairs):
            left = blocks[ids[i, 0, side + k]]
            right = blocks[ids[i, 0, side + k + pairs]] if k + pairs < count else jnp.zeros_like(left)
            lhs = jnp.concatenate([left, right], axis=0)
            prod[i * pairs + k] = jnp.dot(lhs, part[d, k], preferred_element_type=jnp.float32)

    lane = lax.broadcasted_iota(jnp.int32, (rows, 2 * side), 1)

    def add(part, d, i):
        for k in range(pairs):
            acc[ids[i, 1, side + k]] += jnp.where(lane < side, prod[i * pairs + k, 0:rows, :], 0.0)
            if k + pairs < count:
                acc[ids[i, 1, side + k + pairs]] += jnp.where(
                    lane >= side, prod[i * pairs + k, rows:2 * rows, :], 0.0
                )

    over(gathered, multiply)
    over(gathered, add)
    me = lax.axis_index("tensor")
    for k in range(n_tensor):
        start = pl.multiple_of(lax.bitwise_xor(me, k) * share, share)
        for c in range(0, col_count, 2):
            sums = []
            for i in (c, c + 1):
                value = acc[i, k * share:(k + 1) * share, :]
                sums.append(value[:, :side] + value[:, side:])
            stage[pl.ds(start, share), c * side:(c + 2) * side] = jnp.concatenate(sums, axis=1)
    out[...] = stage[...].astype(jnp.bfloat16)


def swap(value, axis, n, k):
    return lax.ppermute(value, axis, [(i, i ^ k) for i in range(n)])


def gather_parts(packed, n_dp):
    if n_dp > 8 or n_dp & (n_dp - 1):
        return [lax.all_gather(packed, "dp", axis=0, tiled=True)]
    same_core = [packed] + [swap(packed, "dp", n_dp, k) for k in range(n_dp - 2, 0, -2)]
    return same_core + [swap(part, "dp", n_dp, 1) for part in same_core]


def on_device(n_dp, n_tensor, inputs, block_values, block_slot, grad_out):
    share, width = inputs.shape
    rows, hidden = grad_out.shape
    _, count, side, _ = block_values.shape
    row_count, col_count = width // side, hidden // side
    pairs = count // 2 + 1
    bf16, f32, i32 = jnp.bfloat16, jnp.float32, jnp.int32
    grant = (12 if n_dp <= 8 else 48) * MIB
    far_first = range(n_tensor - 1, 0, -1)

    packed = pl.pallas_call(
        functools.partial(pack_kernel, count, row_count, col_count),
        out_shape=jax.ShapeDtypeStruct((1, pairs, side, 2 * side), bf16),
        in_specs=[SMEM, VMEM],
        out_specs=VMEM,
        compiler_params=pltpu.CompilerParams(vmem_limit_bytes=4 * MIB),
    )(block_slot, block_values)
    gathered = gather_parts(packed, n_dp)
    moved = {k: swap(inputs, "tensor", n_tensor, k) for k in far_first}
    tokens = [inputs] + [moved[k] for k in range(1, n_tensor)]
    n_parts = len(gathered)
    total = n_dp * pairs
    ids = [
        pltpu.VMEM((n_dp, 8, 2 * side), i32),
        pltpu.SMEM((n_dp, 8, 2 * side), i32),
    ]
    partial_sums = pl.pallas_call(
        functools.partial(backward_kernel, count, n_parts, n_tensor),
        out_shape=jax.ShapeDtypeStruct((n_tensor, share, width), bf16),
        in_specs=[VMEM] * (n_parts + 1),
        out_specs=VMEM,
        scratch_shapes=ids + [
            pltpu.VMEM((col_count + 1, rows, 2 * side), bf16),
            pltpu.VMEM((col_count + 1, rows, 2 * side), bf16),
            pltpu.VMEM((total, 2 * rows, side), f32),
            pltpu.VMEM((row_count + 1, rows, side), f32),
            pltpu.SemaphoreType.DMA,
        ],
        compiler_params=pltpu.CompilerParams(vmem_limit_bytes=grant),
    )(*gathered, grad_out)
    arrived = lax.all_to_all(partial_sums, "tensor", 0, 0, tiled=True)
    outputs = pl.pallas_call(
        functools.partial(forward_kernel, count, n_parts, n_tensor),
        out_shape=jax.ShapeDtypeStruct((rows, hidden), bf16),
        in_specs=[VMEM] * (n_parts + n_tensor),
        out_specs=VMEM,
        scratch_shapes=ids + [
            pltpu.VMEM((row_count + 1, rows, side), bf16),
            pltpu.VMEM((total, 2 * rows, 2 * side), f32),
            pltpu.VMEM((col_count + 1, rows, 2 * side), f32),
            pltpu.VMEM((rows, hidden), f32),
            pltpu.SemaphoreType.DMA,
        ],
        compiler_params=pltpu.CompilerParams(vmem_limit_bytes=grant),
    )(*gathered, *tokens)
    total_grad = arrived[0].astype(f32)
    for k in range(1, n_tensor):
        total_grad = total_grad + arrived[k].astype(f32)
    return (outputs, total_grad.astype(bf16))


def solution(mesh):
    placed = (
        P(("dp", "tensor"), None),
        P("tensor", "dp", None, None),
        P("tensor", "dp"),
        P("dp", "tensor"),
    )
    return jax.shard_map(
        functools.partial(on_device, mesh.shape["dp"], mesh.shape["tensor"]),
        mesh=mesh,
        in_specs=placed,
        out_specs=(P("dp", "tensor"), P(("dp", "tensor"), None)),
        check_vma=False,
    )
```

```python
import functools

import jax
import jax.numpy as jnp
from jax import lax
from jax.experimental import pallas as pl
from jax.experimental.pallas import tpu as pltpu
from jax.sharding import PartitionSpec as P

VMEM = pl.BlockSpec(memory_space=pltpu.VMEM)
SMEM = pl.BlockSpec(memory_space=pltpu.SMEM)
HBM = pl.BlockSpec(memory_space=pltpu.HBM)
MIB = 1024 * 1024


def pack_kernel(count, row_count, col_count, slots_hbm, values_hbm, packed, slots, values, sems):
    copies = [
        pltpu.make_async_copy(slots_hbm, slots, sems.at[0]),
        pltpu.make_async_copy(values_hbm, values, sems.at[1]),
    ]
    for copy in copies:
        copy.start()
    side = values.shape[2]
    pairs = packed.shape[1]
    copies[0].wait()
    lane = lax.broadcasted_iota(jnp.int32, (side, side), 1)
    line = lax.broadcasted_iota(jnp.int32, (side, side), 0)
    head = jnp.zeros((side, side), jnp.float32)
    for j in range(count):
        p = slots[0, j]
        row = jnp.where(p >= 0, p // col_count, row_count)
        col = jnp.where(p >= 0, p % col_count, col_count)
        here = jnp.where(line == 0, row, col).astype(jnp.float32)
        head = jnp.where(lane == j, here, head)
    head = head.astype(jnp.bfloat16)
    copies[1].wait()
    for k in range(pairs):
        left = values[0, k]
        right = values[0, k + pairs] if k + pairs < count else head
        packed[0, k] = jnp.concatenate([left, right], axis=1)


def load_ids(gathered, ids_vmem, ids, sem):
    start = 0
    for part in gathered:
        n, pairs = part.shape[:2]
        head = part[:, pairs - 1, 0:16, :].astype(jnp.float32).astype(jnp.int32)
        ids_vmem[start:start + n] = head[:, 0:8, :]
        start += n
    copy = pltpu.make_async_copy(ids_vmem, ids, sem)
    copy.start()
    return copy


def over(gathered, body):
    start = 0
    for part in gathered:
        n = part.shape[0]
        if n <= 8:
            for d in range(n):
                body(part, d, start + d)
        else:
            def step(d, carry, part=part, start=start):
                body(part, d, start + d)
                return carry
            lax.fori_loop(0, n, step, 0)
        start += n


def backward_kernel(count, n_parts, n_tensor, *refs):
    gathered, cot, own_tokens = refs[:n_parts], refs[n_parts], refs[n_parts + 1]
    outs, own_later = refs[n_parts + 2:n_parts + 2 + n_tensor], refs[n_parts + 2 + n_tensor]
    ids_vmem, ids, cot_left, cot_right, prod, acc, sem = refs[n_parts + 3 + n_tensor:]
    own_later[...] = own_tokens[...]
    pairs, side = gathered[0].shape[1:3]
    col_count = cot_left.shape[0] - 1
    row_count = acc.shape[0] - 1
    rows = cot.shape[0]
    copy = load_ids(gathered, ids_vmem, ids, sem)
    acc[...] = jnp.zeros_like(acc)
    zero = jnp.zeros((rows, side), jnp.bfloat16)
    for c in range(col_count):
        part = cot[:, c * side:(c + 1) * side]
        cot_left[c] = jnp.concatenate([part, zero], axis=1)
        cot_right[c] = jnp.concatenate([zero, part], axis=1)
    both = jnp.concatenate([zero, zero], axis=1)
    cot_left[col_count] = both
    cot_right[col_count] = both
    copy.wait()

    def multiply(part, d, i):
        for k in range(pairs):
            left = cot_left[ids[i, 1, side + k]]
            right = cot_right[ids[i, 1, side + k + pairs]] if k + pairs < count else both
            lhs = jnp.concatenate([left, right], axis=0)
            prod[i * pairs + k] = lax.dot_general(
                lhs, part[d, k], (((1,), (1,)), ((), ())), preferred_element_type=jnp.float32
            )

    def add(part, d, i):
        for k in range(pairs):
            acc[ids[i, 0, side + k]] += prod[i * pairs + k, 0:rows, :]
            if k + pairs < count:
                acc[ids[i, 0, side + k + pairs]] += prod[i * pairs + k, rows:2 * rows, :]

    over(gathered, multiply)
    over(gathered, add)
    me = lax.axis_index("tensor")
    share = rows // n_tensor
    for k in range(n_tensor):
        start = pl.multiple_of(lax.bitwise_xor(me, k) * share, share)
        for r in range(0, row_count, 2):
            pair = jnp.concatenate(
                [acc[r, pl.ds(start, share), :], acc[r + 1, pl.ds(start, share), :]], axis=1
            )
            outs[k][:, r * side:(r + 2) * side] = pair.astype(jnp.bfloat16)


def forward_kernel(count, n_parts, n_tensor, *refs):
    gathered, tokens = refs[:n_parts], refs[n_parts:n_parts + n_tensor]
    out, ids_vmem, ids, blocks, prod, acc, stage, sem = refs[n_parts + n_tensor:]
    pairs, side = gathered[0].shape[1:3]
    row_count = blocks.shape[0] - 1
    col_count = acc.shape[0] - 1
    rows = blocks.shape[1]
    share = rows // n_tensor
    copy = load_ids(gathered, ids_vmem, ids, sem)
    acc[...] = jnp.zeros_like(acc)
    for r in range(row_count):
        parts = [tokens[k][:, r * side:(r + 1) * side].astype(jnp.float32) for k in range(n_tensor)]
        blocks[r] = jnp.concatenate(parts, axis=0).astype(jnp.bfloat16)
    blocks[row_count] = jnp.zeros((rows, side), jnp.bfloat16)
    copy.wait()

    def multiply(part, d, i):
        for k in range(pairs):
            left = blocks[ids[i, 0, side + k]]
            right = blocks[ids[i, 0, side + k + pairs]] if k + pairs < count else jnp.zeros_like(left)
            lhs = jnp.concatenate([left, right], axis=0)
            prod[i * pairs + k] = jnp.dot(lhs, part[d, k], preferred_element_type=jnp.float32)

    lane = lax.broadcasted_iota(jnp.int32, (rows, 2 * side), 1)

    def add(part, d, i):
        for k in range(pairs):
            acc[ids[i, 1, side + k]] += jnp.where(lane < side, prod[i * pairs + k, 0:rows, :], 0.0)
            if k + pairs < count:
                acc[ids[i, 1, side + k + pairs]] += jnp.where(
                    lane >= side, prod[i * pairs + k, rows:2 * rows, :], 0.0
                )

    over(gathered, multiply)
    over(gathered, add)
    me = lax.axis_index("tensor")
    for k in range(n_tensor):
        start = pl.multiple_of(lax.bitwise_xor(me, k) * share, share)
        for c in range(0, col_count, 2):
            sums = []
            for i in (c, c + 1):
                value = acc[i, k * share:(k + 1) * share, :]
                sums.append(value[:, :side] + value[:, side:])
            stage[pl.ds(start, share), c * side:(c + 2) * side] = jnp.concatenate(sums, axis=1)
    out[...] = stage[...].astype(jnp.bfloat16)


def swap(value, axis, n, k):
    return lax.ppermute(value, axis, [(i, i ^ k) for i in range(n)])


def gather_parts(packed, n_dp):
    if n_dp > 8 or n_dp & (n_dp - 1):
        return [lax.all_gather(packed, "dp", axis=0, tiled=True)]
    same_core = [swap(packed, "dp", n_dp, k) for k in range(n_dp - 2, 0, -2)]
    later, first = lax.optimization_barrier((packed, same_core[-1]))
    same_core = same_core[:-1] + [first]
    return [packed] + same_core + [swap(part, "dp", n_dp, 1) for part in same_core + [later]]


def on_device(n_dp, n_tensor, inputs, block_values, block_slot, grad_out):
    share, width = inputs.shape
    rows, hidden = grad_out.shape
    _, count, side, _ = block_values.shape
    row_count, col_count = width // side, hidden // side
    pairs = count // 2 + 1
    bf16, f32, i32 = jnp.bfloat16, jnp.float32, jnp.int32
    grant = (12 if n_dp <= 8 else 48) * MIB
    far_first = range(n_tensor - 1, 0, -1)

    packed = pl.pallas_call(
        functools.partial(pack_kernel, count, row_count, col_count),
        out_shape=pltpu.VMEM((1, pairs, side, 2 * side), bf16),
        in_specs=[HBM, HBM],
        out_specs=VMEM,
        scratch_shapes=[
            pltpu.SMEM(block_slot.shape, i32),
            pltpu.VMEM(block_values.shape, bf16),
            pltpu.SemaphoreType.DMA((2,)),
        ],
        compiler_params=pltpu.CompilerParams(vmem_limit_bytes=4 * MIB),
    )(pltpu.with_memory_space_constraint(block_slot, pltpu.HBM), pltpu.with_memory_space_constraint(block_values, pltpu.HBM))
    gathered = gather_parts(packed, n_dp)
    moved = {k: swap(inputs, "tensor", n_tensor, k) for k in range(2, n_tensor)}
    n_parts = len(gathered)
    total = n_dp * pairs
    ids = [
        pltpu.VMEM((n_dp, 8, 2 * side), i32),
        pltpu.SMEM((n_dp, 8, 2 * side), i32),
    ]
    *partial_sums, own_later = pl.pallas_call(
        functools.partial(backward_kernel, count, n_parts, n_tensor),
        out_shape=[jax.ShapeDtypeStruct((share, width), bf16)] * (n_tensor + 1),
        in_specs=[VMEM] * (n_parts + 2),
        out_specs=[VMEM] * (n_tensor + 1),
        scratch_shapes=ids + [
            pltpu.VMEM((col_count + 1, rows, 2 * side), bf16),
            pltpu.VMEM((col_count + 1, rows, 2 * side), bf16),
            pltpu.VMEM((total, 2 * rows, side), f32),
            pltpu.VMEM((row_count + 1, rows, side), f32),
            pltpu.SemaphoreType.DMA,
        ],
        compiler_params=pltpu.CompilerParams(vmem_limit_bytes=grant),
    )(*gathered, grad_out, inputs)
    arrived = [partial_sums[0]] + [swap(partial_sums[k], "tensor", n_tensor, k) for k in far_first]
    moved[1] = swap(own_later, "tensor", n_tensor, 1)
    tokens = [inputs] + [moved[k] for k in range(1, n_tensor)]
    outputs = pl.pallas_call(
        functools.partial(forward_kernel, count, n_parts, n_tensor),
        out_shape=jax.ShapeDtypeStruct((rows, hidden), bf16),
        in_specs=[VMEM] * (n_parts + n_tensor),
        out_specs=VMEM,
        scratch_shapes=ids + [
            pltpu.VMEM((row_count + 1, rows, side), bf16),
            pltpu.VMEM((total, 2 * rows, 2 * side), f32),
            pltpu.VMEM((col_count + 1, rows, 2 * side), f32),
            pltpu.VMEM((rows, hidden), f32),
            pltpu.SemaphoreType.DMA,
        ],
        compiler_params=pltpu.CompilerParams(vmem_limit_bytes=grant),
    )(*gathered, *tokens)
    total_grad = arrived[0].astype(f32)
    for value in arrived[1:]:
        total_grad = total_grad + value.astype(f32)
    return (outputs, total_grad.astype(bf16))


def solution(mesh):
    placed = (
        P(("dp", "tensor"), None),
        P("tensor", "dp", None, None),
        P("tensor", "dp"),
        P("dp", "tensor"),
    )
    return jax.shard_map(
        functools.partial(on_device, mesh.shape["dp"], mesh.shape["tensor"]),
        mesh=mesh,
        in_specs=placed,
        out_specs=(P("dp", "tensor"), P(("dp", "tensor"), None)),
        check_vma=False,
    )
```

```python
import functools

import jax
import jax.numpy as jnp
from jax import lax
from jax.experimental import pallas as pl
from jax.experimental.pallas import tpu as pltpu
from jax.sharding import PartitionSpec as P

VMEM = pl.BlockSpec(memory_space=pltpu.VMEM)
SMEM = pl.BlockSpec(memory_space=pltpu.SMEM)
HBM = pl.BlockSpec(memory_space=pltpu.HBM)
MIB = 1024 * 1024


def pack_kernel(count, row_count, col_count, slots_hbm, values_hbm, packed, slots, values, sems):
    copies = [
        pltpu.make_async_copy(slots_hbm, slots, sems.at[0]),
        pltpu.make_async_copy(values_hbm, values, sems.at[1]),
    ]
    for copy in copies:
        copy.start()
    side = values.shape[2]
    pairs = packed.shape[1]
    copies[0].wait()
    lane = lax.broadcasted_iota(jnp.int32, (side, side), 1)
    line = lax.broadcasted_iota(jnp.int32, (side, side), 0)
    head = jnp.zeros((side, side), jnp.float32)
    for j in range(count):
        p = slots[0, j]
        row = jnp.where(p >= 0, p // col_count, row_count)
        col = jnp.where(p >= 0, p % col_count, col_count)
        here = jnp.where(line == 0, row, col).astype(jnp.float32)
        head = jnp.where(lane == j, here, head)
    head = head.astype(jnp.bfloat16)
    copies[1].wait()
    for k in range(pairs):
        left = values[0, k]
        right = values[0, k + pairs] if k + pairs < count else head
        packed[0, k] = jnp.concatenate([left, right], axis=1)


def join_kernel(*refs):
    for i, part in enumerate(refs[:-1]):
        refs[-1][i] = part[0]


def load_ids(gathered, ids_vmem, ids, sem):
    start = 0
    for part in gathered:
        n, pairs = part.shape[:2]
        head = part[:, pairs - 1, 0:16, :].astype(jnp.float32).astype(jnp.int32)
        ids_vmem[start:start + n] = head[:, 0:8, :]
        start += n
    copy = pltpu.make_async_copy(ids_vmem, ids, sem)
    copy.start()
    return copy


def over(gathered, body):
    start = 0
    for part in gathered:
        n = part.shape[0]
        if n <= 8:
            for d in range(n):
                body(part, d, start + d)
        else:
            def step(d, carry, part=part, start=start):
                body(part, d, start + d)
                return carry
            lax.fori_loop(0, n, step, 0)
        start += n


def backward_kernel(count, n_parts, n_tensor, *refs):
    gathered, cot, outs = refs[:n_parts], refs[n_parts], refs[n_parts + 1:n_parts + 1 + n_tensor]
    ids_vmem, ids, cot_left, cot_right, prod, acc, sem = refs[n_parts + 1 + n_tensor:]
    pairs, side = gathered[0].shape[1:3]
    col_count = cot_left.shape[0] - 1
    row_count = acc.shape[0] - 1
    rows = cot.shape[0]
    copy = load_ids(gathered, ids_vmem, ids, sem)
    acc[...] = jnp.zeros_like(acc)
    zero = jnp.zeros((rows, side), jnp.bfloat16)
    for c in range(col_count):
        part = cot[:, c * side:(c + 1) * side]
        cot_left[c] = jnp.concatenate([part, zero], axis=1)
        cot_right[c] = jnp.concatenate([zero, part], axis=1)
    both = jnp.concatenate([zero, zero], axis=1)
    cot_left[col_count] = both
    cot_right[col_count] = both
    copy.wait()

    def multiply(part, d, i):
        for k in range(pairs):
            left = cot_left[ids[i, 1, side + k]]
            right = cot_right[ids[i, 1, side + k + pairs]] if k + pairs < count else both
            lhs = jnp.concatenate([left, right], axis=0)
            prod[i * pairs + k] = lax.dot_general(
                lhs, part[d, k], (((1,), (1,)), ((), ())), preferred_element_type=jnp.float32
            )

    def add(part, d, i):
        for k in range(pairs):
            acc[ids[i, 0, side + k]] += prod[i * pairs + k, 0:rows, :]
            if k + pairs < count:
                acc[ids[i, 0, side + k + pairs]] += prod[i * pairs + k, rows:2 * rows, :]

    over(gathered, multiply)
    over(gathered, add)
    me = lax.axis_index("tensor")
    share = rows // n_tensor
    for k in range(n_tensor):
        start = pl.multiple_of(lax.bitwise_xor(me, k) * share, share)
        for r in range(0, row_count, 2):
            pair = jnp.concatenate(
                [acc[r, pl.ds(start, share), :], acc[r + 1, pl.ds(start, share), :]], axis=1
            )
            outs[k][:, r * side:(r + 2) * side] = pair.astype(jnp.bfloat16)


def forward_kernel(count, n_parts, n_tensor, *refs):
    gathered, tokens = refs[:n_parts], refs[n_parts:n_parts + n_tensor]
    out, ids_vmem, ids, blocks, prod, acc, stage, sem = refs[n_parts + n_tensor:]
    pairs, side = gathered[0].shape[1:3]
    row_count = blocks.shape[0] - 1
    col_count = acc.shape[0] - 1
    rows = blocks.shape[1]
    share = rows // n_tensor
    copy = load_ids(gathered, ids_vmem, ids, sem)
    acc[...] = jnp.zeros_like(acc)
    for r in range(row_count):
        parts = [tokens[k][:, r * side:(r + 1) * side].astype(jnp.float32) for k in range(n_tensor)]
        blocks[r] = jnp.concatenate(parts, axis=0).astype(jnp.bfloat16)
    blocks[row_count] = jnp.zeros((rows, side), jnp.bfloat16)
    copy.wait()

    def multiply(part, d, i):
        for k in range(pairs):
            left = blocks[ids[i, 0, side + k]]
            right = blocks[ids[i, 0, side + k + pairs]] if k + pairs < count else jnp.zeros_like(left)
            lhs = jnp.concatenate([left, right], axis=0)
            prod[i * pairs + k] = jnp.dot(lhs, part[d, k], preferred_element_type=jnp.float32)

    lane = lax.broadcasted_iota(jnp.int32, (rows, 2 * side), 1)

    def add(part, d, i):
        for k in range(pairs):
            acc[ids[i, 1, side + k]] += jnp.where(lane < side, prod[i * pairs + k, 0:rows, :], 0.0)
            if k + pairs < count:
                acc[ids[i, 1, side + k + pairs]] += jnp.where(
                    lane >= side, prod[i * pairs + k, rows:2 * rows, :], 0.0
                )

    over(gathered, multiply)
    over(gathered, add)
    me = lax.axis_index("tensor")
    for k in range(n_tensor):
        start = pl.multiple_of(lax.bitwise_xor(me, k) * share, share)
        for c in range(0, col_count, 2):
            sums = []
            for i in (c, c + 1):
                value = acc[i, k * share:(k + 1) * share, :]
                sums.append(value[:, :side] + value[:, side:])
            stage[pl.ds(start, share), c * side:(c + 2) * side] = jnp.concatenate(sums, axis=1)
    out[...] = stage[...].astype(jnp.bfloat16)


def swap(value, axis, n, k):
    return lax.ppermute(value, axis, [(i, i ^ k) for i in range(n)])


def gather_parts(packed, n_dp):
    if n_dp > 8 or n_dp & (n_dp - 1):
        return [lax.all_gather(packed, "dp", axis=0, tiled=True)]
    *near, second, last = [packed] + [swap(packed, "dp", n_dp, k) for k in range(2, n_dp, 2)]
    joined = pl.pallas_call(
        join_kernel,
        out_shape=pltpu.VMEM((len(near), *packed.shape[1:]), packed.dtype),
        in_specs=[VMEM] * len(near),
        out_specs=VMEM,
        compiler_params=pltpu.CompilerParams(vmem_limit_bytes=4 * MIB),
    )(*near)
    same_core = [joined, second, last]
    return same_core + [swap(part, "dp", n_dp, 1) for part in same_core]


def on_device(n_dp, n_tensor, inputs, block_values, block_slot, grad_out):
    share, width = inputs.shape
    rows, hidden = grad_out.shape
    _, count, side, _ = block_values.shape
    row_count, col_count = width // side, hidden // side
    pairs = count // 2 + 1
    bf16, f32, i32 = jnp.bfloat16, jnp.float32, jnp.int32
    grant = (12 if n_dp <= 8 else 48) * MIB
    far_first = range(n_tensor - 1, 0, -1)

    packed = pl.pallas_call(
        functools.partial(pack_kernel, count, row_count, col_count),
        out_shape=pltpu.VMEM((1, pairs, side, 2 * side), bf16),
        in_specs=[HBM, HBM],
        out_specs=VMEM,
        scratch_shapes=[
            pltpu.SMEM(block_slot.shape, i32),
            pltpu.VMEM(block_values.shape, bf16),
            pltpu.SemaphoreType.DMA((2,)),
        ],
        compiler_params=pltpu.CompilerParams(vmem_limit_bytes=4 * MIB),
    )(pltpu.with_memory_space_constraint(block_slot, pltpu.HBM), pltpu.with_memory_space_constraint(block_values, pltpu.HBM))
    gathered = gather_parts(packed, n_dp)
    moved = {k: swap(inputs, "tensor", n_tensor, k) for k in far_first}
    tokens = [inputs] + [moved[k] for k in range(1, n_tensor)]
    n_parts = len(gathered)
    total = n_dp * pairs
    ids = [
        pltpu.VMEM((n_dp, 8, 2 * side), i32),
        pltpu.SMEM((n_dp, 8, 2 * side), i32),
    ]
    partial_sums = pl.pallas_call(
        functools.partial(backward_kernel, count, n_parts, n_tensor),
        out_shape=[jax.ShapeDtypeStruct((share, width), bf16)] * n_tensor,
        in_specs=[VMEM] * (n_parts + 1),
        out_specs=[VMEM] * n_tensor,
        scratch_shapes=ids + [
            pltpu.VMEM((col_count + 1, rows, 2 * side), bf16),
            pltpu.VMEM((col_count + 1, rows, 2 * side), bf16),
            pltpu.VMEM((total, 2 * rows, side), f32),
            pltpu.VMEM((row_count + 1, rows, side), f32),
            pltpu.SemaphoreType.DMA,
        ],
        compiler_params=pltpu.CompilerParams(vmem_limit_bytes=grant),
    )(*gathered, grad_out)
    arrived = [partial_sums[0]] + [swap(partial_sums[k], "tensor", n_tensor, k) for k in far_first]
    outputs = pl.pallas_call(
        functools.partial(forward_kernel, count, n_parts, n_tensor),
        out_shape=jax.ShapeDtypeStruct((rows, hidden), bf16),
        in_specs=[VMEM] * (n_parts + n_tensor),
        out_specs=VMEM,
        scratch_shapes=ids + [
            pltpu.VMEM((row_count + 1, rows, side), bf16),
            pltpu.VMEM((total, 2 * rows, 2 * side), f32),
            pltpu.VMEM((col_count + 1, rows, 2 * side), f32),
            pltpu.VMEM((rows, hidden), f32),
            pltpu.SemaphoreType.DMA,
        ],
        compiler_params=pltpu.CompilerParams(vmem_limit_bytes=grant),
    )(*gathered, *tokens)
    total_grad = arrived[0].astype(f32)
    for value in arrived[1:]:
        total_grad = total_grad + value.astype(f32)
    return (outputs, total_grad.astype(bf16))


def solution(mesh):
    placed = (
        P(("dp", "tensor"), None),
        P("tensor", "dp", None, None),
        P("tensor", "dp"),
        P("dp", "tensor"),
    )
    return jax.shard_map(
        functools.partial(on_device, mesh.shape["dp"], mesh.shape["tensor"]),
        mesh=mesh,
        in_specs=placed,
        out_specs=(P("dp", "tensor"), P(("dp", "tensor"), None)),
        check_vma=False,
    )
```

```python
import functools

import jax
import jax.numpy as jnp
from jax import lax
from jax.experimental import pallas as pl
from jax.experimental.pallas import tpu as pltpu
from jax.sharding import PartitionSpec as P

VMEM = pl.BlockSpec(memory_space=pltpu.VMEM)
HBM = pl.BlockSpec(memory_space=pltpu.HBM)
MIB = 1024 * 1024
BF16, F32, I32 = jnp.bfloat16, jnp.float32, jnp.int32


def pack_kernel(count, row_count, col_count, slots_hbm, values_hbm, packed, slots, values, sems):
    copies = [
        pltpu.make_async_copy(slots_hbm, slots, sems.at[0]),
        pltpu.make_async_copy(values_hbm, values, sems.at[1]),
    ]
    for copy in copies:
        copy.start()
    side = values.shape[2]
    pairs = packed.shape[1]
    copies[0].wait()
    lane = lax.broadcasted_iota(I32, (side, side), 1)
    line = lax.broadcasted_iota(I32, (side, side), 0)
    head = jnp.zeros((side, side), F32)
    for j in range(count):
        p = slots[0, j]
        row = jnp.where(p >= 0, p // col_count, row_count)
        col = jnp.where(p >= 0, p % col_count, col_count)
        here = jnp.where(line == 0, row, col).astype(F32)
        head = jnp.where(lane == j, here, head)
    head = head.astype(BF16)
    copies[1].wait()
    for k in range(pairs):
        left = values[0, k]
        right = values[0, k + pairs] if k + pairs < count else head
        packed[0, k] = jnp.concatenate([left, right], axis=1)


def join_kernel(*refs):
    for i, part in enumerate(refs[:-1]):
        refs[-1][i] = part[0]


def load_ids(gathered, ids_vmem, ids, sem):
    i = 0
    for part in gathered:
        n, pairs = part.shape[:2]
        for d in range(n):
            head = part[d, pairs - 1, 0:16, :].astype(F32).astype(I32)
            ids_vmem[0, i:i + 1, :] = head[0:1]
            ids_vmem[1, i:i + 1, :] = head[1:2]
            i += 1
    copy = pltpu.make_async_copy(ids_vmem, ids, sem)
    copy.start()
    return copy


def over(gathered, body):
    start = 0
    for part in gathered:
        n = part.shape[0]
        if n <= 8:
            for d in range(n):
                body(part, d, start + d)
        else:
            def step(d, carry, part=part, start=start):
                body(part, d, start + d)
                return carry
            lax.fori_loop(0, n, step, 0)
        start += n


def low_half(shape):
    return lax.broadcasted_iota(I32, shape, 1) < shape[1] // 2


def swap_halves(x):
    half = x.shape[1] // 2
    return jnp.concatenate([x[:, half:], x[:, :half]], axis=1)


def twice(x):
    low, y = low_half(x.shape), swap_halves(x)
    return jnp.where(low, x, y), jnp.where(low, y, x)


def diagonal(tile, other=None):
    low = low_half(tile.shape)
    zero = jnp.zeros_like(tile)
    top = jnp.where(low, tile, zero)
    bottom = jnp.where(low, zero, tile if other is None else swap_halves(other))
    return jnp.concatenate([top, bottom], axis=0)


def fold(x):
    return x + pltpu.roll(x, x.shape[1] // 2, 1)


def across(lhs, rhs):
    return lax.dot_general(lhs, rhs, (((1,), (1,)), ((), ())), preferred_element_type=F32)


def load_cotangent(cot, cots):
    col_count = cots.shape[0] - 1
    for c in range(0, col_count, 2):
        width = cots.shape[2]
        cots[c], cots[c + 1] = twice(cot[:, c * width // 2:(c + 2) * width // 2])
    cots[col_count] = jnp.zeros_like(cots[col_count])


def slots_kernel(count, n_parts, n_tensor, *refs):
    gathered, cot, outs = refs[:n_parts], refs[n_parts], refs[n_parts + 1:n_parts + 1 + n_tensor]
    ids_vmem, ids, cots, prod, sem = refs[n_parts + 1 + n_tensor:]
    pairs, side = gathered[0].shape[1:3]
    rows = cot.shape[0]
    share = rows // n_tensor
    copy = load_ids(gathered, ids_vmem, ids, sem)
    load_cotangent(cot, cots)
    low = low_half((rows, 2 * side))
    heads = jnp.concatenate([ids_vmem[0].astype(F32)] * 2, axis=0).astype(BF16)
    where = [(part, d) for part in gathered for d in range(part.shape[0])]
    copy.wait()
    tiles = slot_tiles(len(where), pairs)
    for t, ((i, j), (m, l)) in enumerate(tiles):
        part, d = where[i]
        other, e = where[m]
        blocks = diagonal(part[d, j]) if i == m else diagonal(part[d, j], other[e, l])
        lhs = jnp.where(low, cots[ids[1, i, side + j]], cots[ids[1, m, side + l]])
        prod[t] = across(lhs, blocks)
    me = lax.axis_index("tensor")
    for k in range(n_tensor):
        start = pl.multiple_of(lax.bitwise_xor(me, k) * share, share)
        for t in range(0, len(tiles), 2):
            two = [prod[t, pl.ds(start, share), :], prod[t + 1, pl.ds(start, share), :]]
            outs[k][t * share:(t + 2) * share, :] = jnp.concatenate(two, axis=0).astype(BF16)
        outs[k][len(tiles) * share:, :] = heads


def slot_tiles(n, pairs):
    full = [((i, j), (i, j + pairs)) for i in range(n) for j in range(pairs - 1)]
    return full + [((i, pairs - 1), (i + 1, pairs - 1)) for i in range(0, n, 2)]


def sum_kernel(n_tensor, pairs, n_dp, *refs):
    messages, out = refs[:n_tensor], refs[n_tensor]
    ids_vmem, ids, sem = refs[n_tensor + 1:n_tensor + 4]
    accs = refs[n_tensor + 4:]
    share, width = out.shape
    side = messages[0].shape[1] // 2
    tiles = slot_tiles(n_dp, pairs)
    for m, message in enumerate(messages):
        ids_vmem[m] = message[len(tiles) * share:, :].astype(F32)[:n_dp].astype(I32)
    copy = pltpu.make_async_copy(ids_vmem, ids, sem)
    copy.start()
    for acc in accs:
        acc[...] = jnp.zeros_like(acc)
    low = low_half((share, 2 * side))
    copy.wait()
    for t in range(0, len(tiles), 2):
        for m, (message, acc) in enumerate(zip(messages, accs)):
            two = message[t * share:(t + 2) * share, :].astype(F32)
            for u in range(2):
                value = two[u * share:(u + 1) * share]
                (i, j), (p, l) = tiles[t + u]
                acc[ids[m, i, side + j]] += jnp.where(low, value, 0.0)
                acc[ids[m, p, side + l]] += jnp.where(low, 0.0, value)

    def total(r):
        value = accs[0][r]
        for acc in accs[1:]:
            value = value + acc[r]
        return fold(value)

    for r in range(0, width // side, 2):
        out[:, r * side:(r + 2) * side] = jnp.where(low, total(r), total(r + 1)).astype(BF16)


def rows_kernel(count, n_parts, n_tensor, *refs):
    gathered, cot, outs = refs[:n_parts], refs[n_parts], refs[n_parts + 1:n_parts + 1 + n_tensor]
    ids_vmem, ids, cots, acc, sem = refs[n_parts + 1 + n_tensor:]
    pairs, side = gathered[0].shape[1:3]
    row_count = acc.shape[0] - 1
    rows = cot.shape[0]
    copy = load_ids(gathered, ids_vmem, ids, sem)
    acc[...] = jnp.zeros_like(acc)
    load_cotangent(cot, cots)
    low = low_half((rows, 2 * side))
    copy.wait()

    def add(part, d, i):
        for k in range(pairs):
            left, right = ids[1, i, side + k], ids[1, i, side + k + pairs]
            lhs = cots[left]
            if k + pairs >= count:
                prod = across(lhs[:, :side], part[d, k][:, :side])
                acc[ids[0, i, side + k], :, :side] += prod
            else:
                prod = across(jnp.where(low, lhs, cots[right]), diagonal(part[d, k]))
                acc[ids[0, i, side + k]] += jnp.where(low, prod, 0.0)
                acc[ids[0, i, side + k + pairs]] += jnp.where(low, 0.0, prod)

    over(gathered, add)
    me = lax.axis_index("tensor")
    share = rows // n_tensor
    for k in range(n_tensor):
        start = pl.multiple_of(lax.bitwise_xor(me, k) * share, share)
        half = low_half((share, 2 * side))
        for r in range(0, row_count, 2):
            pair = [fold(acc[r + u, pl.ds(start, share), :]) for u in range(2)]
            outs[k][:, r * side:(r + 2) * side] = jnp.where(half, *pair).astype(BF16)


def forward_kernel(count, n_parts, n_tensor, *refs):
    gathered, tokens = refs[:n_parts], refs[n_parts:n_parts + n_tensor]
    out, ids_vmem, ids, blocks, prod, left_acc, right_acc, stage, sem = refs[n_parts + n_tensor:]
    pairs, side = gathered[0].shape[1:3]
    row_count = blocks.shape[0] - 1
    col_count = left_acc.shape[0] - 1
    rows = blocks.shape[1]
    share = rows // n_tensor
    copy = load_ids(gathered, ids_vmem, ids, sem)
    left_acc[...] = jnp.zeros_like(left_acc)
    right_acc[...] = jnp.zeros_like(right_acc)
    for r in range(0, row_count, 2):
        parts = [tokens[k][:, r * side:(r + 2) * side].astype(F32) for k in range(n_tensor)]
        blocks[r], blocks[r + 1] = twice(jnp.concatenate(parts, axis=0).astype(BF16))
    blocks[row_count] = jnp.zeros_like(blocks[row_count])
    low = low_half((rows, 2 * side))
    copy.wait()

    def multiply(part, d, i):
        for k in range(pairs):
            lhs = blocks[ids[0, i, side + k]]
            if k + pairs < count:
                lhs = jnp.where(low, lhs, blocks[ids[0, i, side + k + pairs]])
                tile = diagonal(part[d, k])
            else:
                lhs, tile = lhs[:, :side], part[d, k]
            prod[i * pairs + k] = jnp.dot(lhs, tile, preferred_element_type=F32)

    def add(part, d, i):
        for k in range(pairs):
            left_acc[ids[1, i, side + k]] += prod[i * pairs + k]
            if k + pairs < count:
                right_acc[ids[1, i, side + k + pairs]] += prod[i * pairs + k]

    over(gathered, multiply)
    over(gathered, add)
    me = lax.axis_index("tensor")
    half = low_half((share, 2 * side))
    for k in range(n_tensor):
        start = pl.multiple_of(lax.bitwise_xor(me, k) * share, share)
        mine = slice(k * share, (k + 1) * share)
        for c in range(0, col_count, 2):
            sums = [fold(jnp.where(half, left_acc[c + u, mine, :], right_acc[c + u, mine, :])) for u in range(2)]
            stage[pl.ds(start, share), c * side:(c + 2) * side] = jnp.where(half, *sums)
    out[...] = stage[...].astype(BF16)


def swap(value, axis, n, k):
    return lax.ppermute(value, axis, [(i, i ^ k) for i in range(n)])


def gather_parts(packed, n_dp):
    if n_dp != 8:
        return [lax.all_gather(packed, "dp", axis=0, tiled=True)]
    near, second, last = [packed, swap(packed, "dp", n_dp, 2)], swap(packed, "dp", n_dp, 4), swap(packed, "dp", n_dp, 6)
    joined = pl.pallas_call(
        join_kernel,
        out_shape=pltpu.VMEM((len(near), *packed.shape[1:]), packed.dtype),
        in_specs=[VMEM] * len(near),
        out_specs=VMEM,
        compiler_params=pltpu.CompilerParams(vmem_limit_bytes=4 * MIB),
    )(*near)
    same_core = [joined, second, last]
    return same_core + [swap(part, "dp", n_dp, 1) for part in same_core]


def on_device(n_dp, n_tensor, inputs, block_values, block_slot, grad_out):
    share, width = inputs.shape
    rows, hidden = grad_out.shape
    _, count, side, _ = block_values.shape
    row_count, col_count = width // side, hidden // side
    pairs = count // 2 + 1
    small = n_dp == 8
    per_slot = small and n_dp * count < row_count and count == 2 * pairs - 1
    params = pltpu.CompilerParams(vmem_limit_bytes=(12 if small else 48) * MIB)

    packed = pl.pallas_call(
        functools.partial(pack_kernel, count, row_count, col_count),
        out_shape=pltpu.VMEM((1, pairs, side, 2 * side), BF16),
        in_specs=[HBM, HBM],
        out_specs=VMEM,
        scratch_shapes=[
            pltpu.SMEM(block_slot.shape, I32),
            pltpu.VMEM(block_values.shape, BF16),
            pltpu.SemaphoreType.DMA((2,)),
        ],
        compiler_params=pltpu.CompilerParams(vmem_limit_bytes=4 * MIB),
    )(
        pltpu.with_memory_space_constraint(block_slot, pltpu.HBM),
        pltpu.with_memory_space_constraint(block_values, pltpu.HBM),
    )
    gathered = gather_parts(packed, n_dp)
    moved = {k: swap(inputs, "tensor", n_tensor, k) for k in range(n_tensor - 1, 0, -1)}
    tokens = [inputs] + [moved[k] for k in range(1, n_tensor)]
    n_parts = len(gathered)
    ids = [pltpu.VMEM((2, n_dp, 2 * side), I32), pltpu.SMEM((2, n_dp, 2 * side), I32)]
    cots = pltpu.VMEM((col_count + 1, rows, 2 * side), BF16)
    tiles = len(slot_tiles(n_dp, pairs))
    if per_slot:
        kernel, shape = slots_kernel, (tiles * share + 2 * n_dp, 2 * side)
        scratch = pltpu.VMEM((tiles, rows, 2 * side), F32)
    else:
        kernel, shape = rows_kernel, (share, width)
        scratch = pltpu.VMEM((row_count + 1, rows, 2 * side), F32)
    partial_sums = pl.pallas_call(
        functools.partial(kernel, count, n_parts, n_tensor),
        out_shape=[jax.ShapeDtypeStruct(shape, BF16)] * n_tensor,
        in_specs=[VMEM] * (n_parts + 1),
        out_specs=[VMEM] * n_tensor,
        scratch_shapes=ids + [cots, scratch, pltpu.SemaphoreType.DMA],
        compiler_params=params,
    )(*gathered, grad_out)
    order = sorted(range(1, n_tensor), key=lambda k: (k != 2, -k))
    received = {k: swap(partial_sums[k], "tensor", n_tensor, k) for k in order}
    arrived = [partial_sums[0]] + [received[k] for k in order]
    outputs = pl.pallas_call(
        functools.partial(forward_kernel, count, n_parts, n_tensor),
        out_shape=jax.ShapeDtypeStruct((rows, hidden), BF16),
        in_specs=[VMEM] * (n_parts + n_tensor),
        out_specs=VMEM,
        scratch_shapes=ids + [
            pltpu.VMEM((row_count + 1, rows, 2 * side), BF16),
            pltpu.VMEM((n_dp * pairs, rows, 2 * side), F32),
            pltpu.VMEM((col_count + 1, rows, 2 * side), F32),
            pltpu.VMEM((col_count + 1, rows, 2 * side), F32),
            pltpu.VMEM((rows, hidden), F32),
            pltpu.SemaphoreType.DMA,
        ],
        compiler_params=params,
    )(*gathered, *tokens)
    if per_slot:
        grad_in = pl.pallas_call(
            functools.partial(sum_kernel, n_tensor, pairs, n_dp),
            out_shape=jax.ShapeDtypeStruct((share, width), BF16),
            in_specs=[VMEM] * n_tensor,
            out_specs=VMEM,
            scratch_shapes=[
                pltpu.VMEM((n_tensor, n_dp, 2 * side), I32),
                pltpu.SMEM((n_tensor, n_dp, 2 * side), I32),
                pltpu.SemaphoreType.DMA,
            ] + [pltpu.VMEM((row_count + 1, share, 2 * side), F32)] * n_tensor,
            compiler_params=params,
        )(*arrived)
    else:
        total = arrived[0].astype(F32)
        for value in arrived[1:]:
            total = total + value.astype(F32)
        grad_in = total.astype(BF16)
    return (outputs, grad_in)


def solution(mesh):
    placed = (
        P(("dp", "tensor"), None),
        P("tensor", "dp", None, None),
        P("tensor", "dp"),
        P("dp", "tensor"),
    )
    return jax.shard_map(
        functools.partial(on_device, mesh.shape["dp"], mesh.shape["tensor"]),
        mesh=mesh,
        in_specs=placed,
        out_specs=(P("dp", "tensor"), P(("dp", "tensor"), None)),
        check_vma=False,
    )
```

```python
import functools

import jax
import jax.numpy as jnp
from jax import lax
from jax.experimental import pallas as pl
from jax.experimental.pallas import tpu as pltpu
from jax.sharding import PartitionSpec as P

VMEM = pl.BlockSpec(memory_space=pltpu.VMEM)
HBM = pl.BlockSpec(memory_space=pltpu.HBM)
MIB = 1024 * 1024
BF16, F32, I32 = jnp.bfloat16, jnp.float32, jnp.int32


def pack_kernel(count, row_count, col_count, slots_hbm, values_hbm, packed, slots, values, sems):
    copies = [
        pltpu.make_async_copy(slots_hbm, slots, sems.at[0]),
        pltpu.make_async_copy(values_hbm, values, sems.at[1]),
    ]
    for copy in copies:
        copy.start()
    side = values.shape[2]
    pairs = packed.shape[1]
    copies[0].wait()
    lane = lax.broadcasted_iota(I32, (side, side), 1)
    line = lax.broadcasted_iota(I32, (side, side), 0)
    head = jnp.zeros((side, side), F32)
    for j in range(count):
        p = slots[0, j]
        row = jnp.where(p >= 0, p // col_count, row_count)
        col = jnp.where(p >= 0, p % col_count, col_count)
        here = jnp.where(line == 0, row, col).astype(F32)
        head = jnp.where(lane == j, here, head)
    head = head.astype(BF16)
    copies[1].wait()
    for k in range(pairs):
        left = values[0, k]
        right = values[0, k + pairs] if k + pairs < count else head
        packed[0, k] = jnp.concatenate([left, right], axis=1)


def join_kernel(*refs):
    for i, part in enumerate(refs[:-1]):
        refs[-1][i] = part[0]


def load_ids(gathered, ids_vmem, ids, sem):
    i = 0
    for part in gathered:
        n, pairs = part.shape[:2]
        for d in range(n):
            head = part[d, pairs - 1, 0:16, :].astype(F32).astype(I32)
            ids_vmem[0, i:i + 1, :] = head[0:1]
            ids_vmem[1, i:i + 1, :] = head[1:2]
            i += 1
    copy = pltpu.make_async_copy(ids_vmem, ids, sem)
    copy.start()
    return copy


def over(gathered, body):
    start = 0
    for part in gathered:
        n = part.shape[0]
        if n <= 8:
            for d in range(n):
                body(part, d, start + d)
        else:
            def step(d, carry, part=part, start=start):
                body(part, d, start + d)
                return carry
            lax.fori_loop(0, n, step, 0)
        start += n


def low_half(shape):
    return lax.broadcasted_iota(I32, shape, 1) < shape[1] // 2


def swap_halves(x):
    half = x.shape[1] // 2
    return jnp.concatenate([x[:, half:], x[:, :half]], axis=1)


def twice(x):
    low, y = low_half(x.shape), swap_halves(x)
    return jnp.where(low, x, y), jnp.where(low, y, x)


def diagonal(tile, other=None):
    low = low_half(tile.shape)
    zero = jnp.zeros_like(tile)
    top = jnp.where(low, tile, zero)
    bottom = jnp.where(low, zero, tile if other is None else swap_halves(other))
    return jnp.concatenate([top, bottom], axis=0)


def fold(x):
    return x + pltpu.roll(x, x.shape[1] // 2, 1)


def across(lhs, rhs):
    return lax.dot_general(lhs, rhs, (((1,), (1,)), ((), ())), preferred_element_type=F32)


def load_cotangent(cot, cots):
    col_count = cots.shape[0] - 1
    for c in range(0, col_count, 2):
        width = cots.shape[2]
        cots[c], cots[c + 1] = twice(cot[:, c * width // 2:(c + 2) * width // 2])
    cots[col_count] = jnp.zeros_like(cots[col_count])


def slots_kernel(count, n_parts, n_tensor, *refs):
    gathered, cot, outs = refs[:n_parts], refs[n_parts], refs[n_parts + 1:n_parts + 1 + n_tensor]
    ids_vmem, ids, cots, prod, sem = refs[n_parts + 1 + n_tensor:]
    pairs, side = gathered[0].shape[1:3]
    rows = cot.shape[0]
    share = rows // n_tensor
    copy = load_ids(gathered, ids_vmem, ids, sem)
    load_cotangent(cot, cots)
    low = low_half((rows, 2 * side))
    heads = jnp.concatenate([ids_vmem[0].astype(F32)] * 2, axis=0).astype(BF16)
    where = [(part, d) for part in gathered for d in range(part.shape[0])]
    copy.wait()
    tiles = slot_tiles(len(where), pairs)
    for t, ((i, j), (m, l)) in enumerate(tiles):
        part, d = where[i]
        other, e = where[m]
        blocks = diagonal(part[d, j]) if i == m else diagonal(part[d, j], other[e, l])
        lhs = jnp.where(low, cots[ids[1, i, side + j]], cots[ids[1, m, side + l]])
        prod[t] = across(lhs, blocks)
    me = lax.axis_index("tensor")
    for k in range(n_tensor):
        start = pl.multiple_of(lax.bitwise_xor(me, k) * share, share)
        for t in range(0, len(tiles), 2):
            two = [prod[t, pl.ds(start, share), :], prod[t + 1, pl.ds(start, share), :]]
            outs[k][t * share:(t + 2) * share, :] = jnp.concatenate(two, axis=0).astype(BF16)
        outs[k][len(tiles) * share:, :] = heads


def slot_tiles(n, pairs):
    full = [((i, j), (i, j + pairs)) for i in range(n) for j in range(pairs - 1)]
    return full + [((i, pairs - 1), (i + 1, pairs - 1)) for i in range(0, n, 2)]


def sum_kernel(n_tensor, pairs, n_dp, *refs):
    messages, out = refs[:n_tensor], refs[n_tensor]
    ids_vmem, ids, sem = refs[n_tensor + 1:n_tensor + 4]
    accs = refs[n_tensor + 4:]
    share, width = out.shape
    side = messages[0].shape[1] // 2
    tiles = slot_tiles(n_dp, pairs)
    for m, message in enumerate(messages):
        ids_vmem[m] = message[len(tiles) * share:, :].astype(F32)[:n_dp].astype(I32)
    copy = pltpu.make_async_copy(ids_vmem, ids, sem)
    copy.start()
    for acc in accs:
        acc[...] = jnp.zeros_like(acc)
    low = low_half((share, 2 * side))
    copy.wait()
    for t in range(0, len(tiles), 2):
        both = [message[t * share:(t + 2) * share, :].astype(F32) for message in messages]
        for u in range(2):
            values = [two[u * share:(u + 1) * share] for two in both]
            for h, (i, j) in enumerate(tiles[t + u]):
                rows = [ids[m, i, side + j] for m in range(n_tensor)]
                halves = [jnp.where(low, 0.0, value) if h else jnp.where(low, value, 0.0) for value in values]
                sums = [acc[row] + half for acc, row, half in zip(accs, rows, halves)]
                for acc, row, value in zip(accs, rows, sums):
                    acc[row] = value

    def total(r):
        value = accs[0][r]
        for acc in accs[1:]:
            value = value + acc[r]
        return fold(value)

    for r in range(0, width // side, 2):
        out[:, r * side:(r + 2) * side] = jnp.where(low, total(r), total(r + 1)).astype(BF16)


def rows_kernel(count, n_parts, n_tensor, *refs):
    gathered, cot, outs = refs[:n_parts], refs[n_parts], refs[n_parts + 1:n_parts + 1 + n_tensor]
    ids_vmem, ids, cots, acc, sem = refs[n_parts + 1 + n_tensor:]
    pairs, side = gathered[0].shape[1:3]
    row_count = acc.shape[0] - 1
    rows = cot.shape[0]
    copy = load_ids(gathered, ids_vmem, ids, sem)
    acc[...] = jnp.zeros_like(acc)
    load_cotangent(cot, cots)
    low = low_half((rows, 2 * side))
    copy.wait()

    def add(part, d, i):
        for k in range(pairs):
            left, right = ids[1, i, side + k], ids[1, i, side + k + pairs]
            lhs = cots[left]
            if k + pairs >= count:
                prod = across(lhs[:, :side], part[d, k][:, :side])
                acc[ids[0, i, side + k], :, :side] += prod
            else:
                prod = across(jnp.where(low, lhs, cots[right]), diagonal(part[d, k]))
                acc[ids[0, i, side + k]] += jnp.where(low, prod, 0.0)
                acc[ids[0, i, side + k + pairs]] += jnp.where(low, 0.0, prod)

    over(gathered, add)
    me = lax.axis_index("tensor")
    share = rows // n_tensor
    for k in range(n_tensor):
        start = pl.multiple_of(lax.bitwise_xor(me, k) * share, share)
        half = low_half((share, 2 * side))
        for r in range(0, row_count, 2):
            pair = [fold(acc[r + u, pl.ds(start, share), :]) for u in range(2)]
            outs[k][:, r * side:(r + 2) * side] = jnp.where(half, *pair).astype(BF16)


def forward_kernel(count, n_parts, n_tensor, *refs):
    gathered, tokens = refs[:n_parts], refs[n_parts:n_parts + n_tensor]
    out, ids_vmem, ids, blocks, prod, left_acc, right_acc, stage, sem = refs[n_parts + n_tensor:]
    pairs, side = gathered[0].shape[1:3]
    row_count = blocks.shape[0] - 1
    col_count = left_acc.shape[0] - 1
    rows = blocks.shape[1]
    share = rows // n_tensor
    copy = load_ids(gathered, ids_vmem, ids, sem)
    left_acc[...] = jnp.zeros_like(left_acc)
    right_acc[...] = jnp.zeros_like(right_acc)
    for r in range(0, row_count, 2):
        parts = [tokens[k][:, r * side:(r + 2) * side].astype(F32) for k in range(n_tensor)]
        blocks[r], blocks[r + 1] = twice(jnp.concatenate(parts, axis=0).astype(BF16))
    blocks[row_count] = jnp.zeros_like(blocks[row_count])
    low = low_half((rows, 2 * side))
    copy.wait()

    def multiply(part, d, i):
        for k in range(pairs):
            lhs = blocks[ids[0, i, side + k]]
            if k + pairs < count:
                lhs = jnp.where(low, lhs, blocks[ids[0, i, side + k + pairs]])
                tile = diagonal(part[d, k])
            else:
                lhs, tile = lhs[:, :side], part[d, k]
            prod[i * pairs + k] = jnp.dot(lhs, tile, preferred_element_type=F32)

    def add(part, d, i):
        for k in range(pairs):
            value, left = prod[i * pairs + k], ids[1, i, side + k]
            left_sum = left_acc[left] + value
            if k + pairs < count:
                right = ids[1, i, side + k + pairs]
                right_sum = right_acc[right] + value
                right_acc[right] = right_sum
            left_acc[left] = left_sum

    over(gathered, multiply)
    over(gathered, add)
    me = lax.axis_index("tensor")
    half = low_half((share, 2 * side))
    for k in range(n_tensor):
        start = pl.multiple_of(lax.bitwise_xor(me, k) * share, share)
        mine = slice(k * share, (k + 1) * share)
        for c in range(0, col_count, 2):
            sums = [fold(jnp.where(half, left_acc[c + u, mine, :], right_acc[c + u, mine, :])) for u in range(2)]
            stage[pl.ds(start, share), c * side:(c + 2) * side] = jnp.where(half, *sums)
    out[...] = stage[...].astype(BF16)


def swap(value, axis, n, k):
    return lax.ppermute(value, axis, [(i, i ^ k) for i in range(n)])


def gather_parts(packed, n_dp):
    if n_dp != 8:
        return [lax.all_gather(packed, "dp", axis=0, tiled=True)]
    near, second, last = [packed, swap(packed, "dp", n_dp, 2)], swap(packed, "dp", n_dp, 4), swap(packed, "dp", n_dp, 6)
    joined = pl.pallas_call(
        join_kernel,
        out_shape=pltpu.VMEM((len(near), *packed.shape[1:]), packed.dtype),
        in_specs=[VMEM] * len(near),
        out_specs=VMEM,
        compiler_params=pltpu.CompilerParams(vmem_limit_bytes=4 * MIB),
    )(*near)
    same_core = [joined, second, last]
    return same_core + [swap(part, "dp", n_dp, 1) for part in same_core]


def on_device(n_dp, n_tensor, inputs, block_values, block_slot, grad_out):
    share, width = inputs.shape
    rows, hidden = grad_out.shape
    _, count, side, _ = block_values.shape
    row_count, col_count = width // side, hidden // side
    pairs = count // 2 + 1
    small = n_dp == 8
    per_slot = small and n_dp * count < row_count and count == 2 * pairs - 1
    params = pltpu.CompilerParams(vmem_limit_bytes=(12 if small else 48) * MIB)

    packed = pl.pallas_call(
        functools.partial(pack_kernel, count, row_count, col_count),
        out_shape=pltpu.VMEM((1, pairs, side, 2 * side), BF16),
        in_specs=[HBM, HBM],
        out_specs=VMEM,
        scratch_shapes=[
            pltpu.SMEM(block_slot.shape, I32),
            pltpu.VMEM(block_values.shape, BF16),
            pltpu.SemaphoreType.DMA((2,)),
        ],
        compiler_params=pltpu.CompilerParams(vmem_limit_bytes=4 * MIB),
    )(
        pltpu.with_memory_space_constraint(block_slot, pltpu.HBM),
        pltpu.with_memory_space_constraint(block_values, pltpu.HBM),
    )
    gathered = gather_parts(packed, n_dp)
    tokens = [inputs]
    while len(tokens) < n_tensor:
        tokens = tokens + [swap(value, "tensor", n_tensor, len(tokens)) for value in tokens]
    n_parts = len(gathered)
    ids = [pltpu.VMEM((2, n_dp, 2 * side), I32), pltpu.SMEM((2, n_dp, 2 * side), I32)]
    cots = pltpu.VMEM((col_count + 1, rows, 2 * side), BF16)
    tiles = len(slot_tiles(n_dp, pairs))
    if per_slot:
        kernel, shape = slots_kernel, (tiles * share + 2 * n_dp, 2 * side)
        scratch = pltpu.VMEM((tiles, rows, 2 * side), F32)
    else:
        kernel, shape = rows_kernel, (share, width)
        scratch = pltpu.VMEM((row_count + 1, rows, 2 * side), F32)
    partial_sums = pl.pallas_call(
        functools.partial(kernel, count, n_parts, n_tensor),
        out_shape=[jax.ShapeDtypeStruct(shape, BF16)] * n_tensor,
        in_specs=[VMEM] * (n_parts + 1),
        out_specs=[VMEM] * n_tensor,
        scratch_shapes=ids + [cots, scratch, pltpu.SemaphoreType.DMA],
        compiler_params=params,
    )(*gathered, grad_out)
    order = sorted(range(1, n_tensor), key=lambda k: (k != 2, -k))
    received = {k: swap(partial_sums[k], "tensor", n_tensor, k) for k in order}
    arrived = [partial_sums[0]] + [received[k] for k in order]
    outputs = pl.pallas_call(
        functools.partial(forward_kernel, count, n_parts, n_tensor),
        out_shape=jax.ShapeDtypeStruct((rows, hidden), BF16),
        in_specs=[VMEM] * (n_parts + n_tensor),
        out_specs=VMEM,
        scratch_shapes=ids + [
            pltpu.VMEM((row_count + 1, rows, 2 * side), BF16),
            pltpu.VMEM((n_dp * pairs, rows, 2 * side), F32),
            pltpu.VMEM((col_count + 1, rows, 2 * side), F32),
            pltpu.VMEM((col_count + 1, rows, 2 * side), F32),
            pltpu.VMEM((rows, hidden), F32),
            pltpu.SemaphoreType.DMA,
        ],
        compiler_params=params,
    )(*gathered, *tokens)
    if per_slot:
        grad_in = pl.pallas_call(
            functools.partial(sum_kernel, n_tensor, pairs, n_dp),
            out_shape=jax.ShapeDtypeStruct((share, width), BF16),
            in_specs=[VMEM] * n_tensor,
            out_specs=VMEM,
            scratch_shapes=[
                pltpu.VMEM((n_tensor, n_dp, 2 * side), I32),
                pltpu.SMEM((n_tensor, n_dp, 2 * side), I32),
                pltpu.SemaphoreType.DMA,
            ] + [pltpu.VMEM((row_count + 1, share, 2 * side), F32)] * n_tensor,
            compiler_params=params,
        )(*arrived)
    else:
        total = arrived[0].astype(F32)
        for value in arrived[1:]:
            total = total + value.astype(F32)
        grad_in = total.astype(BF16)
    return (outputs, grad_in)


def solution(mesh):
    placed = (
        P(("dp", "tensor"), None),
        P("tensor", "dp", None, None),
        P("tensor", "dp"),
        P("dp", "tensor"),
    )
    return jax.shard_map(
        functools.partial(on_device, mesh.shape["dp"], mesh.shape["tensor"]),
        mesh=mesh,
        in_specs=placed,
        out_specs=(P("dp", "tensor"), P(("dp", "tensor"), None)),
        check_vma=False,
    )
```

```python
import functools

import jax
import jax.numpy as jnp
from jax import lax
from jax.experimental import pallas as pl
from jax.experimental.pallas import tpu as pltpu
from jax.sharding import PartitionSpec as P

VMEM = pl.BlockSpec(memory_space=pltpu.VMEM)
HBM = pl.BlockSpec(memory_space=pltpu.HBM)
MIB = 1024 * 1024
BF16, F32, I32 = jnp.bfloat16, jnp.float32, jnp.int32


def pack_kernel(count, row_count, col_count, slots_hbm, values_hbm, packed, slots, values, sems):
    copies = [
        pltpu.make_async_copy(slots_hbm, slots, sems.at[0]),
        pltpu.make_async_copy(values_hbm, values, sems.at[1]),
    ]
    for copy in copies:
        copy.start()
    side = values.shape[2]
    pairs = packed.shape[1]
    copies[0].wait()
    lane = lax.broadcasted_iota(I32, (side, side), 1)
    line = lax.broadcasted_iota(I32, (side, side), 0)
    head = jnp.zeros((side, side), F32)
    for j in range(count):
        p = slots[0, j]
        row = jnp.where(p >= 0, p // col_count, row_count)
        col = jnp.where(p >= 0, p % col_count, col_count)
        here = jnp.where(line == 0, row, col).astype(F32)
        head = jnp.where(lane == j, here, head)
    head = head.astype(BF16)
    copies[1].wait()
    for k in range(pairs):
        left = values[0, k]
        right = values[0, k + pairs] if k + pairs < count else head
        packed[0, k] = jnp.concatenate([left, right], axis=1)


def join_kernel(n, *refs):
    for i, part in enumerate(refs[:n]):
        refs[-1][i] = part[0]


def load_ids(gathered, ids_vmem, ids, sem):
    i = 0
    for part in gathered:
        n, pairs = part.shape[:2]
        for d in range(n):
            head = part[d, pairs - 1, 0:16, :].astype(F32).astype(I32)
            ids_vmem[0, i:i + 1, :] = head[0:1]
            ids_vmem[1, i:i + 1, :] = head[1:2]
            i += 1
    copy = pltpu.make_async_copy(ids_vmem, ids, sem)
    copy.start()
    return copy


def over(gathered, body):
    start = 0
    for part in gathered:
        n = part.shape[0]
        if n <= 8:
            for d in range(n):
                body(part, d, start + d)
        else:
            def step(d, carry, part=part, start=start):
                body(part, d, start + d)
                return carry
            lax.fori_loop(0, n, step, 0)
        start += n


def low_half(shape):
    return lax.broadcasted_iota(I32, shape, 1) < shape[1] // 2


def swap_halves(x):
    half = x.shape[1] // 2
    return jnp.concatenate([x[:, half:], x[:, :half]], axis=1)


def twice(x):
    low, y = low_half(x.shape), swap_halves(x)
    return jnp.where(low, x, y), jnp.where(low, y, x)


def diagonal(tile, other=None):
    low = low_half(tile.shape)
    zero = jnp.zeros_like(tile)
    top = jnp.where(low, tile, zero)
    bottom = jnp.where(low, zero, tile if other is None else swap_halves(other))
    return jnp.concatenate([top, bottom], axis=0)


def fold(x):
    return x + pltpu.roll(x, x.shape[1] // 2, 1)


def across(lhs, rhs):
    return lax.dot_general(lhs, rhs, (((1,), (1,)), ((), ())), preferred_element_type=F32)


def load_cotangent(cot, cots):
    col_count = cots.shape[0] - 1
    for c in range(0, col_count, 2):
        width = cots.shape[2]
        cots[c], cots[c + 1] = twice(cot[:, c * width // 2:(c + 2) * width // 2])
    cots[col_count] = jnp.zeros_like(cots[col_count])


def slots_kernel(count, n_parts, n_tensor, *refs):
    gathered, cot, outs = refs[:n_parts], refs[n_parts], refs[n_parts + 1:n_parts + 1 + n_tensor]
    ids_vmem, ids, cots, prod, sem = refs[n_parts + 1 + n_tensor:]
    pairs, side = gathered[0].shape[1:3]
    rows = cot.shape[0]
    share = rows // n_tensor
    copy = load_ids(gathered, ids_vmem, ids, sem)
    load_cotangent(cot, cots)
    low = low_half((rows, 2 * side))
    heads = jnp.concatenate([ids_vmem[0].astype(F32)] * 2, axis=0).astype(BF16)
    where = [(part, d) for part in gathered for d in range(part.shape[0])]
    copy.wait()
    tiles = slot_tiles(len(where), pairs)
    for t, ((i, j), (m, l)) in enumerate(tiles):
        part, d = where[i]
        other, e = where[m]
        blocks = diagonal(part[d, j]) if i == m else diagonal(part[d, j], other[e, l])
        lhs = jnp.where(low, cots[ids[1, i, side + j]], cots[ids[1, m, side + l]])
        prod[t] = across(lhs, blocks)
    me = lax.axis_index("tensor")
    for k in range(n_tensor):
        start = pl.multiple_of(lax.bitwise_xor(me, k) * share, share)
        for t in range(0, len(tiles), 2):
            two = [prod[t, pl.ds(start, share), :], prod[t + 1, pl.ds(start, share), :]]
            outs[k][t * share:(t + 2) * share, :] = jnp.concatenate(two, axis=0).astype(BF16)
        outs[k][len(tiles) * share:, :] = heads


def slot_tiles(n, pairs):
    full = [((i, j), (i, j + pairs)) for i in range(n) for j in range(pairs - 1)]
    return full + [((i, pairs - 1), (i + 1, pairs - 1)) for i in range(0, n, 2)]


def sum_kernel(n_tensor, pairs, n_dp, *refs):
    messages, out = refs[:n_tensor], refs[n_tensor]
    ids_vmem, ids, sem = refs[n_tensor + 1:n_tensor + 4]
    accs = refs[n_tensor + 4:]
    share, width = out.shape
    side = messages[0].shape[1] // 2
    tiles = slot_tiles(n_dp, pairs)
    for m, message in enumerate(messages):
        ids_vmem[m] = message[len(tiles) * share:, :].astype(F32)[:n_dp].astype(I32)
    copy = pltpu.make_async_copy(ids_vmem, ids, sem)
    copy.start()
    for acc in accs:
        acc[...] = jnp.zeros_like(acc)
    low = low_half((share, 2 * side))
    copy.wait()
    for t in range(0, len(tiles), 2):
        both = [message[t * share:(t + 2) * share, :].astype(F32) for message in messages]
        for u in range(2):
            values = [two[u * share:(u + 1) * share] for two in both]
            for h, (i, j) in enumerate(tiles[t + u]):
                rows = [ids[m, i, side + j] for m in range(n_tensor)]
                halves = [jnp.where(low, 0.0, value) if h else jnp.where(low, value, 0.0) for value in values]
                sums = [acc[row] + half for acc, row, half in zip(accs, rows, halves)]
                for acc, row, value in zip(accs, rows, sums):
                    acc[row] = value

    def total(r):
        value = accs[0][r]
        for acc in accs[1:]:
            value = value + acc[r]
        return fold(value)

    for r in range(0, width // side, 2):
        out[:, r * side:(r + 2) * side] = jnp.where(low, total(r), total(r + 1)).astype(BF16)


def rows_kernel(count, n_parts, n_tensor, *refs):
    gathered, cot, outs = refs[:n_parts], refs[n_parts], refs[n_parts + 1:n_parts + 1 + n_tensor]
    ids_vmem, ids, cots, acc, sem = refs[n_parts + 1 + n_tensor:]
    pairs, side = gathered[0].shape[1:3]
    row_count = acc.shape[0] - 1
    rows = cot.shape[0]
    copy = load_ids(gathered, ids_vmem, ids, sem)
    acc[...] = jnp.zeros_like(acc)
    load_cotangent(cot, cots)
    low = low_half((rows, 2 * side))
    copy.wait()

    def add(part, d, i):
        for k in range(pairs):
            left, right = ids[1, i, side + k], ids[1, i, side + k + pairs]
            lhs = cots[left]
            if k + pairs >= count:
                prod = across(lhs[:, :side], part[d, k][:, :side])
                acc[ids[0, i, side + k], :, :side] += prod
            else:
                prod = across(jnp.where(low, lhs, cots[right]), diagonal(part[d, k]))
                acc[ids[0, i, side + k]] += jnp.where(low, prod, 0.0)
                acc[ids[0, i, side + k + pairs]] += jnp.where(low, 0.0, prod)

    over(gathered, add)
    me = lax.axis_index("tensor")
    share = rows // n_tensor
    for k in range(n_tensor):
        start = pl.multiple_of(lax.bitwise_xor(me, k) * share, share)
        half = low_half((share, 2 * side))
        for r in range(0, row_count, 2):
            pair = [fold(acc[r + u, pl.ds(start, share), :]) for u in range(2)]
            outs[k][:, r * side:(r + 2) * side] = jnp.where(half, *pair).astype(BF16)


def forward_kernel(count, n_parts, n_tensor, *refs):
    gathered, tokens = refs[:n_parts], refs[n_parts:n_parts + n_tensor]
    out, ids_vmem, ids, blocks, prod, left_acc, right_acc, stage, sem = refs[n_parts + n_tensor:]
    pairs, side = gathered[0].shape[1:3]
    row_count = blocks.shape[0] - 1
    col_count = left_acc.shape[0] - 1
    rows = blocks.shape[1]
    share = rows // n_tensor
    copy = load_ids(gathered, ids_vmem, ids, sem)
    left_acc[...] = jnp.zeros_like(left_acc)
    right_acc[...] = jnp.zeros_like(right_acc)
    for r in range(0, row_count, 2):
        parts = [tokens[k][:, r * side:(r + 2) * side].astype(F32) for k in range(n_tensor)]
        blocks[r], blocks[r + 1] = twice(jnp.concatenate(parts, axis=0).astype(BF16))
    blocks[row_count] = jnp.zeros_like(blocks[row_count])
    low = low_half((rows, 2 * side))
    copy.wait()

    def multiply(part, d, i):
        for k in range(pairs):
            lhs = blocks[ids[0, i, side + k]]
            if k + pairs < count:
                lhs = jnp.where(low, lhs, blocks[ids[0, i, side + k + pairs]])
                tile = diagonal(part[d, k])
            else:
                lhs, tile = lhs[:, :side], part[d, k]
            prod[i * pairs + k] = jnp.dot(lhs, tile, preferred_element_type=F32)

    def add(part, d, i):
        for k in range(pairs):
            value, left = prod[i * pairs + k], ids[1, i, side + k]
            left_sum = left_acc[left] + value
            if k + pairs < count:
                right = ids[1, i, side + k + pairs]
                right_sum = right_acc[right] + value
                right_acc[right] = right_sum
            left_acc[left] = left_sum

    over(gathered, multiply)
    over(gathered, add)
    me = lax.axis_index("tensor")
    half = low_half((share, 2 * side))
    for k in range(n_tensor):
        start = pl.multiple_of(lax.bitwise_xor(me, k) * share, share)
        mine = slice(k * share, (k + 1) * share)
        for c in range(0, col_count, 2):
            sums = [fold(jnp.where(half, left_acc[c + u, mine, :], right_acc[c + u, mine, :])) for u in range(2)]
            stage[pl.ds(start, share), c * side:(c + 2) * side] = jnp.where(half, *sums)
    out[...] = stage[...].astype(BF16)


def swap(value, axis, n, k):
    return lax.ppermute(value, axis, [(i, i ^ k) for i in range(n)])


def gather_parts(packed, n_dp, early):
    if n_dp != 8:
        return [lax.all_gather(packed, "dp", axis=0, tiled=True)]
    near, second, last = [packed, swap(packed, "dp", n_dp, 2)], swap(packed, "dp", n_dp, 4), swap(packed, "dp", n_dp, 6)
    joined = pl.pallas_call(
        functools.partial(join_kernel, len(near)),
        out_shape=pltpu.VMEM((len(near), *packed.shape[1:]), packed.dtype),
        in_specs=[VMEM] * len(near) + [pl.BlockSpec(memory_space=pl.ANY)] * len(early),
        out_specs=VMEM,
        compiler_params=pltpu.CompilerParams(vmem_limit_bytes=4 * MIB),
    )(*near, *early)
    same_core = [joined, second, last]
    return same_core + [swap(part, "dp", n_dp, 1) for part in same_core]


def on_device(n_dp, n_tensor, inputs, block_values, block_slot, grad_out):
    share, width = inputs.shape
    rows, hidden = grad_out.shape
    _, count, side, _ = block_values.shape
    row_count, col_count = width // side, hidden // side
    pairs = count // 2 + 1
    small = n_dp == 8
    per_slot = small and n_dp * count < row_count and count == 2 * pairs - 1
    params = pltpu.CompilerParams(vmem_limit_bytes=(12 if small else 48) * MIB)

    packed = pl.pallas_call(
        functools.partial(pack_kernel, count, row_count, col_count),
        out_shape=pltpu.VMEM((1, pairs, side, 2 * side), BF16),
        in_specs=[HBM, HBM],
        out_specs=VMEM,
        scratch_shapes=[
            pltpu.SMEM(block_slot.shape, I32),
            pltpu.VMEM(block_values.shape, BF16),
            pltpu.SemaphoreType.DMA((2,)),
        ],
        compiler_params=pltpu.CompilerParams(vmem_limit_bytes=4 * MIB),
    )(
        pltpu.with_memory_space_constraint(block_slot, pltpu.HBM),
        pltpu.with_memory_space_constraint(block_values, pltpu.HBM),
    )
    tokens = [inputs]
    while len(tokens) < n_tensor:
        tokens = tokens + [swap(value, "tensor", n_tensor, len(tokens)) for value in tokens]
    gathered = gather_parts(packed, n_dp, tokens[1:3])
    n_parts = len(gathered)
    ids = [pltpu.VMEM((2, n_dp, 2 * side), I32), pltpu.SMEM((2, n_dp, 2 * side), I32)]
    cots = pltpu.VMEM((col_count + 1, rows, 2 * side), BF16)
    tiles = len(slot_tiles(n_dp, pairs))
    if per_slot:
        kernel, shape = slots_kernel, (tiles * share + 2 * n_dp, 2 * side)
        scratch = pltpu.VMEM((tiles, rows, 2 * side), F32)
    else:
        kernel, shape = rows_kernel, (share, width)
        scratch = pltpu.VMEM((row_count + 1, rows, 2 * side), F32)
    partial_sums = pl.pallas_call(
        functools.partial(kernel, count, n_parts, n_tensor),
        out_shape=[jax.ShapeDtypeStruct(shape, BF16)] * n_tensor,
        in_specs=[VMEM] * (n_parts + 1),
        out_specs=[VMEM] * n_tensor,
        scratch_shapes=ids + [cots, scratch, pltpu.SemaphoreType.DMA],
        compiler_params=params,
    )(*gathered, grad_out)
    order = sorted(range(1, n_tensor), key=lambda k: (k != 2, -k))
    received = {k: swap(partial_sums[k], "tensor", n_tensor, k) for k in order}
    arrived = [partial_sums[0]] + [received[k] for k in order]
    outputs = pl.pallas_call(
        functools.partial(forward_kernel, count, n_parts, n_tensor),
        out_shape=jax.ShapeDtypeStruct((rows, hidden), BF16),
        in_specs=[VMEM] * (n_parts + n_tensor),
        out_specs=VMEM,
        scratch_shapes=ids + [
            pltpu.VMEM((row_count + 1, rows, 2 * side), BF16),
            pltpu.VMEM((n_dp * pairs, rows, 2 * side), F32),
            pltpu.VMEM((col_count + 1, rows, 2 * side), F32),
            pltpu.VMEM((col_count + 1, rows, 2 * side), F32),
            pltpu.VMEM((rows, hidden), F32),
            pltpu.SemaphoreType.DMA,
        ],
        compiler_params=params,
    )(*gathered, *tokens)
    if per_slot:
        grad_in = pl.pallas_call(
            functools.partial(sum_kernel, n_tensor, pairs, n_dp),
            out_shape=jax.ShapeDtypeStruct((share, width), BF16),
            in_specs=[VMEM] * n_tensor,
            out_specs=VMEM,
            scratch_shapes=[
                pltpu.VMEM((n_tensor, n_dp, 2 * side), I32),
                pltpu.SMEM((n_tensor, n_dp, 2 * side), I32),
                pltpu.SemaphoreType.DMA,
            ] + [pltpu.VMEM((row_count + 1, share, 2 * side), F32)] * n_tensor,
            compiler_params=params,
        )(*arrived)
    else:
        total = arrived[0].astype(F32)
        for value in arrived[1:]:
            total = total + value.astype(F32)
        grad_in = total.astype(BF16)
    return (outputs, grad_in)


def solution(mesh):
    placed = (
        P(("dp", "tensor"), None),
        P("tensor", "dp", None, None),
        P("tensor", "dp"),
        P("dp", "tensor"),
    )
    return jax.shard_map(
        functools.partial(on_device, mesh.shape["dp"], mesh.shape["tensor"]),
        mesh=mesh,
        in_specs=placed,
        out_specs=(P("dp", "tensor"), P(("dp", "tensor"), None)),
        check_vma=False,
    )
```

```python
import functools

import jax
import jax.numpy as jnp
from jax import lax
from jax.experimental import pallas as pl
from jax.experimental.pallas import tpu as pltpu
from jax.sharding import PartitionSpec as P

VMEM = pl.BlockSpec(memory_space=pltpu.VMEM)
HBM = pl.BlockSpec(memory_space=pltpu.HBM)
MIB = 1024 * 1024
BF16, F32, I32 = jnp.bfloat16, jnp.float32, jnp.int32


def pack_kernel(count, row_count, col_count, slots_hbm, values_hbm, packed, slots, values, sems):
    copies = [
        pltpu.make_async_copy(slots_hbm, slots, sems.at[0]),
        pltpu.make_async_copy(values_hbm, values, sems.at[1]),
    ]
    for copy in copies:
        copy.start()
    side = values.shape[2]
    pairs = packed.shape[1]
    copies[0].wait()
    lane = lax.broadcasted_iota(I32, (side, side), 1)
    line = lax.broadcasted_iota(I32, (side, side), 0)
    head = jnp.zeros((side, side), F32)
    for j in range(count):
        p = slots[0, j]
        row = jnp.where(p >= 0, p // col_count, row_count)
        col = jnp.where(p >= 0, p % col_count, col_count)
        here = jnp.where(line == 0, row, col).astype(F32)
        head = jnp.where(lane == j, here, head)
    head = head.astype(BF16)
    copies[1].wait()
    for k in range(pairs):
        left = values[0, k]
        right = values[0, k + pairs] if k + pairs < count else head
        packed[0, k] = jnp.concatenate([left, right], axis=1)


def join_kernel(own, near, tokens, near_tokens, joined, joined_tokens):
    joined[0], joined[1] = own[0], near[0]
    joined_tokens[0], joined_tokens[1] = tokens[...], near_tokens[...]


def load_ids(gathered, ids_vmem, ids, sem):
    i = 0
    for part in gathered:
        n, pairs = part.shape[:2]
        for d in range(n):
            head = part[d, pairs - 1, 0:16, :].astype(F32).astype(I32)
            ids_vmem[0, i:i + 1, :] = head[0:1]
            ids_vmem[1, i:i + 1, :] = head[1:2]
            i += 1
    copy = pltpu.make_async_copy(ids_vmem, ids, sem)
    copy.start()
    return copy


def over(gathered, body):
    start = 0
    for part in gathered:
        n = part.shape[0]
        if n <= 8:
            for d in range(n):
                body(part, d, start + d)
        else:
            def step(d, carry, part=part, start=start):
                body(part, d, start + d)
                return carry
            lax.fori_loop(0, n, step, 0)
        start += n


def low_half(shape):
    return lax.broadcasted_iota(I32, shape, 1) < shape[1] // 2


def swap_halves(x):
    half = x.shape[1] // 2
    return jnp.concatenate([x[:, half:], x[:, :half]], axis=1)


def twice(x):
    low, y = low_half(x.shape), swap_halves(x)
    return jnp.where(low, x, y), jnp.where(low, y, x)


def diagonal(tile, other=None):
    low = low_half(tile.shape)
    zero = jnp.zeros_like(tile)
    top = jnp.where(low, tile, zero)
    bottom = jnp.where(low, zero, tile if other is None else swap_halves(other))
    return jnp.concatenate([top, bottom], axis=0)


def fold(x):
    return x + pltpu.roll(x, x.shape[1] // 2, 1)


def across(lhs, rhs):
    return lax.dot_general(lhs, rhs, (((1,), (1,)), ((), ())), preferred_element_type=F32)


def load_cotangent(cot, cots):
    col_count = cots.shape[0] - 1
    for c in range(0, col_count, 2):
        width = cots.shape[2]
        cots[c], cots[c + 1] = twice(cot[:, c * width // 2:(c + 2) * width // 2])
    cots[col_count] = jnp.zeros_like(cots[col_count])


def slots_kernel(count, n_parts, n_tensor, *refs):
    gathered, cot, outs = refs[:n_parts], refs[n_parts], refs[n_parts + 1:n_parts + 1 + n_tensor]
    ids_vmem, ids, cots, prod, blocks, sem = refs[n_parts + 1 + n_tensor:]
    pairs, side = gathered[0].shape[1:3]
    rows = cot.shape[0]
    share = rows // n_tensor
    copy = load_ids(gathered, ids_vmem, ids, sem)
    load_cotangent(cot, cots)
    low = low_half((rows, 2 * side))
    heads = jnp.concatenate([ids_vmem[0].astype(F32)] * 2, axis=0).astype(BF16)
    where = [(part, d) for part in gathered for d in range(part.shape[0])]
    tiles = slot_tiles(len(where), pairs)
    for t, ((i, j), (m, l)) in enumerate(tiles):
        part, d = where[i]
        other, e = where[m]
        blocks[t] = diagonal(part[d, j]) if i == m else diagonal(part[d, j], other[e, l])
    copy.wait()
    for t, ((i, j), (m, l)) in enumerate(tiles):
        lhs = jnp.where(low, cots[ids[1, i, side + j]], cots[ids[1, m, side + l]])
        prod[t] = across(lhs, blocks[t])
    me = lax.axis_index("tensor")
    for k in range(n_tensor):
        start = pl.multiple_of(lax.bitwise_xor(me, k) * share, share)
        for t in range(0, len(tiles), 2):
            two = [prod[t, pl.ds(start, share), :], prod[t + 1, pl.ds(start, share), :]]
            outs[k][t * share:(t + 2) * share, :] = jnp.concatenate(two, axis=0).astype(BF16)
        outs[k][len(tiles) * share:, :] = heads


def slot_tiles(n, pairs):
    full = [((i, j), (i, j + pairs)) for i in range(n) for j in range(pairs - 1)]
    return full + [((i, pairs - 1), (i + 1, pairs - 1)) for i in range(0, n, 2)]


def sum_kernel(n, pairs, n_dp, *refs):
    messages, before, out = refs[:n], refs[n:-4 - n], refs[-4 - n]
    ids_vmem, ids, sem = refs[-3 - n:-n]
    accs = refs[-n:]
    share, width = out.shape
    side = messages[0].shape[1] // 2
    tiles = slot_tiles(n_dp, pairs)
    for m, message in enumerate(messages):
        ids_vmem[m] = message[len(tiles) * share:, :].astype(F32)[:n_dp].astype(I32)
    copy = pltpu.make_async_copy(ids_vmem, ids, sem)
    copy.start()
    for acc in accs:
        acc[...] = jnp.zeros_like(acc)
    low = low_half((share, 2 * side))
    copy.wait()
    for t in range(0, len(tiles), 2):
        both = [message[t * share:(t + 2) * share, :].astype(F32) for message in messages]
        for u in range(2):
            values = [two[u * share:(u + 1) * share] for two in both]
            for h, (i, j) in enumerate(tiles[t + u]):
                rows = [ids[m, i, side + j] for m in range(n)]
                halves = [jnp.where(low, 0.0, value) if h else jnp.where(low, value, 0.0) for value in values]
                sums = [acc[row] + half for acc, row, half in zip(accs, rows, halves)]
                for acc, row, value in zip(accs, rows, sums):
                    acc[row] = value

    def total(r):
        value = accs[0][r]
        for acc in accs[1:]:
            value = value + acc[r]
        return fold(value)

    for r in range(0, width // side, 2):
        here = slice(r * side, (r + 2) * side)
        value = jnp.where(low, total(r), total(r + 1))
        for earlier in before:
            value = value + earlier[:, here]
        out[:, here] = value.astype(out.dtype)


def add_slots(messages, before, shape, dtype, n_dp, pairs, side, params):
    n, (share, width) = len(messages), shape
    return pl.pallas_call(
        functools.partial(sum_kernel, n, pairs, n_dp),
        out_shape=jax.ShapeDtypeStruct(shape, dtype),
        in_specs=[VMEM] * (n + len(before)),
        out_specs=VMEM,
        scratch_shapes=[
            pltpu.VMEM((n, n_dp, 2 * side), I32),
            pltpu.SMEM((n, n_dp, 2 * side), I32),
            pltpu.SemaphoreType.DMA,
        ] + [pltpu.VMEM((width // side + 1, share, 2 * side), F32)] * n,
        compiler_params=params,
    )(*messages, *before)


def rows_kernel(count, n_parts, n_tensor, *refs):
    gathered, cot, outs = refs[:n_parts], refs[n_parts], refs[n_parts + 1:n_parts + 1 + n_tensor]
    ids_vmem, ids, cots, acc, sem = refs[n_parts + 1 + n_tensor:]
    pairs, side = gathered[0].shape[1:3]
    row_count = acc.shape[0] - 1
    rows = cot.shape[0]
    copy = load_ids(gathered, ids_vmem, ids, sem)
    acc[...] = jnp.zeros_like(acc)
    load_cotangent(cot, cots)
    low = low_half((rows, 2 * side))
    copy.wait()

    def add(part, d, i):
        for k in range(pairs):
            left, right = ids[1, i, side + k], ids[1, i, side + k + pairs]
            lhs = cots[left]
            if k + pairs >= count:
                prod = across(lhs[:, :side], part[d, k][:, :side])
                acc[ids[0, i, side + k], :, :side] += prod
            else:
                prod = across(jnp.where(low, lhs, cots[right]), diagonal(part[d, k]))
                acc[ids[0, i, side + k]] += jnp.where(low, prod, 0.0)
                acc[ids[0, i, side + k + pairs]] += jnp.where(low, 0.0, prod)

    over(gathered, add)
    me = lax.axis_index("tensor")
    share = rows // n_tensor
    for k in range(n_tensor):
        start = pl.multiple_of(lax.bitwise_xor(me, k) * share, share)
        half = low_half((share, 2 * side))
        for r in range(0, row_count, 2):
            pair = [fold(acc[r + u, pl.ds(start, share), :]) for u in range(2)]
            outs[k][:, r * side:(r + 2) * side] = jnp.where(half, *pair).astype(BF16)


def forward_kernel(count, n_parts, n_token_parts, n_tensor, *refs):
    gathered, token_parts = refs[:n_parts], refs[n_parts:n_parts + n_token_parts]
    out, ids_vmem, ids, blocks, prod, left_acc, right_acc, stage, sem = refs[n_parts + n_token_parts:]
    tokens = [part.at[i] for part in token_parts for i in range(part.shape[0])]
    pairs, side = gathered[0].shape[1:3]
    row_count = blocks.shape[0] - 1
    col_count = left_acc.shape[0] - 1
    rows = blocks.shape[1]
    share = rows // n_tensor
    copy = load_ids(gathered, ids_vmem, ids, sem)
    left_acc[...] = jnp.zeros_like(left_acc)
    right_acc[...] = jnp.zeros_like(right_acc)
    for r in range(0, row_count, 2):
        parts = [tokens[k][:, r * side:(r + 2) * side].astype(F32) for k in range(n_tensor)]
        blocks[r], blocks[r + 1] = twice(jnp.concatenate(parts, axis=0).astype(BF16))
    blocks[row_count] = jnp.zeros_like(blocks[row_count])
    low = low_half((rows, 2 * side))
    copy.wait()

    def multiply(part, d, i):
        for k in range(pairs):
            lhs = blocks[ids[0, i, side + k]]
            if k + pairs < count:
                lhs = jnp.where(low, lhs, blocks[ids[0, i, side + k + pairs]])
                tile = diagonal(part[d, k])
            else:
                lhs, tile = lhs[:, :side], part[d, k]
            prod[i * pairs + k] = jnp.dot(lhs, tile, preferred_element_type=F32)

    def add(part, d, i):
        for k in range(pairs):
            value, left = prod[i * pairs + k], ids[1, i, side + k]
            left_sum = left_acc[left] + value
            if k + pairs < count:
                right = ids[1, i, side + k + pairs]
                right_sum = right_acc[right] + value
                right_acc[right] = right_sum
            left_acc[left] = left_sum

    over(gathered, multiply)
    over(gathered, add)
    me = lax.axis_index("tensor")
    half = low_half((share, 2 * side))
    for k in range(n_tensor):
        start = pl.multiple_of(lax.bitwise_xor(me, k) * share, share)
        mine = slice(k * share, (k + 1) * share)
        for c in range(0, col_count, 2):
            sums = [fold(jnp.where(half, left_acc[c + u, mine, :], right_acc[c + u, mine, :])) for u in range(2)]
            stage[pl.ds(start, share), c * side:(c + 2) * side] = jnp.where(half, *sums)
    out[...] = stage[...].astype(BF16)


def swap(value, axis, n, k):
    return lax.ppermute(value, axis, [(i, i ^ k) for i in range(n)])


def gather_all(packed, inputs, n_dp, n_tensor):
    if (n_dp, n_tensor) != (8, 4):
        tokens = [inputs[None]]
        while len(tokens) < n_tensor:
            tokens = tokens + [swap(value, "tensor", n_tensor, len(tokens)) for value in tokens]
        return [lax.all_gather(packed, "dp", axis=0, tiled=True)], tokens
    near_tokens = swap(inputs, "tensor", n_tensor, 1)
    near, second, last = [swap(packed, "dp", n_dp, k) for k in (2, 4, 6)]
    joined, tokens = pl.pallas_call(
        join_kernel,
        out_shape=[
            pltpu.VMEM((2, *packed.shape[1:]), packed.dtype),
            pltpu.VMEM((2, *inputs.shape), inputs.dtype),
        ],
        in_specs=[VMEM] * 4,
        out_specs=[VMEM] * 2,
        compiler_params=pltpu.CompilerParams(vmem_limit_bytes=4 * MIB),
    )(packed, near, inputs, near_tokens)
    same_core = [joined, second, last]
    parts = same_core + [swap(part, "dp", n_dp, 1) for part in same_core]
    return parts, [tokens, swap(tokens, "tensor", n_tensor, 2)]


def on_device(n_dp, n_tensor, inputs, block_values, block_slot, grad_out):
    share, width = inputs.shape
    rows, hidden = grad_out.shape
    _, count, side, _ = block_values.shape
    row_count, col_count = width // side, hidden // side
    pairs = count // 2 + 1
    small = (n_dp, n_tensor) == (8, 4)
    per_slot = small and n_dp * count < row_count and count == 2 * pairs - 1
    params = pltpu.CompilerParams(vmem_limit_bytes=(12 if small else 48) * MIB)

    packed = pl.pallas_call(
        functools.partial(pack_kernel, count, row_count, col_count),
        out_shape=pltpu.VMEM((1, pairs, side, 2 * side), BF16),
        in_specs=[HBM, HBM],
        out_specs=VMEM,
        scratch_shapes=[
            pltpu.SMEM(block_slot.shape, I32),
            pltpu.VMEM(block_values.shape, BF16),
            pltpu.SemaphoreType.DMA((2,)),
        ],
        compiler_params=pltpu.CompilerParams(vmem_limit_bytes=4 * MIB),
    )(
        pltpu.with_memory_space_constraint(block_slot, pltpu.HBM),
        pltpu.with_memory_space_constraint(block_values, pltpu.HBM),
    )
    gathered, tokens = gather_all(packed, inputs, n_dp, n_tensor)
    n_parts = len(gathered)
    ids = [pltpu.VMEM((2, n_dp, 2 * side), I32), pltpu.SMEM((2, n_dp, 2 * side), I32)]
    cots = pltpu.VMEM((col_count + 1, rows, 2 * side), BF16)
    tiles = len(slot_tiles(n_dp, pairs))
    if per_slot:
        kernel, shape = slots_kernel, (tiles * share + 2 * n_dp, 2 * side)
        scratch = [pltpu.VMEM((tiles, rows, 2 * side), F32), pltpu.VMEM((tiles, 2 * side, 2 * side), BF16)]
    else:
        kernel, shape = rows_kernel, (share, width)
        scratch = [pltpu.VMEM((row_count + 1, rows, 2 * side), F32)]
    partial_sums = pl.pallas_call(
        functools.partial(kernel, count, n_parts, n_tensor),
        out_shape=[jax.ShapeDtypeStruct(shape, BF16)] * n_tensor,
        in_specs=[VMEM] * (n_parts + 1),
        out_specs=[VMEM] * n_tensor,
        scratch_shapes=ids + [cots] + scratch + [pltpu.SemaphoreType.DMA],
        compiler_params=params,
    )(*gathered, grad_out)
    order = sorted(range(1, n_tensor), key=lambda k: (k != 2, -k))
    received = {k: swap(partial_sums[k], "tensor", n_tensor, k) for k in order}
    arrived = [partial_sums[0]] + [received[k] for k in order]
    outputs = pl.pallas_call(
        functools.partial(forward_kernel, count, n_parts, len(tokens), n_tensor),
        out_shape=jax.ShapeDtypeStruct((rows, hidden), BF16),
        in_specs=[VMEM] * (n_parts + len(tokens)),
        out_specs=VMEM,
        scratch_shapes=ids + [
            pltpu.VMEM((row_count + 1, rows, 2 * side), BF16),
            pltpu.VMEM((n_dp * pairs, rows, 2 * side), F32),
            pltpu.VMEM((col_count + 1, rows, 2 * side), F32),
            pltpu.VMEM((col_count + 1, rows, 2 * side), F32),
            pltpu.VMEM((rows, hidden), F32),
            pltpu.SemaphoreType.DMA,
        ],
        compiler_params=params,
    )(*gathered, *tokens)
    if per_slot:
        first_sum = add_slots(arrived[:2], [], (share, width), F32, n_dp, pairs, side, params)
        grad_in = add_slots(arrived[2:], [first_sum], (share, width), BF16, n_dp, pairs, side, params)
    else:
        total = arrived[0].astype(F32)
        for value in arrived[1:]:
            total = total + value.astype(F32)
        grad_in = total.astype(BF16)
    return (outputs, grad_in)


def solution(mesh):
    placed = (
        P(("dp", "tensor"), None),
        P("tensor", "dp", None, None),
        P("tensor", "dp"),
        P("dp", "tensor"),
    )
    return jax.shard_map(
        functools.partial(on_device, mesh.shape["dp"], mesh.shape["tensor"]),
        mesh=mesh,
        in_specs=placed,
        out_specs=(P("dp", "tensor"), P(("dp", "tensor"), None)),
        check_vma=False,
    )
```

```python
import functools

import jax
import jax.numpy as jnp
from jax import lax
from jax.experimental import pallas as pl
from jax.experimental.pallas import tpu as pltpu
from jax.sharding import PartitionSpec as P

VMEM = pl.BlockSpec(memory_space=pltpu.VMEM)
HBM = pl.BlockSpec(memory_space=pltpu.HBM)
MIB = 1024 * 1024
BF16, F32, I32 = jnp.bfloat16, jnp.float32, jnp.int32


def pack_kernel(count, row_count, col_count, slots_hbm, values_hbm, packed, slots, values, sems):
    copies = [
        pltpu.make_async_copy(slots_hbm, slots, sems.at[0]),
        pltpu.make_async_copy(values_hbm, values, sems.at[1]),
    ]
    for copy in copies:
        copy.start()
    side = values.shape[2]
    pairs = packed.shape[1]
    copies[0].wait()
    lane = lax.broadcasted_iota(I32, (side, side), 1)
    line = lax.broadcasted_iota(I32, (side, side), 0)
    head = jnp.zeros((side, side), F32)
    for j in range(count):
        p = slots[0, j]
        row = jnp.where(p >= 0, p // col_count, row_count)
        col = jnp.where(p >= 0, p % col_count, col_count)
        here = jnp.where(line == 0, row, col).astype(F32)
        head = jnp.where(lane == j, here, head)
    head = head.astype(BF16)
    copies[1].wait()
    for k in range(pairs):
        left = values[0, k]
        right = values[0, k + pairs] if k + pairs < count else head
        packed[0, k] = jnp.concatenate([left, right], axis=1)


def join_kernel(own, near, tokens, far_tokens, joined, joined_tokens):
    joined[0], joined[1] = own[0], near[0]
    joined_tokens[0], joined_tokens[1] = tokens[...], far_tokens[...]


def load_ids(gathered, ids_vmem, ids, sem):
    i = 0
    for part in gathered:
        n, pairs = part.shape[:2]
        for d in range(n):
            head = part[d, pairs - 1, 0:16, :].astype(F32).astype(I32)
            ids_vmem[0, i:i + 1, :] = head[0:1]
            ids_vmem[1, i:i + 1, :] = head[1:2]
            i += 1
    copy = pltpu.make_async_copy(ids_vmem, ids, sem)
    copy.start()
    return copy


def over(gathered, body):
    start = 0
    for part in gathered:
        n = part.shape[0]
        if n <= 8:
            for d in range(n):
                body(part, d, start + d)
        else:
            def step(d, carry, part=part, start=start):
                body(part, d, start + d)
                return carry
            lax.fori_loop(0, n, step, 0)
        start += n


def low_half(shape):
    return lax.broadcasted_iota(I32, shape, 1) < shape[1] // 2


def swap_halves(x):
    half = x.shape[1] // 2
    return jnp.concatenate([x[:, half:], x[:, :half]], axis=1)


def twice(x):
    low, y = low_half(x.shape), swap_halves(x)
    return jnp.where(low, x, y), jnp.where(low, y, x)


def diagonal(tile, other=None):
    low = low_half(tile.shape)
    zero = jnp.zeros_like(tile)
    top = jnp.where(low, tile, zero)
    bottom = jnp.where(low, zero, tile if other is None else swap_halves(other))
    return jnp.concatenate([top, bottom], axis=0)


def fold(x):
    return x + pltpu.roll(x, x.shape[1] // 2, 1)


def across(lhs, rhs):
    return lax.dot_general(lhs, rhs, (((1,), (1,)), ((), ())), preferred_element_type=F32)


def load_cotangent(cot, cots):
    col_count = cots.shape[0] - 1
    for c in range(0, col_count, 2):
        width = cots.shape[2]
        cots[c], cots[c + 1] = twice(cot[:, c * width // 2:(c + 2) * width // 2])
    cots[col_count] = jnp.zeros_like(cots[col_count])


def slots_kernel(count, n_parts, n_tensor, *refs):
    gathered, cot, outs = refs[:n_parts], refs[n_parts], refs[n_parts + 1:n_parts + 1 + n_tensor]
    ids_vmem, ids, cots, prod, blocks, sem = refs[n_parts + 1 + n_tensor:]
    pairs, side = gathered[0].shape[1:3]
    rows = cot.shape[0]
    share = rows // n_tensor
    copy = load_ids(gathered, ids_vmem, ids, sem)
    load_cotangent(cot, cots)
    low = low_half((rows, 2 * side))
    heads = jnp.concatenate([ids_vmem[0].astype(F32)] * 2, axis=0).astype(BF16)
    where = [(part, d) for part in gathered for d in range(part.shape[0])]
    tiles = slot_tiles(len(where), pairs)
    for t, ((i, j), (m, l)) in enumerate(tiles):
        part, d = where[i]
        other, e = where[m]
        blocks[t] = diagonal(part[d, j]) if i == m else diagonal(part[d, j], other[e, l])
    copy.wait()
    for t, ((i, j), (m, l)) in enumerate(tiles):
        lhs = jnp.where(low, cots[ids[1, i, side + j]], cots[ids[1, m, side + l]])
        prod[t] = across(lhs, blocks[t])
    me = lax.axis_index("tensor")
    for k in range(n_tensor):
        start = pl.multiple_of(lax.bitwise_xor(me, k) * share, share)
        for t in range(0, len(tiles), 2):
            two = [prod[t, pl.ds(start, share), :], prod[t + 1, pl.ds(start, share), :]]
            outs[k][t * share:(t + 2) * share, :] = jnp.concatenate(two, axis=0).astype(BF16)
        outs[k][len(tiles) * share:, :] = heads


def slot_tiles(n, pairs):
    full = [((i, j), (i, j + pairs)) for i in range(n) for j in range(pairs - 1)]
    return full + [((i, pairs - 1), (i + 1, pairs - 1)) for i in range(0, n, 2)]


def rows_kernel(count, n_parts, n_tensor, *refs):
    gathered, cot, outs = refs[:n_parts], refs[n_parts], refs[n_parts + 1:n_parts + 1 + n_tensor]
    ids_vmem, ids, cots, acc, sem = refs[n_parts + 1 + n_tensor:]
    pairs, side = gathered[0].shape[1:3]
    row_count = acc.shape[0] - 1
    rows = cot.shape[0]
    copy = load_ids(gathered, ids_vmem, ids, sem)
    acc[...] = jnp.zeros_like(acc)
    load_cotangent(cot, cots)
    low = low_half((rows, 2 * side))
    copy.wait()

    def add(part, d, i):
        for k in range(pairs):
            left, right = ids[1, i, side + k], ids[1, i, side + k + pairs]
            lhs = cots[left]
            if k + pairs >= count:
                prod = across(lhs[:, :side], part[d, k][:, :side])
                acc[ids[0, i, side + k], :, :side] += prod
            else:
                prod = across(jnp.where(low, lhs, cots[right]), diagonal(part[d, k]))
                acc[ids[0, i, side + k]] += jnp.where(low, prod, 0.0)
                acc[ids[0, i, side + k + pairs]] += jnp.where(low, 0.0, prod)

    over(gathered, add)
    me = lax.axis_index("tensor")
    share = rows // n_tensor
    for k in range(n_tensor):
        start = pl.multiple_of(lax.bitwise_xor(me, k) * share, share)
        half = low_half((share, 2 * side))
        for r in range(0, row_count, 2):
            pair = [fold(acc[r + u, pl.ds(start, share), :]) for u in range(2)]
            outs[k][:, r * side:(r + 2) * side] = jnp.where(half, *pair).astype(BF16)


def load_tokens(token_parts, blocks):
    tokens = [part.at[i] for part in token_parts for i in range(part.shape[0])]
    row_count, width = blocks.shape[0] - 1, blocks.shape[2]
    for r in range(0, row_count, 2):
        parts = [value[:, r * width // 2:(r + 2) * width // 2].astype(F32) for value in tokens]
        blocks[r], blocks[r + 1] = twice(jnp.concatenate(parts, axis=0).astype(BF16))
    blocks[row_count] = jnp.zeros_like(blocks[row_count])


def multiply_tokens(count, gathered, ids, blocks, prod):
    pairs, side = gathered[0].shape[1:3]
    low = low_half(blocks.shape[1:])

    def multiply(part, d, i):
        for k in range(pairs):
            lhs = blocks[ids[0, i, side + k]]
            if k + pairs < count:
                lhs = jnp.where(low, lhs, blocks[ids[0, i, side + k + pairs]])
                tile = diagonal(part[d, k])
            else:
                lhs, tile = lhs[:, :side], part[d, k]
            prod[i * pairs + k] = jnp.dot(lhs, tile, preferred_element_type=F32)

    over(gathered, multiply)


def add_tokens(count, gathered, ids, prod, left_acc, right_acc):
    pairs, side = gathered[0].shape[1:3]

    def add(part, d, i):
        for k in range(pairs):
            value, left = prod[i * pairs + k], ids[1, i, side + k]
            left_sum = left_acc[left] + value
            if k + pairs < count:
                right = ids[1, i, side + k + pairs]
                right_sum = right_acc[right] + value
                right_acc[right] = right_sum
            left_acc[left] = left_sum

    over(gathered, add)


def place_outputs(n_tensor, left_acc, right_acc, stage):
    col_count, rows, width = left_acc.shape[0] - 1, left_acc.shape[1], left_acc.shape[2]
    share = rows // n_tensor
    me = lax.axis_index("tensor")
    half = low_half((share, width))
    for i, k in enumerate(peer_order(n_tensor)):
        start = pl.multiple_of(lax.bitwise_xor(me, k) * share, share)
        mine = slice(i * share, (i + 1) * share)
        for c in range(0, col_count, 2):
            sums = [fold(jnp.where(half, left_acc[c + u, mine, :], right_acc[c + u, mine, :])) for u in range(2)]
            stage[pl.ds(start, share), c * width // 2:(c + 2) * width // 2] = jnp.where(half, *sums)


def forward_kernel(count, n_parts, n_token_parts, n_tensor, *refs):
    gathered, token_parts = refs[:n_parts], refs[n_parts:n_parts + n_token_parts]
    out, ids_vmem, ids, blocks, prod, left_acc, right_acc, stage, sem = refs[n_parts + n_token_parts:]
    copy = load_ids(gathered, ids_vmem, ids, sem)
    left_acc[...] = jnp.zeros_like(left_acc)
    right_acc[...] = jnp.zeros_like(right_acc)
    load_tokens(token_parts, blocks)
    copy.wait()
    multiply_tokens(count, gathered, ids, blocks, prod)
    add_tokens(count, gathered, ids, prod, left_acc, right_acc)
    place_outputs(n_tensor, left_acc, right_acc, stage)
    out[...] = stage[...].astype(BF16)


def last_kernel(count, n_parts, n_token_parts, n_tensor, *refs):
    gathered, refs = refs[:n_parts], refs[n_parts:]
    token_parts, refs = refs[:n_token_parts], refs[n_token_parts:]
    messages, refs = refs[:n_tensor], refs[n_tensor:]
    (out, grad, ids_vmem, ids, blocks, prod, left_acc, right_acc, stage, out_vmem, grad_vmem), refs = refs[:11], refs[11:]
    accs, (id_sem, out_sem, grad_sems) = refs[:n_tensor], refs[n_tensor:]
    pairs, side = gathered[0].shape[1:3]
    n_dp = ids.shape[1]
    share, width = grad.shape
    tiles = slot_tiles(n_dp, pairs)
    for m, message in enumerate(messages):
        ids_vmem[2 + m] = message[len(tiles) * share:, :].astype(F32)[:n_dp].astype(I32)
    copy = load_ids(gathered, ids_vmem, ids, id_sem)
    for acc in (left_acc, right_acc, *accs):
        acc[...] = jnp.zeros_like(acc)
    load_tokens(token_parts, blocks)
    copy.wait()
    multiply_tokens(count, gathered, ids, blocks, prod)
    low = low_half((share, 2 * side))
    for t in range(0, len(tiles), 2):
        both = [message[t * share:(t + 2) * share, :].astype(F32) for message in messages]
        for u in range(2):
            values = [two[u * share:(u + 1) * share] for two in both]
            for h, (i, j) in enumerate(tiles[t + u]):
                rows = [ids[2 + m, i, side + j] for m in range(n_tensor)]
                halves = [jnp.where(low, 0.0, value) if h else jnp.where(low, value, 0.0) for value in values]
                sums = [acc[row] + half for acc, row, half in zip(accs, rows, halves)]
                for acc, row, value in zip(accs, rows, sums):
                    acc[row] = value
    add_tokens(count, gathered, ids, prod, left_acc, right_acc)
    place_outputs(n_tensor, left_acc, right_acc, stage)
    out_vmem[...] = stage[...].astype(BF16)
    copies = [pltpu.make_async_copy(out_vmem, out, out_sem)]
    copies[0].start()

    def total(r):
        value = accs[0][r]
        for acc in accs[1:]:
            value = value + acc[r]
        return fold(value)

    chunk = width // grad_sems.shape[0]
    for c in range(grad_sems.shape[0]):
        for r in range(c * chunk // side, (c + 1) * chunk // side, 2):
            grad_vmem[:, r * side:(r + 2) * side] = jnp.where(low, total(r), total(r + 1)).astype(BF16)
        here = slice(c * chunk, (c + 1) * chunk)
        copies.append(pltpu.make_async_copy(grad_vmem.at[:, here], grad.at[:, here], grad_sems.at[c]))
        copies[-1].start()
    for copy in copies:
        copy.wait()


def steps(n):
    return [n >> i for i in range(1, n.bit_length())]


def peer_order(n):
    order = [0]
    for k in steps(n):
        order = order + [i ^ k for i in order]
    return order


def swap(value, axis, n, k):
    return lax.ppermute(value, axis, [(i, i ^ k) for i in range(n)])


def gather_all(packed, inputs, n_dp, n_tensor):
    if (n_dp, n_tensor) != (8, 4):
        tokens = [inputs[None]]
        for k in steps(n_tensor):
            tokens = tokens + [swap(value, "tensor", n_tensor, k) for value in tokens]
        return [lax.all_gather(packed, "dp", axis=0, tiled=True)], tokens
    far_tokens = swap(inputs, "tensor", n_tensor, 2)
    near, second, last = [swap(packed, "dp", n_dp, k) for k in (2, 4, 6)]
    joined, tokens = pl.pallas_call(
        join_kernel,
        out_shape=[
            pltpu.VMEM((2, *packed.shape[1:]), packed.dtype),
            pltpu.VMEM((2, *inputs.shape), inputs.dtype),
        ],
        in_specs=[VMEM] * 4,
        out_specs=[VMEM] * 2,
        compiler_params=pltpu.CompilerParams(vmem_limit_bytes=4 * MIB),
    )(packed, near, inputs, far_tokens)
    same_core = [joined, second, last]
    parts = same_core + [swap(part, "dp", n_dp, 1) for part in same_core]
    return parts, [tokens, swap(tokens, "tensor", n_tensor, 1)]


def on_device(n_dp, n_tensor, inputs, block_values, block_slot, grad_out):
    share, width = inputs.shape
    rows, hidden = grad_out.shape
    _, count, side, _ = block_values.shape
    row_count, col_count = width // side, hidden // side
    pairs = count // 2 + 1
    small = (n_dp, n_tensor) == (8, 4)
    per_slot = small and n_dp * count < row_count and count == 2 * pairs - 1
    params = pltpu.CompilerParams(vmem_limit_bytes=(12 if small else 48) * MIB)

    packed = pl.pallas_call(
        functools.partial(pack_kernel, count, row_count, col_count),
        out_shape=pltpu.VMEM((1, pairs, side, 2 * side), BF16),
        in_specs=[HBM, HBM],
        out_specs=VMEM,
        scratch_shapes=[
            pltpu.SMEM(block_slot.shape, I32),
            pltpu.VMEM(block_values.shape, BF16),
            pltpu.SemaphoreType.DMA((2,)),
        ],
        compiler_params=pltpu.CompilerParams(vmem_limit_bytes=4 * MIB),
    )(
        pltpu.with_memory_space_constraint(block_slot, pltpu.HBM),
        pltpu.with_memory_space_constraint(block_values, pltpu.HBM),
    )
    gathered, tokens = gather_all(packed, inputs, n_dp, n_tensor)
    n_parts = len(gathered)
    ids = [pltpu.VMEM((2, n_dp, 2 * side), I32), pltpu.SMEM((2, n_dp, 2 * side), I32)]
    cots = pltpu.VMEM((col_count + 1, rows, 2 * side), BF16)
    tiles = len(slot_tiles(n_dp, pairs))
    if per_slot:
        kernel, shape = slots_kernel, (tiles * share + 2 * n_dp, 2 * side)
        scratch = [pltpu.VMEM((tiles, rows, 2 * side), F32), pltpu.VMEM((tiles, 2 * side, 2 * side), BF16)]
    else:
        kernel, shape = rows_kernel, (share, width)
        scratch = [pltpu.VMEM((row_count + 1, rows, 2 * side), F32)]
    partial_sums = pl.pallas_call(
        functools.partial(kernel, count, n_parts, n_tensor),
        out_shape=[jax.ShapeDtypeStruct(shape, BF16)] * n_tensor,
        in_specs=[VMEM] * (n_parts + 1),
        out_specs=[VMEM] * n_tensor,
        scratch_shapes=ids + [cots] + scratch + [pltpu.SemaphoreType.DMA],
        compiler_params=params,
    )(*gathered, grad_out)
    order = range(n_tensor - 1, 0, -1)
    received = {k: swap(partial_sums[k], "tensor", n_tensor, k) for k in order}
    arrived = [partial_sums[0]] + [received[k] for k in order]
    forward = [
        pltpu.VMEM((row_count + 1, rows, 2 * side), BF16),
        pltpu.VMEM((n_dp * pairs, rows, 2 * side), F32),
        pltpu.VMEM((col_count + 1, rows, 2 * side), F32),
        pltpu.VMEM((col_count + 1, rows, 2 * side), F32),
        pltpu.VMEM((rows, hidden), F32),
    ]
    if per_slot:
        return pl.pallas_call(
            functools.partial(last_kernel, count, n_parts, len(tokens), n_tensor),
            out_shape=[
                jax.ShapeDtypeStruct((rows, hidden), BF16),
                jax.ShapeDtypeStruct((share, width), BF16),
            ],
            in_specs=[VMEM] * (n_parts + len(tokens) + n_tensor),
            out_specs=[HBM] * 2,
            scratch_shapes=[
                pltpu.VMEM((2 + n_tensor, n_dp, 2 * side), I32),
                pltpu.SMEM((2 + n_tensor, n_dp, 2 * side), I32),
            ] + forward + [
                pltpu.VMEM((rows, hidden), BF16),
                pltpu.VMEM((share, width), BF16),
            ] + [pltpu.VMEM((row_count + 1, share, 2 * side), F32)] * n_tensor + [
                pltpu.SemaphoreType.DMA,
                pltpu.SemaphoreType.DMA,
                pltpu.SemaphoreType.DMA((4,)),
            ],
            compiler_params=params,
        )(*gathered, *tokens, *arrived)
    outputs = pl.pallas_call(
        functools.partial(forward_kernel, count, n_parts, len(tokens), n_tensor),
        out_shape=jax.ShapeDtypeStruct((rows, hidden), BF16),
        in_specs=[VMEM] * (n_parts + len(tokens)),
        out_specs=VMEM,
        scratch_shapes=ids + forward + [pltpu.SemaphoreType.DMA],
        compiler_params=params,
    )(*gathered, *tokens)
    total = arrived[0].astype(F32)
    for value in arrived[1:]:
        total = total + value.astype(F32)
    return (outputs, total.astype(BF16))


def solution(mesh):
    placed = (
        P(("dp", "tensor"), None),
        P("tensor", "dp", None, None),
        P("tensor", "dp"),
        P("dp", "tensor"),
    )
    return jax.shard_map(
        functools.partial(on_device, mesh.shape["dp"], mesh.shape["tensor"]),
        mesh=mesh,
        in_specs=placed,
        out_specs=(P("dp", "tensor"), P(("dp", "tensor"), None)),
        check_vma=False,
    )
```

```python
import functools

import jax
import jax.numpy as jnp
from jax import lax
from jax.experimental import pallas as pl
from jax.experimental.pallas import tpu as pltpu
from jax.sharding import PartitionSpec as P

VMEM = pl.BlockSpec(memory_space=pltpu.VMEM)
HBM = pl.BlockSpec(memory_space=pltpu.HBM)
MIB = 1024 * 1024
BF16, F32, I32 = jnp.bfloat16, jnp.float32, jnp.int32


def pack_kernel(count, row_count, col_count, slots_hbm, values_hbm, packed, slots, values, sems):
    copies = [
        pltpu.make_async_copy(slots_hbm, slots, sems.at[0]),
        pltpu.make_async_copy(values_hbm, values, sems.at[1]),
    ]
    for copy in copies:
        copy.start()
    side = values.shape[2]
    pairs = packed.shape[1]
    lane = lax.broadcasted_iota(I32, (16, side), 1)
    line = lax.broadcasted_iota(I32, (16, side), 0)
    copies[0].wait()
    position = jnp.full((16, side), -1, I32)
    for j in range(count):
        position = jnp.where(lane == j, slots[0, j], position)
    exact = position.astype(F32)
    row = jnp.floor((exact + 0.5) * (1.0 / col_count))
    col = exact - row * col_count
    row = jnp.where(position >= 0, row, float(row_count))
    col = jnp.where(position >= 0, col, float(col_count))
    head = jnp.where(line == 0, row, col).astype(BF16)
    head = jnp.concatenate([head, jnp.zeros((side - 16, side), BF16)], axis=0)
    copies[1].wait()
    for k in range(pairs):
        left = values[0, k]
        right = values[0, k + pairs] if k + pairs < count else head
        packed[0, k] = jnp.concatenate([left, right], axis=1)


def join_kernel(own, near, tokens, far_tokens, joined, joined_tokens):
    joined[0], joined[1] = own[0], near[0]
    joined_tokens[0], joined_tokens[1] = tokens[...], far_tokens[...]


def load_ids(gathered, ids_vmem, ids, sem):
    i = 0
    for part in gathered:
        n, pairs = part.shape[:2]
        for d in range(n):
            head = part[d, pairs - 1, 0:16, :].astype(F32).astype(I32)
            ids_vmem[0, i:i + 1, :] = head[0:1]
            ids_vmem[1, i:i + 1, :] = head[1:2]
            i += 1
    copy = pltpu.make_async_copy(ids_vmem, ids, sem)
    copy.start()
    return copy


def over(gathered, body):
    start = 0
    for part in gathered:
        n = part.shape[0]
        if n <= 8:
            for d in range(n):
                body(part, d, start + d)
        else:
            def step(d, carry, part=part, start=start):
                body(part, d, start + d)
                return carry
            lax.fori_loop(0, n, step, 0)
        start += n


def low_half(shape):
    return lax.broadcasted_iota(I32, shape, 1) < shape[1] // 2


def swap_halves(x):
    half = x.shape[1] // 2
    return jnp.concatenate([x[:, half:], x[:, :half]], axis=1)


def twice(x):
    low, y = low_half(x.shape), swap_halves(x)
    return jnp.where(low, x, y), jnp.where(low, y, x)


def diagonal(tile, other=None):
    low = low_half(tile.shape)
    zero = jnp.zeros_like(tile)
    top = jnp.where(low, tile, zero)
    bottom = jnp.where(low, zero, tile if other is None else swap_halves(other))
    return jnp.concatenate([top, bottom], axis=0)


def fold(x):
    return x + pltpu.roll(x, x.shape[1] // 2, 1)


def across(lhs, rhs):
    return lax.dot_general(lhs, rhs, (((1,), (1,)), ((), ())), preferred_element_type=F32)


def load_cotangent(cot, cots):
    col_count = cots.shape[0] - 1
    for c in range(0, col_count, 2):
        width = cots.shape[2]
        cots[c], cots[c + 1] = twice(cot[:, c * width // 2:(c + 2) * width // 2])
    cots[col_count] = jnp.zeros_like(cots[col_count])


def slots_kernel(count, n_parts, n_tensor, *refs):
    gathered, cot, outs = refs[:n_parts], refs[n_parts], refs[n_parts + 1:n_parts + 1 + n_tensor]
    ids_vmem, ids, cots, prod, blocks, sem = refs[n_parts + 1 + n_tensor:]
    pairs, side = gathered[0].shape[1:3]
    rows = cot.shape[0]
    share = rows // n_tensor
    copy = load_ids(gathered, ids_vmem, ids, sem)
    load_cotangent(cot, cots)
    low = low_half((rows, 2 * side))
    heads = jnp.concatenate([ids_vmem[0].astype(F32)] * 2, axis=0).astype(BF16)
    where = [(part, d) for part in gathered for d in range(part.shape[0])]
    tiles = slot_tiles(len(where), pairs)
    for t, ((i, j), (m, l)) in enumerate(tiles):
        part, d = where[i]
        other, e = where[m]
        blocks[t] = diagonal(part[d, j]) if i == m else diagonal(part[d, j], other[e, l])
    copy.wait()
    for t, ((i, j), (m, l)) in enumerate(tiles):
        lhs = jnp.where(low, cots[ids[1, i, side + j]], cots[ids[1, m, side + l]])
        prod[t] = across(lhs, blocks[t])
    me = lax.axis_index("tensor")
    for k in range(n_tensor):
        start = pl.multiple_of(lax.rem(me + k, n_tensor) * share, share)
        for t in range(0, len(tiles), 2):
            two = [prod[t, pl.ds(start, share), :], prod[t + 1, pl.ds(start, share), :]]
            outs[k][t * share:(t + 2) * share, :] = jnp.concatenate(two, axis=0).astype(BF16)
        outs[k][len(tiles) * share:, :] = heads


def slot_tiles(n, pairs):
    full = [((i, j), (i, j + pairs)) for i in range(n) for j in range(pairs - 1)]
    return full + [((i, pairs - 1), (i + 1, pairs - 1)) for i in range(0, n, 2)]


def rows_kernel(count, n_parts, n_tensor, *refs):
    gathered, cot, outs = refs[:n_parts], refs[n_parts], refs[n_parts + 1:n_parts + 1 + n_tensor]
    ids_vmem, ids, cots, acc, sem = refs[n_parts + 1 + n_tensor:]
    pairs, side = gathered[0].shape[1:3]
    row_count = acc.shape[0] - 1
    rows = cot.shape[0]
    copy = load_ids(gathered, ids_vmem, ids, sem)
    acc[...] = jnp.zeros_like(acc)
    load_cotangent(cot, cots)
    low = low_half((rows, 2 * side))
    copy.wait()

    def add(part, d, i):
        for k in range(pairs):
            left, right = ids[1, i, side + k], ids[1, i, side + k + pairs]
            lhs = cots[left]
            if k + pairs >= count:
                prod = across(lhs[:, :side], part[d, k][:, :side])
                acc[ids[0, i, side + k], :, :side] += prod
            else:
                prod = across(jnp.where(low, lhs, cots[right]), diagonal(part[d, k]))
                acc[ids[0, i, side + k]] += jnp.where(low, prod, 0.0)
                acc[ids[0, i, side + k + pairs]] += jnp.where(low, 0.0, prod)

    over(gathered, add)
    me = lax.axis_index("tensor")
    share = rows // n_tensor
    for k in range(n_tensor):
        start = pl.multiple_of(lax.rem(me + k, n_tensor) * share, share)
        half = low_half((share, 2 * side))
        for r in range(0, row_count, 2):
            pair = [fold(acc[r + u, pl.ds(start, share), :]) for u in range(2)]
            outs[k][:, r * side:(r + 2) * side] = jnp.where(half, *pair).astype(BF16)


def load_tokens(token_parts, blocks):
    tokens = [part.at[i] for part in token_parts for i in range(part.shape[0])]
    row_count, width = blocks.shape[0] - 1, blocks.shape[2]
    for r in range(0, row_count, 2):
        parts = [value[:, r * width // 2:(r + 2) * width // 2].astype(F32) for value in tokens]
        blocks[r], blocks[r + 1] = twice(jnp.concatenate(parts, axis=0).astype(BF16))
    blocks[row_count] = jnp.zeros_like(blocks[row_count])


def multiply_tokens(count, gathered, ids, blocks, prod):
    pairs, side = gathered[0].shape[1:3]
    low = low_half(blocks.shape[1:])

    def multiply(part, d, i):
        for k in range(pairs):
            lhs = blocks[ids[0, i, side + k]]
            if k + pairs < count:
                lhs = jnp.where(low, lhs, blocks[ids[0, i, side + k + pairs]])
                tile = diagonal(part[d, k])
            else:
                lhs, tile = lhs[:, :side], part[d, k]
            prod[i * pairs + k] = jnp.dot(lhs, tile, preferred_element_type=F32)

    over(gathered, multiply)


def add_tokens(count, gathered, ids, prod, left_acc, right_acc):
    pairs, side = gathered[0].shape[1:3]

    def add(part, d, i):
        for k in range(pairs):
            value, left = prod[i * pairs + k], ids[1, i, side + k]
            left_sum = left_acc[left] + value
            if k + pairs < count:
                right = ids[1, i, side + k + pairs]
                right_sum = right_acc[right] + value
                right_acc[right] = right_sum
            left_acc[left] = left_sum

    over(gathered, add)


def place_outputs(n_tensor, left_acc, right_acc, stage):
    col_count, rows, width = left_acc.shape[0] - 1, left_acc.shape[1], left_acc.shape[2]
    share = rows // n_tensor
    me = lax.axis_index("tensor")
    half = low_half((share, width))
    for i, k in enumerate(peer_order(n_tensor)):
        start = pl.multiple_of(lax.bitwise_xor(me, k) * share, share)
        mine = slice(i * share, (i + 1) * share)
        for c in range(0, col_count, 2):
            sums = [fold(jnp.where(half, left_acc[c + u, mine, :], right_acc[c + u, mine, :])) for u in range(2)]
            stage[pl.ds(start, share), c * width // 2:(c + 2) * width // 2] = jnp.where(half, *sums)


def forward_kernel(count, n_parts, n_token_parts, n_tensor, *refs):
    gathered, token_parts = refs[:n_parts], refs[n_parts:n_parts + n_token_parts]
    out, ids_vmem, ids, blocks, prod, left_acc, right_acc, stage, sem = refs[n_parts + n_token_parts:]
    copy = load_ids(gathered, ids_vmem, ids, sem)
    left_acc[...] = jnp.zeros_like(left_acc)
    right_acc[...] = jnp.zeros_like(right_acc)
    load_tokens(token_parts, blocks)
    copy.wait()
    multiply_tokens(count, gathered, ids, blocks, prod)
    add_tokens(count, gathered, ids, prod, left_acc, right_acc)
    place_outputs(n_tensor, left_acc, right_acc, stage)
    out[...] = stage[...].astype(BF16)


def sum_kernel(n_tensor, pairs, *refs):
    messages, refs = refs[:n_tensor], refs[n_tensor:]
    (grad, ids_vmem, ids, grad_vmem, id_sem, grad_sems), accs = refs[:6], refs[6:]
    n_dp = ids.shape[1]
    share, width = grad.shape
    side = messages[0].shape[1] // 2
    tiles = slot_tiles(n_dp, pairs)
    for m, message in enumerate(messages):
        ids_vmem[m] = message[len(tiles) * share:, :].astype(F32)[:n_dp].astype(I32)
    copy = pltpu.make_async_copy(ids_vmem, ids, id_sem)
    copy.start()
    for acc in accs:
        acc[...] = jnp.zeros_like(acc)
    low = low_half((share, 2 * side))
    copy.wait()
    for t in range(0, len(tiles), 2):
        both = [message[t * share:(t + 2) * share, :].astype(F32) for message in messages]
        for u in range(2):
            values = [two[u * share:(u + 1) * share] for two in both]
            for h, (i, j) in enumerate(tiles[t + u]):
                rows = [ids[m, i, side + j] for m in range(n_tensor)]
                halves = [jnp.where(low, 0.0, value) if h else jnp.where(low, value, 0.0) for value in values]
                sums = [acc[row] + half for acc, row, half in zip(accs, rows, halves)]
                for acc, row, value in zip(accs, rows, sums):
                    acc[row] = value

    def total(r):
        value = accs[0][r]
        for acc in accs[1:]:
            value = value + acc[r]
        return fold(value)

    copies = []
    chunk = width // grad_sems.shape[0]
    for c in range(grad_sems.shape[0]):
        for r in range(c * chunk // side, (c + 1) * chunk // side, 2):
            grad_vmem[:, r * side:(r + 2) * side] = jnp.where(low, total(r), total(r + 1)).astype(BF16)
        here = slice(c * chunk, (c + 1) * chunk)
        copies.append(pltpu.make_async_copy(grad_vmem.at[:, here], grad.at[:, here], grad_sems.at[c]))
        copies[-1].start()
    for copy in copies:
        copy.wait()


def steps(n):
    return [n >> i for i in range(1, n.bit_length())]


def peer_order(n):
    order = [0]
    for k in steps(n):
        order = order + [i ^ k for i in order]
    return order


def swap(value, axis, n, k):
    return lax.ppermute(value, axis, [(i, i ^ k) for i in range(n)])


def shift(value, axis, n, k):
    return lax.ppermute(value, axis, [(i, (i + k) % n) for i in range(n)])


def gather_all(packed, inputs, n_dp, n_tensor):
    if (n_dp, n_tensor) != (8, 4):
        tokens = [inputs[None]]
        for k in steps(n_tensor):
            tokens = tokens + [swap(value, "tensor", n_tensor, k) for value in tokens]
        return [lax.all_gather(packed, "dp", axis=0, tiled=True)], tokens
    far_tokens = swap(inputs, "tensor", n_tensor, 2)
    near, second, last = [swap(packed, "dp", n_dp, k) for k in (2, 4, 6)]
    joined, tokens = pl.pallas_call(
        join_kernel,
        out_shape=[
            pltpu.VMEM((2, *packed.shape[1:]), packed.dtype),
            pltpu.VMEM((2, *inputs.shape), inputs.dtype),
        ],
        in_specs=[VMEM] * 4,
        out_specs=[VMEM] * 2,
        compiler_params=pltpu.CompilerParams(vmem_limit_bytes=4 * MIB),
    )(packed, near, inputs, far_tokens)
    same_core = [joined, second, last]
    parts = same_core + [swap(part, "dp", n_dp, 1) for part in same_core]
    return parts, [tokens, swap(tokens, "tensor", n_tensor, 1)]


def on_device(n_dp, n_tensor, inputs, block_values, block_slot, grad_out):
    share, width = inputs.shape
    rows, hidden = grad_out.shape
    _, count, side, _ = block_values.shape
    row_count, col_count = width // side, hidden // side
    pairs = count // 2 + 1
    small = (n_dp, n_tensor) == (8, 4)
    per_slot = small and n_dp * count < row_count and count == 2 * pairs - 1
    params = pltpu.CompilerParams(vmem_limit_bytes=(12 if small else 48) * MIB)

    packed = pl.pallas_call(
        functools.partial(pack_kernel, count, row_count, col_count),
        out_shape=pltpu.VMEM((1, pairs, side, 2 * side), BF16),
        in_specs=[HBM, HBM],
        out_specs=VMEM,
        scratch_shapes=[
            pltpu.SMEM(block_slot.shape, I32),
            pltpu.VMEM(block_values.shape, BF16),
            pltpu.SemaphoreType.DMA((2,)),
        ],
        compiler_params=pltpu.CompilerParams(vmem_limit_bytes=4 * MIB),
    )(
        pltpu.with_memory_space_constraint(block_slot, pltpu.HBM),
        pltpu.with_memory_space_constraint(block_values, pltpu.HBM),
    )
    gathered, tokens = gather_all(packed, inputs, n_dp, n_tensor)
    n_parts = len(gathered)
    ids = [pltpu.VMEM((2, n_dp, 2 * side), I32), pltpu.SMEM((2, n_dp, 2 * side), I32)]
    cots = pltpu.VMEM((col_count + 1, rows, 2 * side), BF16)
    tiles = len(slot_tiles(n_dp, pairs))
    if per_slot:
        kernel, shape = slots_kernel, (tiles * share + 2 * n_dp, 2 * side)
        scratch = [pltpu.VMEM((tiles, rows, 2 * side), F32), pltpu.VMEM((tiles, 2 * side, 2 * side), BF16)]
    else:
        kernel, shape = rows_kernel, (share, width)
        scratch = [pltpu.VMEM((row_count + 1, rows, 2 * side), F32)]
    partial_sums = pl.pallas_call(
        functools.partial(kernel, count, n_parts, n_tensor),
        out_shape=[jax.ShapeDtypeStruct(shape, BF16)] * n_tensor,
        in_specs=[VMEM] * (n_parts + 1),
        out_specs=[VMEM] * n_tensor,
        scratch_shapes=ids + [cots] + scratch + [pltpu.SemaphoreType.DMA],
        compiler_params=params,
    )(*gathered, grad_out)
    arrived = [partial_sums[0]] + [shift(partial_sums[k], "tensor", n_tensor, k) for k in range(1, n_tensor)]
    outputs = pl.pallas_call(
        functools.partial(forward_kernel, count, n_parts, len(tokens), n_tensor),
        out_shape=jax.ShapeDtypeStruct((rows, hidden), BF16),
        in_specs=[VMEM] * (n_parts + len(tokens)),
        out_specs=VMEM,
        scratch_shapes=ids + [
            pltpu.VMEM((row_count + 1, rows, 2 * side), BF16),
            pltpu.VMEM((n_dp * pairs, rows, 2 * side), F32),
            pltpu.VMEM((col_count + 1, rows, 2 * side), F32),
            pltpu.VMEM((col_count + 1, rows, 2 * side), F32),
            pltpu.VMEM((rows, hidden), F32),
            pltpu.SemaphoreType.DMA,
        ],
        compiler_params=params,
    )(*gathered, *tokens)
    if per_slot:
        grad_in = pl.pallas_call(
            functools.partial(sum_kernel, n_tensor, pairs),
            out_shape=jax.ShapeDtypeStruct((share, width), BF16),
            in_specs=[VMEM] * n_tensor,
            out_specs=HBM,
            scratch_shapes=[
                pltpu.VMEM((n_tensor, n_dp, 2 * side), I32),
                pltpu.SMEM((n_tensor, n_dp, 2 * side), I32),
                pltpu.VMEM((share, width), BF16),
                pltpu.SemaphoreType.DMA,
                pltpu.SemaphoreType.DMA((4,)),
            ] + [pltpu.VMEM((row_count + 1, share, 2 * side), F32)] * n_tensor,
            compiler_params=params,
        )(*arrived)
        return (outputs, grad_in)
    total = arrived[0].astype(F32)
    for value in arrived[1:]:
        total = total + value.astype(F32)
    return (outputs, total.astype(BF16))


def solution(mesh):
    placed = (
        P(("dp", "tensor"), None),
        P("tensor", "dp", None, None),
        P("tensor", "dp"),
        P("dp", "tensor"),
    )
    return jax.shard_map(
        functools.partial(on_device, mesh.shape["dp"], mesh.shape["tensor"]),
        mesh=mesh,
        in_specs=placed,
        out_specs=(P("dp", "tensor"), P(("dp", "tensor"), None)),
        check_vma=False,
    )
```

```python
import functools

import jax
import jax.numpy as jnp
from jax import lax
from jax.experimental import pallas as pl
from jax.experimental.pallas import tpu as pltpu
from jax.sharding import PartitionSpec as P

VMEM = pl.BlockSpec(memory_space=pltpu.VMEM)
HBM = pl.BlockSpec(memory_space=pltpu.HBM)
MIB = 1024 * 1024
BF16, F32, I32 = jnp.bfloat16, jnp.float32, jnp.int32


def pack_kernel(count, row_count, col_count, slots_hbm, values_hbm, packed, slots, values, sems):
    copies = [
        pltpu.make_async_copy(slots_hbm, slots, sems.at[0]),
        pltpu.make_async_copy(values_hbm, values, sems.at[1]),
    ]
    for copy in copies:
        copy.start()
    side = values.shape[2]
    pairs = packed.shape[1]
    lane = lax.broadcasted_iota(I32, (16, side), 1)
    line = lax.broadcasted_iota(I32, (16, side), 0)
    copies[0].wait()
    position = jnp.full((16, side), -1, I32)
    for j in range(count):
        position = jnp.where(lane == j, slots[0, j], position)
    exact = position.astype(F32)
    row = jnp.floor((exact + 0.5) * (1.0 / col_count))
    col = exact - row * col_count
    row = jnp.where(position >= 0, row, float(row_count))
    col = jnp.where(position >= 0, col, float(col_count))
    head = jnp.where(line == 0, row, col).astype(BF16)
    head = jnp.concatenate([head, jnp.zeros((side - 16, side), BF16)], axis=0)
    copies[1].wait()
    for k in range(pairs):
        left = values[0, k]
        right = values[0, k + pairs] if k + pairs < count else head
        packed[0, k] = jnp.concatenate([left, right], axis=1)


def join_kernel(own, near, tokens, far_tokens, joined, joined_tokens):
    joined[0], joined[1] = own[0], near[0]
    joined_tokens[0], joined_tokens[1] = tokens[...], far_tokens[...]


def load_ids(gathered, ids_vmem, ids, sem):
    i = 0
    for part in gathered:
        n, pairs = part.shape[:2]
        for d in range(n):
            head = part[d, pairs - 1, 0:16, :].astype(F32).astype(I32)
            ids_vmem[0, i:i + 1, :] = head[0:1]
            ids_vmem[1, i:i + 1, :] = head[1:2]
            i += 1
    copy = pltpu.make_async_copy(ids_vmem, ids, sem)
    copy.start()
    return copy


def over(gathered, body):
    start = 0
    for part in gathered:
        n = part.shape[0]
        if n <= 8:
            for d in range(n):
                body(part, d, start + d)
        else:
            def step(d, carry, part=part, start=start):
                body(part, d, start + d)
                return carry
            lax.fori_loop(0, n, step, 0)
        start += n


def low_half(shape):
    return lax.broadcasted_iota(I32, shape, 1) < shape[1] // 2


def swap_halves(x):
    half = x.shape[1] // 2
    return jnp.concatenate([x[:, half:], x[:, :half]], axis=1)


def twice(x):
    low, y = low_half(x.shape), swap_halves(x)
    return jnp.where(low, x, y), jnp.where(low, y, x)


def diagonal(tile, other=None):
    low = low_half(tile.shape)
    zero = jnp.zeros_like(tile)
    top = jnp.where(low, tile, zero)
    bottom = jnp.where(low, zero, tile if other is None else swap_halves(other))
    return jnp.concatenate([top, bottom], axis=0)


def fold(x):
    return x + pltpu.roll(x, x.shape[1] // 2, 1)


def across(lhs, rhs):
    return lax.dot_general(lhs, rhs, (((1,), (1,)), ((), ())), preferred_element_type=F32)


def load_cotangent(cot, cots):
    col_count = cots.shape[0] - 1
    for c in range(0, col_count, 2):
        width = cots.shape[2]
        cots[c], cots[c + 1] = twice(cot[:, c * width // 2:(c + 2) * width // 2])
    cots[col_count] = jnp.zeros_like(cots[col_count])


def slots_kernel(first, n_parts, n_tensor, *refs):
    gathered, refs = refs[:n_parts], refs[n_parts:]
    if first:
        cot, (*outs, cots), (ids_vmem, ids, prod, blocks, sem) = refs[0], refs[1:n_tensor + 2], refs[n_tensor + 2:]
        before = []
    else:
        cots, before, outs = refs[0], refs[1:n_tensor + 1], refs[n_tensor + 1:2 * n_tensor + 1]
        ids_vmem, ids, prod, blocks, sem = refs[2 * n_tensor + 1:]
    pairs, side = gathered[0].shape[1:3]
    rows = cots.shape[1]
    share = rows // n_tensor
    copy = load_ids(gathered, ids_vmem, ids, sem)
    if first:
        load_cotangent(cot, cots)
    low = low_half((rows, 2 * side))
    where = [(part, d) for part in gathered for d in range(part.shape[0])]
    tiles = slot_tiles(len(where), pairs)[-prod.shape[0]:]
    for t, ((i, j), (m, l)) in enumerate(tiles):
        part, d = where[i]
        other, e = where[m]
        blocks[t] = diagonal(part[d, j]) if i == m else diagonal(part[d, j], other[e, l])
    copy.wait()
    for t, ((i, j), (m, l)) in enumerate(tiles):
        lhs = jnp.where(low, cots[ids[1, i, side + j]], cots[ids[1, m, side + l]])
        prod[t] = across(lhs, blocks[t])
    me = lax.axis_index("tensor")
    begin = 0
    if not first:
        begin = before[0].shape[0]
        heads = jnp.concatenate([ids_vmem[0].astype(F32)] * 2, axis=0).astype(BF16)
        for k in range(n_tensor):
            outs[k][:begin, :] = before[k][...]
            outs[k][begin + len(tiles) * share:, :] = heads
    for k in range(n_tensor):
        start = pl.multiple_of(lax.rem(me + k, n_tensor) * share, share)
        for t in range(0, len(tiles), 2):
            two = [prod[t, pl.ds(start, share), :], prod[t + 1, pl.ds(start, share), :]]
            here = slice(begin + t * share, begin + (t + 2) * share)
            outs[k][here, :] = jnp.concatenate(two, axis=0).astype(BF16)


def slot_tiles(n, pairs):
    tiles = []
    for i in range(0, n, 4):
        tiles += [((m, j), (m, j + pairs)) for m in range(i, i + 4) for j in range(pairs - 1)]
        tiles += [((m, pairs - 1), (m + 1, pairs - 1)) for m in range(i, i + 4, 2)]
    return tiles


def rows_kernel(count, n_parts, n_tensor, *refs):
    gathered, cot, outs = refs[:n_parts], refs[n_parts], refs[n_parts + 1:n_parts + 1 + n_tensor]
    ids_vmem, ids, cots, acc, sem = refs[n_parts + 1 + n_tensor:]
    pairs, side = gathered[0].shape[1:3]
    row_count = acc.shape[0] - 1
    rows = cot.shape[0]
    copy = load_ids(gathered, ids_vmem, ids, sem)
    acc[...] = jnp.zeros_like(acc)
    load_cotangent(cot, cots)
    low = low_half((rows, 2 * side))
    copy.wait()

    def add(part, d, i):
        for k in range(pairs):
            left, right = ids[1, i, side + k], ids[1, i, side + k + pairs]
            lhs = cots[left]
            if k + pairs >= count:
                prod = across(lhs[:, :side], part[d, k][:, :side])
                acc[ids[0, i, side + k], :, :side] += prod
            else:
                prod = across(jnp.where(low, lhs, cots[right]), diagonal(part[d, k]))
                acc[ids[0, i, side + k]] += jnp.where(low, prod, 0.0)
                acc[ids[0, i, side + k + pairs]] += jnp.where(low, 0.0, prod)

    over(gathered, add)
    me = lax.axis_index("tensor")
    share = rows // n_tensor
    for k in range(n_tensor):
        start = pl.multiple_of(lax.rem(me + k, n_tensor) * share, share)
        half = low_half((share, 2 * side))
        for r in range(0, row_count, 2):
            pair = [fold(acc[r + u, pl.ds(start, share), :]) for u in range(2)]
            outs[k][:, r * side:(r + 2) * side] = jnp.where(half, *pair).astype(BF16)


def load_tokens(token_parts, blocks):
    tokens = [part.at[i] for part in token_parts for i in range(part.shape[0])]
    row_count, width = blocks.shape[0] - 1, blocks.shape[2]
    for r in range(0, row_count, 2):
        parts = [value[:, r * width // 2:(r + 2) * width // 2].astype(F32) for value in tokens]
        blocks[r], blocks[r + 1] = twice(jnp.concatenate(parts, axis=0).astype(BF16))
    blocks[row_count] = jnp.zeros_like(blocks[row_count])


def multiply_tokens(count, gathered, ids, blocks, prod):
    pairs, side = gathered[0].shape[1:3]
    low = low_half(blocks.shape[1:])

    def multiply(part, d, i):
        for k in range(pairs):
            lhs = blocks[ids[0, i, side + k]]
            if k + pairs < count:
                lhs = jnp.where(low, lhs, blocks[ids[0, i, side + k + pairs]])
                tile = diagonal(part[d, k])
            else:
                lhs, tile = lhs[:, :side], part[d, k]
            prod[i * pairs + k] = jnp.dot(lhs, tile, preferred_element_type=F32)

    over(gathered, multiply)


def add_tokens(count, gathered, ids, prod, left_acc, right_acc):
    pairs, side = gathered[0].shape[1:3]

    def add(part, d, i):
        for k in range(pairs):
            value, left = prod[i * pairs + k], ids[1, i, side + k]
            left_sum = left_acc[left] + value
            if k + pairs < count:
                right = ids[1, i, side + k + pairs]
                right_sum = right_acc[right] + value
                right_acc[right] = right_sum
            left_acc[left] = left_sum

    over(gathered, add)


def place_outputs(n_tensor, left_acc, right_acc, stage):
    col_count, rows, width = left_acc.shape[0] - 1, left_acc.shape[1], left_acc.shape[2]
    share = rows // n_tensor
    me = lax.axis_index("tensor")
    half = low_half((share, width))
    for i, k in enumerate(peer_order(n_tensor)):
        start = pl.multiple_of(lax.bitwise_xor(me, k) * share, share)
        mine = slice(i * share, (i + 1) * share)
        for c in range(0, col_count, 2):
            sums = [fold(jnp.where(half, left_acc[c + u, mine, :], right_acc[c + u, mine, :])) for u in range(2)]
            stage[pl.ds(start, share), c * width // 2:(c + 2) * width // 2] = jnp.where(half, *sums)


def forward_kernel(count, n_parts, n_token_parts, n_tensor, *refs):
    gathered, token_parts = refs[:n_parts], refs[n_parts:n_parts + n_token_parts]
    out, ids_vmem, ids, blocks, prod, left_acc, right_acc, stage, sem = refs[n_parts + n_token_parts:]
    copy = load_ids(gathered, ids_vmem, ids, sem)
    left_acc[...] = jnp.zeros_like(left_acc)
    right_acc[...] = jnp.zeros_like(right_acc)
    load_tokens(token_parts, blocks)
    copy.wait()
    multiply_tokens(count, gathered, ids, blocks, prod)
    add_tokens(count, gathered, ids, prod, left_acc, right_acc)
    place_outputs(n_tensor, left_acc, right_acc, stage)
    out[...] = stage[...].astype(BF16)


def sum_kernel(sizes, pairs, *refs):
    groups = []
    for size in sizes:
        groups, refs = groups + [refs[:size]], refs[size:]
    n_tensor = len(groups)
    (grad, ids_vmem, ids, grad_vmem, id_sem, grad_sems), accs = refs[:6], refs[6:]
    n_dp = ids.shape[1]
    share, width = grad.shape
    side = groups[0][0].shape[1] // 2
    tiles = slot_tiles(n_dp, pairs)

    def load(group, start, stop):
        value = group[0][start:stop, :].astype(F32)
        for message in group[1:]:
            value = value + message[start:stop, :].astype(F32)
        return value

    for m, group in enumerate(groups):
        ids_vmem[m] = load(group, len(tiles) * share, groups[0][0].shape[0])[:n_dp].astype(I32)
    copy = pltpu.make_async_copy(ids_vmem, ids, id_sem)
    copy.start()
    for acc in accs:
        acc[...] = jnp.zeros_like(acc)
    low = low_half((share, 2 * side))
    copy.wait()
    for t in range(0, len(tiles), 2):
        both = [load(group, t * share, (t + 2) * share) for group in groups]
        for u in range(2):
            values = [two[u * share:(u + 1) * share] for two in both]
            for h, (i, j) in enumerate(tiles[t + u]):
                rows = [ids[m, i, side + j] for m in range(n_tensor)]
                halves = [jnp.where(low, 0.0, value) if h else jnp.where(low, value, 0.0) for value in values]
                sums = [acc[row] + half for acc, row, half in zip(accs, rows, halves)]
                for acc, row, value in zip(accs, rows, sums):
                    acc[row] = value

    def total(r):
        value = accs[0][r]
        for acc in accs[1:]:
            value = value + acc[r]
        return fold(value)

    copies = []
    chunk = width // grad_sems.shape[0]
    for c in range(grad_sems.shape[0]):
        for r in range(c * chunk // side, (c + 1) * chunk // side, 2):
            grad_vmem[:, r * side:(r + 2) * side] = jnp.where(low, total(r), total(r + 1)).astype(BF16)
        here = slice(c * chunk, (c + 1) * chunk)
        copies.append(pltpu.make_async_copy(grad_vmem.at[:, here], grad.at[:, here], grad_sems.at[c]))
        copies[-1].start()
    for copy in copies:
        copy.wait()


def steps(n):
    return [n >> i for i in range(1, n.bit_length())]


def peer_order(n):
    order = [0]
    for k in steps(n):
        order = order + [i ^ k for i in order]
    return order


def swap(value, axis, n, k):
    return lax.ppermute(value, axis, [(i, i ^ k) for i in range(n)])


def shift(value, axis, n, k):
    return lax.ppermute(value, axis, [(i, (i + k) % n) for i in range(n)])


def gather_all(packed, inputs, n_dp, n_tensor):
    if (n_dp, n_tensor) != (8, 4):
        tokens = [inputs[None]]
        for k in steps(n_tensor):
            tokens = tokens + [swap(value, "tensor", n_tensor, k) for value in tokens]
        return [lax.all_gather(packed, "dp", axis=0, tiled=True)], tokens
    far_tokens = swap(inputs, "tensor", n_tensor, 2)
    near, second, last = [swap(packed, "dp", n_dp, k) for k in (2, 4, 6)]
    joined, tokens = pl.pallas_call(
        join_kernel,
        out_shape=[
            pltpu.VMEM((2, *packed.shape[1:]), packed.dtype),
            pltpu.VMEM((2, *inputs.shape), inputs.dtype),
        ],
        in_specs=[VMEM] * 4,
        out_specs=[VMEM] * 2,
        compiler_params=pltpu.CompilerParams(vmem_limit_bytes=4 * MIB),
    )(packed, near, inputs, far_tokens)
    same_core = [joined, second, last]
    parts = same_core + [swap(part, "dp", n_dp, 1) for part in same_core]
    return parts, [tokens, swap(tokens, "tensor", n_tensor, 1)]


def on_device(n_dp, n_tensor, inputs, block_values, block_slot, grad_out):
    share, width = inputs.shape
    rows, hidden = grad_out.shape
    _, count, side, _ = block_values.shape
    row_count, col_count = width // side, hidden // side
    pairs = count // 2 + 1
    small = (n_dp, n_tensor) == (8, 4)
    per_slot = small and n_dp * count < row_count and count == 2 * pairs - 1
    params = pltpu.CompilerParams(vmem_limit_bytes=(12 if small else 48) * MIB)

    packed = pl.pallas_call(
        functools.partial(pack_kernel, count, row_count, col_count),
        out_shape=pltpu.VMEM((1, pairs, side, 2 * side), BF16),
        in_specs=[HBM, HBM],
        out_specs=VMEM,
        scratch_shapes=[
            pltpu.SMEM(block_slot.shape, I32),
            pltpu.VMEM(block_values.shape, BF16),
            pltpu.SemaphoreType.DMA((2,)),
        ],
        compiler_params=pltpu.CompilerParams(vmem_limit_bytes=4 * MIB),
    )(
        pltpu.with_memory_space_constraint(block_slot, pltpu.HBM),
        pltpu.with_memory_space_constraint(block_values, pltpu.HBM),
    )
    gathered, tokens = gather_all(packed, inputs, n_dp, n_tensor)
    n_parts = len(gathered)
    ids = [pltpu.VMEM((2, n_dp, 2 * side), I32), pltpu.SMEM((2, n_dp, 2 * side), I32)]
    cots = (col_count + 1, rows, 2 * side)
    if per_slot:
        half, tiles = n_parts // 2, len(slot_tiles(n_dp, pairs)) // 2
        scratch = [
            pltpu.VMEM((tiles, rows, 2 * side), F32),
            pltpu.VMEM((tiles, 2 * side, 2 * side), BF16),
            pltpu.SemaphoreType.DMA,
        ]
        *first_slots, cotangent = pl.pallas_call(
            functools.partial(slots_kernel, True, half, n_tensor),
            out_shape=[pltpu.VMEM((tiles * share, 2 * side), BF16)] * n_tensor + [pltpu.VMEM(cots, BF16)],
            in_specs=[VMEM] * (half + 1),
            out_specs=[VMEM] * (n_tensor + 1),
            scratch_shapes=[
                pltpu.VMEM((2, n_dp // 2, 2 * side), I32),
                pltpu.SMEM((2, n_dp // 2, 2 * side), I32),
            ] + scratch,
            compiler_params=params,
        )(*gathered[:half], grad_out)
        partial_sums = pl.pallas_call(
            functools.partial(slots_kernel, False, n_parts, n_tensor),
            out_shape=[pltpu.VMEM((2 * tiles * share + 2 * n_dp, 2 * side), BF16)] * n_tensor,
            in_specs=[VMEM] * (n_parts + 1 + n_tensor),
            out_specs=[VMEM] * n_tensor,
            scratch_shapes=ids + scratch,
            compiler_params=params,
        )(*gathered, cotangent, *first_slots)
        groups = [[partial_sums[0]]] + [[shift(partial_sums[k], "tensor", n_tensor, k)] for k in (2, 1, 3)]
    else:
        partial_sums = pl.pallas_call(
            functools.partial(rows_kernel, count, n_parts, n_tensor),
            out_shape=[jax.ShapeDtypeStruct((share, width), BF16)] * n_tensor,
            in_specs=[VMEM] * (n_parts + 1),
            out_specs=[VMEM] * n_tensor,
            scratch_shapes=ids + [
                pltpu.VMEM(cots, BF16),
                pltpu.VMEM((row_count + 1, rows, 2 * side), F32),
                pltpu.SemaphoreType.DMA,
            ],
            compiler_params=params,
        )(*gathered, grad_out)
        arrived = [partial_sums[0]] + [shift(partial_sums[k], "tensor", n_tensor, k) for k in range(1, n_tensor)]
    outputs = pl.pallas_call(
        functools.partial(forward_kernel, count, n_parts, len(tokens), n_tensor),
        out_shape=jax.ShapeDtypeStruct((rows, hidden), BF16),
        in_specs=[VMEM] * (n_parts + len(tokens)),
        out_specs=VMEM,
        scratch_shapes=ids + [
            pltpu.VMEM((row_count + 1, rows, 2 * side), BF16),
            pltpu.VMEM((n_dp * pairs, rows, 2 * side), F32),
            pltpu.VMEM((col_count + 1, rows, 2 * side), F32),
            pltpu.VMEM((col_count + 1, rows, 2 * side), F32),
            pltpu.VMEM((rows, hidden), F32),
            pltpu.SemaphoreType.DMA,
        ],
        compiler_params=params,
    )(*gathered, *tokens)
    if per_slot:
        grad_in = pl.pallas_call(
            functools.partial(sum_kernel, tuple(map(len, groups)), pairs),
            out_shape=jax.ShapeDtypeStruct((share, width), BF16),
            in_specs=[VMEM] * sum(map(len, groups)),
            out_specs=HBM,
            scratch_shapes=[
                pltpu.VMEM((n_tensor, n_dp, 2 * side), I32),
                pltpu.SMEM((n_tensor, n_dp, 2 * side), I32),
                pltpu.VMEM((share, width), BF16),
                pltpu.SemaphoreType.DMA,
                pltpu.SemaphoreType.DMA((4,)),
            ] + [pltpu.VMEM((row_count + 1, share, 2 * side), F32)] * n_tensor,
            compiler_params=params,
        )(*(message for group in groups for message in group))
        return (outputs, grad_in)
    total = arrived[0].astype(F32)
    for value in arrived[1:]:
        total = total + value.astype(F32)
    return (outputs, total.astype(BF16))


def solution(mesh):
    placed = (
        P(("dp", "tensor"), None),
        P("tensor", "dp", None, None),
        P("tensor", "dp"),
        P("dp", "tensor"),
    )
    return jax.shard_map(
        functools.partial(on_device, mesh.shape["dp"], mesh.shape["tensor"]),
        mesh=mesh,
        in_specs=placed,
        out_specs=(P("dp", "tensor"), P(("dp", "tensor"), None)),
        check_vma=False,
    )
```

```python
import functools

import jax
import jax.numpy as jnp
from jax import lax
from jax.experimental import pallas as pl
from jax.experimental.pallas import tpu as pltpu
from jax.sharding import PartitionSpec as P

VMEM = pl.BlockSpec(memory_space=pltpu.VMEM)
HBM = pl.BlockSpec(memory_space=pltpu.HBM)
MIB = 1024 * 1024
BF16, F32, I32 = jnp.bfloat16, jnp.float32, jnp.int32


def pack_kernel(count, row_count, col_count, slots_hbm, values_hbm, packed, slots, values, sems):
    copies = [
        pltpu.make_async_copy(slots_hbm, slots, sems.at[0]),
        pltpu.make_async_copy(values_hbm, values, sems.at[1]),
    ]
    for copy in copies:
        copy.start()
    side = values.shape[2]
    pairs = packed.shape[1]
    copies[0].wait()
    position = jnp.concatenate([slots[...], jnp.full((1, side - count), -1, I32)], axis=1)
    exact = position.astype(F32)
    row = jnp.floor((exact + 0.5) * (1.0 / col_count))
    col = exact - row * col_count
    row = jnp.where(position >= 0, row, float(row_count))
    col = jnp.where(position >= 0, col, float(col_count))
    head = jnp.concatenate([row, col, jnp.zeros((side - 2, side), F32)], axis=0).astype(BF16)
    copies[1].wait()
    for k in range(pairs):
        left = values[0, k]
        right = values[0, k + pairs] if k + pairs < count else head
        packed[0, k] = jnp.concatenate([left, right], axis=1)


def join_kernel(own, near, tokens, far_tokens, joined, joined_tokens):
    joined[0], joined[1] = own[0], near[0]
    joined_tokens[0], joined_tokens[1] = tokens[...], far_tokens[...]


def load_ids(gathered, ids_vmem, ids, sem):
    i = 0
    for part in gathered:
        n, pairs = part.shape[:2]
        for d in range(n):
            head = part[d, pairs - 1, 0:16, :].astype(F32).astype(I32)
            ids_vmem[0, i:i + 1, :] = head[0:1]
            ids_vmem[1, i:i + 1, :] = head[1:2]
            i += 1
    copy = pltpu.make_async_copy(ids_vmem, ids, sem)
    copy.start()
    return copy


def over(gathered, body):
    start = 0
    for part in gathered:
        n = part.shape[0]
        if n <= 8:
            for d in range(n):
                body(part, d, start + d)
        else:
            def step(d, carry, part=part, start=start):
                body(part, d, start + d)
                return carry
            lax.fori_loop(0, n, step, 0)
        start += n


def low_half(shape):
    return lax.broadcasted_iota(I32, shape, 1) < shape[1] // 2


def swap_halves(x):
    half = x.shape[1] // 2
    return jnp.concatenate([x[:, half:], x[:, :half]], axis=1)


def twice(x):
    low, y = low_half(x.shape), swap_halves(x)
    return jnp.where(low, x, y), jnp.where(low, y, x)


def diagonal(tile, other=None):
    low = low_half(tile.shape)
    zero = jnp.zeros_like(tile)
    top = jnp.where(low, tile, zero)
    bottom = jnp.where(low, zero, tile if other is None else swap_halves(other))
    return jnp.concatenate([top, bottom], axis=0)


def fold(x):
    return x + pltpu.roll(x, x.shape[1] // 2, 1)


def across(lhs, rhs):
    return lax.dot_general(lhs, rhs, (((1,), (1,)), ((), ())), preferred_element_type=F32)


def load_cotangent(cot, cots):
    col_count = cots.shape[0] - 1
    for c in range(0, col_count, 2):
        width = cots.shape[2]
        cots[c], cots[c + 1] = twice(cot[:, c * width // 2:(c + 2) * width // 2])
    cots[col_count] = jnp.zeros_like(cots[col_count])


def slots_kernel(first, n_parts, n_tensor, *refs):
    gathered, refs = refs[:n_parts], refs[n_parts:]
    if first:
        cot, (*outs, cots), (prod, blocks) = refs[0], refs[1:n_tensor + 2], refs[n_tensor + 2:]
        before = []
    else:
        cots, before, outs = refs[0], refs[1:n_tensor + 1], refs[n_tensor + 1:2 * n_tensor + 1]
        prod, blocks = refs[2 * n_tensor + 1:]
    pairs, side = gathered[0].shape[1:3]
    rows = cots.shape[1]
    share = rows // n_tensor
    if first:
        load_cotangent(cot, cots)
    low = low_half((rows, 2 * side))
    where = [(part, d) for part in gathered for d in range(part.shape[0])]
    heads = [part[d, pairs - 1, 0:16, :].astype(F32) for part, d in where]
    columns = [head.astype(I32) for head in heads]
    tiles = slot_tiles(len(where), pairs)[-prod.shape[0]:]
    for t, ((i, j), (m, l)) in enumerate(tiles):
        part, d = where[i]
        other, e = where[m]
        blocks[t] = diagonal(part[d, j]) if i == m else diagonal(part[d, j], other[e, l])
    for t, ((i, j), (m, l)) in enumerate(tiles):
        lhs = jnp.where(low, cots[columns[i][1, side + j]], cots[columns[m][1, side + l]])
        prod[t] = across(lhs, blocks[t])
    me = lax.axis_index("tensor")
    begin = 0
    if not first:
        begin = before[0].shape[0]
        rows_of_slots = jnp.concatenate([head[0:1] for head in heads] * 2, axis=0).astype(BF16)
        for k in range(n_tensor):
            outs[k][:begin, :] = before[k][...]
            outs[k][begin + len(tiles) * share:, :] = rows_of_slots
    for k in range(n_tensor):
        start = pl.multiple_of(lax.rem(me + k, n_tensor) * share, share)
        for t in range(0, len(tiles), 2):
            two = [prod[t, pl.ds(start, share), :], prod[t + 1, pl.ds(start, share), :]]
            here = slice(begin + t * share, begin + (t + 2) * share)
            outs[k][here, :] = jnp.concatenate(two, axis=0).astype(BF16)


def slot_tiles(n, pairs):
    tiles = []
    for i in range(0, n, 4):
        tiles += [((m, j), (m, j + pairs)) for m in range(i, i + 4) for j in range(pairs - 1)]
        tiles += [((m, pairs - 1), (m + 1, pairs - 1)) for m in range(i, i + 4, 2)]
    return tiles


def rows_kernel(count, n_parts, n_tensor, *refs):
    gathered, cot, outs = refs[:n_parts], refs[n_parts], refs[n_parts + 1:n_parts + 1 + n_tensor]
    ids_vmem, ids, cots, acc, sem = refs[n_parts + 1 + n_tensor:]
    pairs, side = gathered[0].shape[1:3]
    row_count = acc.shape[0] - 1
    rows = cot.shape[0]
    copy = load_ids(gathered, ids_vmem, ids, sem)
    acc[...] = jnp.zeros_like(acc)
    load_cotangent(cot, cots)
    low = low_half((rows, 2 * side))
    copy.wait()

    def add(part, d, i):
        for k in range(pairs):
            left, right = ids[1, i, side + k], ids[1, i, side + k + pairs]
            lhs = cots[left]
            if k + pairs >= count:
                prod = across(lhs[:, :side], part[d, k][:, :side])
                acc[ids[0, i, side + k], :, :side] += prod
            else:
                prod = across(jnp.where(low, lhs, cots[right]), diagonal(part[d, k]))
                acc[ids[0, i, side + k]] += jnp.where(low, prod, 0.0)
                acc[ids[0, i, side + k + pairs]] += jnp.where(low, 0.0, prod)

    over(gathered, add)
    me = lax.axis_index("tensor")
    share = rows // n_tensor
    for k in range(n_tensor):
        start = pl.multiple_of(lax.rem(me + k, n_tensor) * share, share)
        half = low_half((share, 2 * side))
        for r in range(0, row_count, 2):
            pair = [fold(acc[r + u, pl.ds(start, share), :]) for u in range(2)]
            outs[k][:, r * side:(r + 2) * side] = jnp.where(half, *pair).astype(BF16)


def load_tokens(token_parts, blocks):
    tokens = [part.at[i] for part in token_parts for i in range(part.shape[0])]
    row_count, width = blocks.shape[0] - 1, blocks.shape[2]
    for r in range(0, row_count, 2):
        parts = [value[:, r * width // 2:(r + 2) * width // 2].astype(F32) for value in tokens]
        blocks[r], blocks[r + 1] = twice(jnp.concatenate(parts, axis=0).astype(BF16))
    blocks[row_count] = jnp.zeros_like(blocks[row_count])


def multiply_tokens(count, gathered, ids, blocks, prod):
    pairs, side = gathered[0].shape[1:3]
    low = low_half(blocks.shape[1:])

    def multiply(part, d, i):
        for k in range(pairs):
            lhs = blocks[ids[0, i, side + k]]
            if k + pairs < count:
                lhs = jnp.where(low, lhs, blocks[ids[0, i, side + k + pairs]])
                tile = diagonal(part[d, k])
            else:
                lhs, tile = lhs[:, :side], part[d, k]
            prod[i * pairs + k] = jnp.dot(lhs, tile, preferred_element_type=F32)

    over(gathered, multiply)


def add_tokens(count, gathered, ids, prod, left_acc, right_acc):
    pairs, side = gathered[0].shape[1:3]

    def add(part, d, i):
        for k in range(pairs):
            value, left = prod[i * pairs + k], ids[1, i, side + k]
            left_sum = left_acc[left] + value
            if k + pairs < count:
                right = ids[1, i, side + k + pairs]
                right_sum = right_acc[right] + value
                right_acc[right] = right_sum
            left_acc[left] = left_sum

    over(gathered, add)


def place_outputs(n_tensor, left_acc, right_acc, stage):
    col_count, rows, width = left_acc.shape[0] - 1, left_acc.shape[1], left_acc.shape[2]
    share = rows // n_tensor
    me = lax.axis_index("tensor")
    half = low_half((share, width))
    for i, k in enumerate(peer_order(n_tensor)):
        start = pl.multiple_of(lax.bitwise_xor(me, k) * share, share)
        mine = slice(i * share, (i + 1) * share)
        for c in range(0, col_count, 2):
            sums = [fold(jnp.where(half, left_acc[c + u, mine, :], right_acc[c + u, mine, :])) for u in range(2)]
            stage[pl.ds(start, share), c * width // 2:(c + 2) * width // 2] = jnp.where(half, *sums)


def forward_kernel(count, n_parts, n_token_parts, n_tensor, *refs):
    gathered, token_parts = refs[:n_parts], refs[n_parts:n_parts + n_token_parts]
    out, ids_vmem, ids, blocks, prod, left_acc, right_acc, stage, sem = refs[n_parts + n_token_parts:]
    copy = load_ids(gathered, ids_vmem, ids, sem)
    left_acc[...] = jnp.zeros_like(left_acc)
    right_acc[...] = jnp.zeros_like(right_acc)
    load_tokens(token_parts, blocks)
    copy.wait()
    multiply_tokens(count, gathered, ids, blocks, prod)
    add_tokens(count, gathered, ids, prod, left_acc, right_acc)
    place_outputs(n_tensor, left_acc, right_acc, stage)
    out[...] = stage[...].astype(BF16)


def sum_kernel(sizes, pairs, n_dp, *refs):
    groups = []
    for size in sizes:
        groups, refs = groups + [refs[:size]], refs[size:]
    n_tensor = len(groups)
    (grad, grad_vmem, grad_sems), accs = refs[:3], refs[3:]
    share, width = grad.shape
    side = groups[0][0].shape[1] // 2
    tiles = slot_tiles(n_dp, pairs)
    end = len(tiles) * share

    def load(group, start, stop):
        value = group[0][start:stop, :].astype(F32)
        for message in group[1:]:
            value = value + message[start:stop, :].astype(F32)
        return value

    places = [load(group, end, end + 2 * n_dp)[:n_dp].astype(I32) for group in groups]
    for acc in accs:
        acc[...] = jnp.zeros_like(acc)
    low = low_half((share, 2 * side))
    for t in range(0, len(tiles), 2):
        both = [load(group, t * share, (t + 2) * share) for group in groups]
        for u in range(2):
            values = [two[u * share:(u + 1) * share] for two in both]
            for h, (i, j) in enumerate(tiles[t + u]):
                rows = [place[i, side + j] for place in places]
                halves = [jnp.where(low, 0.0, value) if h else jnp.where(low, value, 0.0) for value in values]
                sums = [acc[row] + half for acc, row, half in zip(accs, rows, halves)]
                for acc, row, value in zip(accs, rows, sums):
                    acc[row] = value

    def total(r):
        value = accs[0][r]
        for acc in accs[1:]:
            value = value + acc[r]
        return fold(value)

    copies = []
    chunk = width // grad_sems.shape[0]
    for c in range(grad_sems.shape[0]):
        for r in range(c * chunk // side, (c + 1) * chunk // side, 2):
            grad_vmem[:, r * side:(r + 2) * side] = jnp.where(low, total(r), total(r + 1)).astype(BF16)
        here = slice(c * chunk, (c + 1) * chunk)
        copies.append(pltpu.make_async_copy(grad_vmem.at[:, here], grad.at[:, here], grad_sems.at[c]))
        copies[-1].start()
    for copy in copies:
        copy.wait()


def steps(n):
    return [n >> i for i in range(1, n.bit_length())]


def peer_order(n):
    order = [0]
    for k in steps(n):
        order = order + [i ^ k for i in order]
    return order


def swap(value, axis, n, k):
    return lax.ppermute(value, axis, [(i, i ^ k) for i in range(n)])


def shift(value, axis, n, k):
    return lax.ppermute(value, axis, [(i, (i + k) % n) for i in range(n)])


def gather_all(packed, inputs, n_dp, n_tensor):
    if (n_dp, n_tensor) != (8, 4):
        tokens = [inputs[None]]
        for k in steps(n_tensor):
            tokens = tokens + [swap(value, "tensor", n_tensor, k) for value in tokens]
        return [lax.all_gather(packed, "dp", axis=0, tiled=True)], tokens
    far_tokens = swap(inputs, "tensor", n_tensor, 2)
    near, second, last = [swap(packed, "dp", n_dp, k) for k in (2, 4, 6)]
    joined, tokens = pl.pallas_call(
        join_kernel,
        out_shape=[
            pltpu.VMEM((2, *packed.shape[1:]), packed.dtype),
            pltpu.VMEM((2, *inputs.shape), inputs.dtype),
        ],
        in_specs=[VMEM] * 4,
        out_specs=[VMEM] * 2,
        compiler_params=pltpu.CompilerParams(vmem_limit_bytes=4 * MIB),
    )(packed, near, inputs, far_tokens)
    same_core = [joined, second, last]
    parts = same_core + [swap(part, "dp", n_dp, 1) for part in same_core]
    return parts, [tokens, swap(tokens, "tensor", n_tensor, 1)]


def on_device(n_dp, n_tensor, inputs, block_values, block_slot, grad_out):
    share, width = inputs.shape
    rows, hidden = grad_out.shape
    _, count, side, _ = block_values.shape
    row_count, col_count = width // side, hidden // side
    pairs = count // 2 + 1
    small = (n_dp, n_tensor) == (8, 4)
    per_slot = small and n_dp * count < row_count and count == 2 * pairs - 1
    params = pltpu.CompilerParams(vmem_limit_bytes=(12 if small else 48) * MIB)

    packed = pl.pallas_call(
        functools.partial(pack_kernel, count, row_count, col_count),
        out_shape=pltpu.VMEM((1, pairs, side, 2 * side), BF16),
        in_specs=[HBM, HBM],
        out_specs=VMEM,
        scratch_shapes=[
            pltpu.VMEM(block_slot.shape, I32),
            pltpu.VMEM(block_values.shape, BF16),
            pltpu.SemaphoreType.DMA((2,)),
        ],
        compiler_params=pltpu.CompilerParams(vmem_limit_bytes=4 * MIB),
    )(
        pltpu.with_memory_space_constraint(block_slot, pltpu.HBM),
        pltpu.with_memory_space_constraint(block_values, pltpu.HBM),
    )
    gathered, tokens = gather_all(packed, inputs, n_dp, n_tensor)
    n_parts = len(gathered)
    ids = [pltpu.VMEM((2, n_dp, 2 * side), I32), pltpu.SMEM((2, n_dp, 2 * side), I32)]
    cots = (col_count + 1, rows, 2 * side)
    if per_slot:
        half, tiles = n_parts // 2, len(slot_tiles(n_dp, pairs)) // 2
        scratch = [
            pltpu.VMEM((tiles, rows, 2 * side), F32),
            pltpu.VMEM((tiles, 2 * side, 2 * side), BF16),
        ]
        *first_slots, cotangent = pl.pallas_call(
            functools.partial(slots_kernel, True, half, n_tensor),
            out_shape=[pltpu.VMEM((tiles * share, 2 * side), BF16)] * n_tensor + [pltpu.VMEM(cots, BF16)],
            in_specs=[VMEM] * (half + 1),
            out_specs=[VMEM] * (n_tensor + 1),
            scratch_shapes=scratch,
            compiler_params=params,
        )(*gathered[:half], grad_out)
        partial_sums = pl.pallas_call(
            functools.partial(slots_kernel, False, n_parts, n_tensor),
            out_shape=[pltpu.VMEM((2 * tiles * share + 2 * n_dp, 2 * side), BF16)] * n_tensor,
            in_specs=[VMEM] * (n_parts + 1 + n_tensor),
            out_specs=[VMEM] * n_tensor,
            scratch_shapes=scratch,
            compiler_params=params,
        )(*gathered, cotangent, *first_slots)
        groups = [[partial_sums[0]]] + [[shift(partial_sums[k], "tensor", n_tensor, k)] for k in (2, 1, 3)]
    else:
        partial_sums = pl.pallas_call(
            functools.partial(rows_kernel, count, n_parts, n_tensor),
            out_shape=[jax.ShapeDtypeStruct((share, width), BF16)] * n_tensor,
            in_specs=[VMEM] * (n_parts + 1),
            out_specs=[VMEM] * n_tensor,
            scratch_shapes=ids + [
                pltpu.VMEM(cots, BF16),
                pltpu.VMEM((row_count + 1, rows, 2 * side), F32),
                pltpu.SemaphoreType.DMA,
            ],
            compiler_params=params,
        )(*gathered, grad_out)
        arrived = [partial_sums[0]] + [shift(partial_sums[k], "tensor", n_tensor, k) for k in range(1, n_tensor)]
    outputs = pl.pallas_call(
        functools.partial(forward_kernel, count, n_parts, len(tokens), n_tensor),
        out_shape=jax.ShapeDtypeStruct((rows, hidden), BF16),
        in_specs=[VMEM] * (n_parts + len(tokens)),
        out_specs=VMEM,
        scratch_shapes=ids + [
            pltpu.VMEM((row_count + 1, rows, 2 * side), BF16),
            pltpu.VMEM((n_dp * pairs, rows, 2 * side), F32),
            pltpu.VMEM((col_count + 1, rows, 2 * side), F32),
            pltpu.VMEM((col_count + 1, rows, 2 * side), F32),
            pltpu.VMEM((rows, hidden), F32),
            pltpu.SemaphoreType.DMA,
        ],
        compiler_params=params,
    )(*gathered, *tokens)
    if per_slot:
        grad_in = pl.pallas_call(
            functools.partial(sum_kernel, tuple(map(len, groups)), pairs, n_dp),
            out_shape=jax.ShapeDtypeStruct((share, width), BF16),
            in_specs=[VMEM] * sum(map(len, groups)),
            out_specs=HBM,
            scratch_shapes=[
                pltpu.VMEM((share, width), BF16),
                pltpu.SemaphoreType.DMA((4,)),
            ] + [pltpu.VMEM((row_count + 1, share, 2 * side), F32)] * n_tensor,
            compiler_params=params,
        )(*(message for group in groups for message in group))
        return (outputs, grad_in)
    total = arrived[0].astype(F32)
    for value in arrived[1:]:
        total = total + value.astype(F32)
    return (outputs, total.astype(BF16))


def solution(mesh):
    placed = (
        P(("dp", "tensor"), None),
        P("tensor", "dp", None, None),
        P("tensor", "dp"),
        P("dp", "tensor"),
    )
    return jax.shard_map(
        functools.partial(on_device, mesh.shape["dp"], mesh.shape["tensor"]),
        mesh=mesh,
        in_specs=placed,
        out_specs=(P("dp", "tensor"), P(("dp", "tensor"), None)),
        check_vma=False,
    )
```

```python
import functools

import jax
import jax.numpy as jnp
from jax import lax
from jax.experimental import pallas as pl
from jax.experimental.pallas import tpu as pltpu
from jax.sharding import PartitionSpec as P

VMEM = pl.BlockSpec(memory_space=pltpu.VMEM)
HBM = pl.BlockSpec(memory_space=pltpu.HBM)
MIB = 1024 * 1024
BF16, F32, I32 = jnp.bfloat16, jnp.float32, jnp.int32


def pack_kernel(count, row_count, col_count, slots_hbm, values_hbm, packed, slots, values, sems):
    copies = [pltpu.make_async_copy(slots_hbm, slots, sems.at[count])]
    copies += [pltpu.make_async_copy(values_hbm.at[0, j], values.at[0, j], sems.at[j]) for j in range(count)]
    for copy in copies:
        copy.start()
    side = values.shape[2]
    pairs = packed.shape[1]
    copies[0].wait()
    position = jnp.concatenate([slots[...], jnp.full((1, side - count), -1, I32)], axis=1)
    exact = position.astype(F32)
    row = jnp.floor((exact + 0.5) * (1.0 / col_count))
    col = exact - row * col_count
    row = jnp.where(position >= 0, row, float(row_count))
    col = jnp.where(position >= 0, col, float(col_count))
    head = jnp.concatenate([row, col, jnp.zeros((side - 2, side), F32)], axis=0).astype(BF16)
    for copy in copies[1:]:
        copy.wait()
    for k in range(pairs):
        left = values[0, k]
        right = values[0, k + pairs] if k + pairs < count else head
        packed[0, k] = jnp.concatenate([left, right], axis=1)


def join_kernel(own, near, tokens, far_tokens, joined, joined_tokens):
    joined[0], joined[1] = own[0], near[0]
    joined_tokens[0], joined_tokens[1] = tokens[...], far_tokens[...]


def load_ids(gathered, ids_vmem, ids, sem):
    i = 0
    for part in gathered:
        n, pairs = part.shape[:2]
        for d in range(n):
            head = part[d, pairs - 1, 0:16, :].astype(F32).astype(I32)
            ids_vmem[0, i:i + 1, :] = head[0:1]
            ids_vmem[1, i:i + 1, :] = head[1:2]
            i += 1
    copy = pltpu.make_async_copy(ids_vmem, ids, sem)
    copy.start()
    return copy


def over(gathered, body):
    start = 0
    for part in gathered:
        n = part.shape[0]
        if n <= 8:
            for d in range(n):
                body(part, d, start + d)
        else:
            def step(d, carry, part=part, start=start):
                body(part, d, start + d)
                return carry
            lax.fori_loop(0, n, step, 0)
        start += n


def low_half(shape):
    return lax.broadcasted_iota(I32, shape, 1) < shape[1] // 2


def swap_halves(x):
    half = x.shape[1] // 2
    return jnp.concatenate([x[:, half:], x[:, :half]], axis=1)


def twice(x):
    low, y = low_half(x.shape), swap_halves(x)
    return jnp.where(low, x, y), jnp.where(low, y, x)


def diagonal(tile, other=None):
    low = low_half(tile.shape)
    zero = jnp.zeros_like(tile)
    top = jnp.where(low, tile, zero)
    bottom = jnp.where(low, zero, tile if other is None else swap_halves(other))
    return jnp.concatenate([top, bottom], axis=0)


def fold(x):
    return x + pltpu.roll(x, x.shape[1] // 2, 1)


def across(lhs, rhs):
    return lax.dot_general(lhs, rhs, (((1,), (1,)), ((), ())), preferred_element_type=F32)


def load_cotangent(cot, cots):
    col_count = cots.shape[0] - 1
    for c in range(0, col_count, 2):
        width = cots.shape[2]
        cots[c], cots[c + 1] = twice(cot[:, c * width // 2:(c + 2) * width // 2])
    cots[col_count] = jnp.zeros_like(cots[col_count])


def slots_kernel(first, n_parts, n_tensor, *refs):
    gathered, refs = refs[:n_parts], refs[n_parts:]
    if first:
        cot, (*outs, cots), (prod, blocks) = refs[0], refs[1:n_tensor + 2], refs[n_tensor + 2:]
        before = []
    else:
        cots, before, outs = refs[0], refs[1:n_tensor + 1], refs[n_tensor + 1:2 * n_tensor + 1]
        prod, blocks = refs[2 * n_tensor + 1:]
    pairs, side = gathered[0].shape[1:3]
    rows = cots.shape[1]
    share = rows // n_tensor
    if first:
        load_cotangent(cot, cots)
    low = low_half((rows, 2 * side))
    where = [(part, d) for part in gathered for d in range(part.shape[0])]
    heads = [part[d, pairs - 1, 0:16, :].astype(F32) for part, d in where]
    columns = [head.astype(I32) for head in heads]
    tiles = slot_tiles(len(where), pairs)[-prod.shape[0]:]
    for t, ((i, j), (m, l)) in enumerate(tiles):
        part, d = where[i]
        other, e = where[m]
        blocks[t] = diagonal(part[d, j]) if i == m else diagonal(part[d, j], other[e, l])
    for t, ((i, j), (m, l)) in enumerate(tiles):
        lhs = jnp.where(low, cots[columns[i][1, side + j]], cots[columns[m][1, side + l]])
        prod[t] = across(lhs, blocks[t])
    me = lax.axis_index("tensor")
    begin = 0
    if not first:
        begin = before[0].shape[0]
        rows_of_slots = jnp.concatenate([head[0:1] for head in heads] * 2, axis=0).astype(BF16)
        for k in range(n_tensor):
            outs[k][:begin, :] = before[k][...]
            outs[k][begin + len(tiles) * share:, :] = rows_of_slots
    for k in range(n_tensor):
        start = pl.multiple_of(lax.rem(me + k, n_tensor) * share, share)
        for t in range(0, len(tiles), 2):
            two = [prod[t, pl.ds(start, share), :], prod[t + 1, pl.ds(start, share), :]]
            here = slice(begin + t * share, begin + (t + 2) * share)
            outs[k][here, :] = jnp.concatenate(two, axis=0).astype(BF16)


def slot_tiles(n, pairs):
    tiles = []
    for i in range(0, n, 4):
        tiles += [((m, j), (m, j + pairs)) for m in range(i, i + 4) for j in range(pairs - 1)]
        tiles += [((m, pairs - 1), (m + 1, pairs - 1)) for m in range(i, i + 4, 2)]
    return tiles


def rows_kernel(count, n_parts, n_tensor, *refs):
    gathered, cot, outs = refs[:n_parts], refs[n_parts], refs[n_parts + 1:n_parts + 1 + n_tensor]
    ids_vmem, ids, cots, acc, sem = refs[n_parts + 1 + n_tensor:]
    pairs, side = gathered[0].shape[1:3]
    row_count = acc.shape[0] - 1
    rows = cot.shape[0]
    copy = load_ids(gathered, ids_vmem, ids, sem)
    acc[...] = jnp.zeros_like(acc)
    load_cotangent(cot, cots)
    low = low_half((rows, 2 * side))
    copy.wait()

    def add(part, d, i):
        for k in range(pairs):
            left, right = ids[1, i, side + k], ids[1, i, side + k + pairs]
            lhs = cots[left]
            if k + pairs >= count:
                prod = across(lhs[:, :side], part[d, k][:, :side])
                acc[ids[0, i, side + k], :, :side] += prod
            else:
                prod = across(jnp.where(low, lhs, cots[right]), diagonal(part[d, k]))
                acc[ids[0, i, side + k]] += jnp.where(low, prod, 0.0)
                acc[ids[0, i, side + k + pairs]] += jnp.where(low, 0.0, prod)

    over(gathered, add)
    me = lax.axis_index("tensor")
    share = rows // n_tensor
    for k in range(n_tensor):
        start = pl.multiple_of(lax.rem(me + k, n_tensor) * share, share)
        half = low_half((share, 2 * side))
        for r in range(0, row_count, 2):
            pair = [fold(acc[r + u, pl.ds(start, share), :]) for u in range(2)]
            outs[k][:, r * side:(r + 2) * side] = jnp.where(half, *pair).astype(BF16)


def load_tokens(token_parts, blocks):
    tokens = [part.at[i] for part in token_parts for i in range(part.shape[0])]
    row_count, width = blocks.shape[0] - 1, blocks.shape[2]
    for r in range(0, row_count, 2):
        parts = [value[:, r * width // 2:(r + 2) * width // 2].astype(F32) for value in tokens]
        blocks[r], blocks[r + 1] = twice(jnp.concatenate(parts, axis=0).astype(BF16))
    blocks[row_count] = jnp.zeros_like(blocks[row_count])


def multiply_tokens(count, gathered, ids, blocks, prod):
    pairs, side = gathered[0].shape[1:3]
    low = low_half(blocks.shape[1:])

    def multiply(part, d, i):
        for k in range(pairs):
            lhs = blocks[ids(0, i, side + k)]
            if k + pairs < count:
                lhs = jnp.where(low, lhs, blocks[ids(0, i, side + k + pairs)])
                tile = diagonal(part[d, k])
            else:
                lhs, tile = lhs[:, :side], part[d, k]
            prod[i * pairs + k] = jnp.dot(lhs, tile, preferred_element_type=F32)

    over(gathered, multiply)


def add_tokens(count, gathered, ids, prod, left_acc, right_acc):
    pairs, side = gathered[0].shape[1:3]

    def add(part, d, i):
        for k in range(pairs):
            value, left = prod[i * pairs + k], ids(1, i, side + k)
            left_sum = left_acc[left] + value
            if k + pairs < count:
                right = ids(1, i, side + k + pairs)
                right_sum = right_acc[right] + value
                right_acc[right] = right_sum
            left_acc[left] = left_sum

    over(gathered, add)


def place_outputs(n_tensor, left_acc, right_acc, stage):
    col_count, rows, width = left_acc.shape[0] - 1, left_acc.shape[1], left_acc.shape[2]
    share = rows // n_tensor
    me = lax.axis_index("tensor")
    half = low_half((share, width))
    for i, k in enumerate(peer_order(n_tensor)):
        start = pl.multiple_of(lax.bitwise_xor(me, k) * share, share)
        mine = slice(i * share, (i + 1) * share)
        for c in range(0, col_count, 2):
            sums = [fold(jnp.where(half, left_acc[c + u, mine, :], right_acc[c + u, mine, :])) for u in range(2)]
            stage[pl.ds(start, share), c * width // 2:(c + 2) * width // 2] = jnp.where(half, *sums)


def forward_kernel(count, few, n_parts, n_token_parts, n_tensor, *refs):
    gathered, token_parts = refs[:n_parts], refs[n_parts:n_parts + n_token_parts]
    out, blocks, prod, left_acc, right_acc, stage = refs[n_parts + n_token_parts:][:6]
    if few:
        heads = [part[d, part.shape[1] - 1, 0:16, :].astype(F32) for part in gathered for d in range(part.shape[0])]
        heads = [head.astype(I32) for head in heads]
        ids = lambda line, i, lane: heads[i][line, lane]
    else:
        ids_vmem, scalars, sem = refs[-3:]
        copy = load_ids(gathered, ids_vmem, scalars, sem)
        ids = lambda line, i, lane: scalars[line, i, lane]
    left_acc[...] = jnp.zeros_like(left_acc)
    right_acc[...] = jnp.zeros_like(right_acc)
    load_tokens(token_parts, blocks)
    if not few:
        copy.wait()
    multiply_tokens(count, gathered, ids, blocks, prod)
    add_tokens(count, gathered, ids, prod, left_acc, right_acc)
    place_outputs(n_tensor, left_acc, right_acc, stage)
    out[...] = stage[...].astype(BF16)


def sum_kernel(sizes, pairs, n_dp, *refs):
    groups = []
    for size in sizes:
        groups, refs = groups + [refs[:size]], refs[size:]
    n_tensor = len(groups)
    (grad, grad_vmem, grad_sems), accs = refs[:3], refs[3:]
    share, width = grad.shape
    side = groups[0][0].shape[1] // 2
    tiles = slot_tiles(n_dp, pairs)
    end = len(tiles) * share

    def load(group, start, stop):
        value = group[0][start:stop, :].astype(F32)
        for message in group[1:]:
            value = value + message[start:stop, :].astype(F32)
        return value

    places = [load(group, end, end + 2 * n_dp)[:n_dp].astype(I32) for group in groups]
    for acc in accs:
        acc[...] = jnp.zeros_like(acc)
    low = low_half((share, 2 * side))
    for t in range(0, len(tiles), 2):
        both = [load(group, t * share, (t + 2) * share) for group in groups]
        for u in range(2):
            values = [two[u * share:(u + 1) * share] for two in both]
            for h, (i, j) in enumerate(tiles[t + u]):
                rows = [place[i, side + j] for place in places]
                halves = [jnp.where(low, 0.0, value) if h else jnp.where(low, value, 0.0) for value in values]
                sums = [acc[row] + half for acc, row, half in zip(accs, rows, halves)]
                for acc, row, value in zip(accs, rows, sums):
                    acc[row] = value

    def total(r):
        value = accs[0][r]
        for acc in accs[1:]:
            value = value + acc[r]
        return fold(value)

    copies = []
    chunk = width // grad_sems.shape[0]
    for c in range(grad_sems.shape[0]):
        for r in range(c * chunk // side, (c + 1) * chunk // side, 2):
            grad_vmem[:, r * side:(r + 2) * side] = jnp.where(low, total(r), total(r + 1)).astype(BF16)
        here = slice(c * chunk, (c + 1) * chunk)
        copies.append(pltpu.make_async_copy(grad_vmem.at[:, here], grad.at[:, here], grad_sems.at[c]))
        copies[-1].start()
    for copy in copies:
        copy.wait()


def steps(n):
    return [n >> i for i in range(1, n.bit_length())]


def peer_order(n):
    order = [0]
    for k in steps(n):
        order = order + [i ^ k for i in order]
    return order


def swap(value, axis, n, k):
    return lax.ppermute(value, axis, [(i, i ^ k) for i in range(n)])


def shift(value, axis, n, k):
    return lax.ppermute(value, axis, [(i, (i + k) % n) for i in range(n)])


def gather_all(packed, inputs, n_dp, n_tensor):
    if (n_dp, n_tensor) != (8, 4):
        tokens = [inputs[None]]
        for k in steps(n_tensor):
            tokens = tokens + [swap(value, "tensor", n_tensor, k) for value in tokens]
        return [lax.all_gather(packed, "dp", axis=0, tiled=True)], tokens
    far_tokens = swap(inputs, "tensor", n_tensor, 2)
    near, second, last = [swap(packed, "dp", n_dp, k) for k in (6, 2, 4)]
    joined, tokens = pl.pallas_call(
        join_kernel,
        out_shape=[
            pltpu.VMEM((2, *packed.shape[1:]), packed.dtype),
            pltpu.VMEM((2, *inputs.shape), inputs.dtype),
        ],
        in_specs=[VMEM] * 4,
        out_specs=[VMEM] * 2,
        compiler_params=pltpu.CompilerParams(vmem_limit_bytes=4 * MIB),
    )(packed, near, inputs, far_tokens)
    same_core = [joined, second, last]
    parts = same_core + [swap(part, "dp", n_dp, 1) for part in same_core]
    return parts, [tokens, swap(tokens, "tensor", n_tensor, 1)]


def on_device(n_dp, n_tensor, inputs, block_values, block_slot, grad_out):
    share, width = inputs.shape
    rows, hidden = grad_out.shape
    _, count, side, _ = block_values.shape
    row_count, col_count = width // side, hidden // side
    pairs = count // 2 + 1
    small = (n_dp, n_tensor) == (8, 4)
    per_slot = small and n_dp * count < row_count and count == 2 * pairs - 1
    params = pltpu.CompilerParams(vmem_limit_bytes=(12 if small else 48) * MIB)

    packed = pl.pallas_call(
        functools.partial(pack_kernel, count, row_count, col_count),
        out_shape=pltpu.VMEM((1, pairs, side, 2 * side), BF16),
        in_specs=[HBM, HBM],
        out_specs=VMEM,
        scratch_shapes=[
            pltpu.VMEM(block_slot.shape, I32),
            pltpu.VMEM(block_values.shape, BF16),
            pltpu.SemaphoreType.DMA((count + 1,)),
        ],
        compiler_params=pltpu.CompilerParams(vmem_limit_bytes=4 * MIB),
    )(
        pltpu.with_memory_space_constraint(block_slot, pltpu.HBM),
        pltpu.with_memory_space_constraint(block_values, pltpu.HBM),
    )
    gathered, tokens = gather_all(packed, inputs, n_dp, n_tensor)
    n_parts = len(gathered)
    ids = [pltpu.VMEM((2, n_dp, 2 * side), I32), pltpu.SMEM((2, n_dp, 2 * side), I32)]
    cots = (col_count + 1, rows, 2 * side)
    if per_slot:
        half, tiles = n_parts // 2, len(slot_tiles(n_dp, pairs)) // 2
        scratch = [
            pltpu.VMEM((tiles, rows, 2 * side), F32),
            pltpu.VMEM((tiles, 2 * side, 2 * side), BF16),
        ]
        *first_slots, cotangent = pl.pallas_call(
            functools.partial(slots_kernel, True, half, n_tensor),
            out_shape=[pltpu.VMEM((tiles * share, 2 * side), BF16)] * n_tensor + [pltpu.VMEM(cots, BF16)],
            in_specs=[VMEM] * (half + 1),
            out_specs=[VMEM] * (n_tensor + 1),
            scratch_shapes=scratch,
            compiler_params=params,
        )(*gathered[:half], grad_out)
        partial_sums = pl.pallas_call(
            functools.partial(slots_kernel, False, n_parts, n_tensor),
            out_shape=[pltpu.VMEM((2 * tiles * share + 2 * n_dp, 2 * side), BF16)] * n_tensor,
            in_specs=[VMEM] * (n_parts + 1 + n_tensor),
            out_specs=[VMEM] * n_tensor,
            scratch_shapes=scratch,
            compiler_params=params,
        )(*gathered, cotangent, *first_slots)
        groups = [[partial_sums[0]]] + [[shift(partial_sums[k], "tensor", n_tensor, k)] for k in (2, 1, 3)]
    else:
        partial_sums = pl.pallas_call(
            functools.partial(rows_kernel, count, n_parts, n_tensor),
            out_shape=[jax.ShapeDtypeStruct((share, width), BF16)] * n_tensor,
            in_specs=[VMEM] * (n_parts + 1),
            out_specs=[VMEM] * n_tensor,
            scratch_shapes=ids + [
                pltpu.VMEM(cots, BF16),
                pltpu.VMEM((row_count + 1, rows, 2 * side), F32),
                pltpu.SemaphoreType.DMA,
            ],
            compiler_params=params,
        )(*gathered, grad_out)
        arrived = [partial_sums[0]] + [shift(partial_sums[k], "tensor", n_tensor, k) for k in range(1, n_tensor)]
    outputs = pl.pallas_call(
        functools.partial(forward_kernel, count, per_slot, n_parts, len(tokens), n_tensor),
        out_shape=jax.ShapeDtypeStruct((rows, hidden), BF16),
        in_specs=[VMEM] * (n_parts + len(tokens)),
        out_specs=VMEM,
        scratch_shapes=[
            pltpu.VMEM((row_count + 1, rows, 2 * side), BF16),
            pltpu.VMEM((n_dp * pairs, rows, 2 * side), F32),
            pltpu.VMEM((col_count + 1, rows, 2 * side), F32),
            pltpu.VMEM((col_count + 1, rows, 2 * side), F32),
            pltpu.VMEM((rows, hidden), F32),
        ] + ([] if per_slot else ids + [pltpu.SemaphoreType.DMA]),
        compiler_params=params,
    )(*gathered, *tokens)
    if per_slot:
        grad_in = pl.pallas_call(
            functools.partial(sum_kernel, tuple(map(len, groups)), pairs, n_dp),
            out_shape=jax.ShapeDtypeStruct((share, width), BF16),
            in_specs=[VMEM] * sum(map(len, groups)),
            out_specs=HBM,
            scratch_shapes=[
                pltpu.VMEM((share, width), BF16),
                pltpu.SemaphoreType.DMA((4,)),
            ] + [pltpu.VMEM((row_count + 1, share, 2 * side), F32)] * n_tensor,
            compiler_params=params,
        )(*(message for group in groups for message in group))
        return (outputs, grad_in)
    total = arrived[0].astype(F32)
    for value in arrived[1:]:
        total = total + value.astype(F32)
    return (outputs, total.astype(BF16))


def solution(mesh):
    placed = (
        P(("dp", "tensor"), None),
        P("tensor", "dp", None, None),
        P("tensor", "dp"),
        P("dp", "tensor"),
    )
    return jax.shard_map(
        functools.partial(on_device, mesh.shape["dp"], mesh.shape["tensor"]),
        mesh=mesh,
        in_specs=placed,
        out_specs=(P("dp", "tensor"), P(("dp", "tensor"), None)),
        check_vma=False,
    )
```

```python
import functools

import jax
import jax.numpy as jnp
from jax import lax
from jax.experimental import pallas as pl
from jax.experimental.pallas import tpu as pltpu
from jax.sharding import PartitionSpec as P

VMEM = pl.BlockSpec(memory_space=pltpu.VMEM)
HBM = pl.BlockSpec(memory_space=pltpu.HBM)
MIB = 1024 * 1024
BF16, F32, I32 = jnp.bfloat16, jnp.float32, jnp.int32


def pack_kernel(count, row_count, col_count, slots_hbm, values_hbm, packed, slots, values, sems):
    copies = [pltpu.make_async_copy(slots_hbm, slots, sems.at[count])]
    copies += [pltpu.make_async_copy(values_hbm.at[0, j], values.at[0, j], sems.at[j]) for j in range(count)]
    for copy in copies:
        copy.start()
    side = values.shape[2]
    pairs = packed.shape[1]
    copies[0].wait()
    position = jnp.concatenate([slots[...], jnp.full((1, side - count), -1, I32)], axis=1)
    exact = position.astype(F32)
    row = jnp.floor((exact + 0.5) * (1.0 / col_count))
    col = exact - row * col_count
    row = jnp.where(position >= 0, row, float(row_count))
    col = jnp.where(position >= 0, col, float(col_count))
    head = jnp.concatenate([row, col, jnp.zeros((side - 2, side), F32)], axis=0).astype(BF16)
    for copy in copies[1:]:
        copy.wait()
    for k in range(pairs):
        left = values[0, k]
        right = values[0, k + pairs] if k + pairs < count else head
        packed[0, k] = jnp.concatenate([left, right], axis=1)


def join_kernel(own, near, tokens, far_tokens, joined, joined_tokens):
    joined[0], joined[1] = own[0], near[0]
    joined_tokens[0], joined_tokens[1] = tokens[...], far_tokens[...]


def load_ids(gathered, ids_vmem, ids, sem):
    i = 0
    for part in gathered:
        n, pairs = part.shape[:2]
        for d in range(n):
            head = part[d, pairs - 1, 0:16, :].astype(F32).astype(I32)
            ids_vmem[0, i:i + 1, :] = head[0:1]
            ids_vmem[1, i:i + 1, :] = head[1:2]
            i += 1
    copy = pltpu.make_async_copy(ids_vmem, ids, sem)
    copy.start()
    return copy


def over(gathered, body):
    start = 0
    for part in gathered:
        n = part.shape[0]
        if n <= 8:
            for d in range(n):
                body(part, d, start + d)
        else:
            def step(d, carry, part=part, start=start):
                body(part, d, start + d)
                return carry
            lax.fori_loop(0, n, step, 0)
        start += n


def low_half(shape):
    return lax.broadcasted_iota(I32, shape, 1) < shape[1] // 2


def swap_halves(x):
    half = x.shape[1] // 2
    return jnp.concatenate([x[:, half:], x[:, :half]], axis=1)


def twice(x):
    low, y = low_half(x.shape), swap_halves(x)
    return jnp.where(low, x, y), jnp.where(low, y, x)


def diagonal(tile, other=None):
    low = low_half(tile.shape)
    zero = jnp.zeros_like(tile)
    top = jnp.where(low, tile, zero)
    bottom = jnp.where(low, zero, tile if other is None else swap_halves(other))
    return jnp.concatenate([top, bottom], axis=0)


def fold(x):
    return x + pltpu.roll(x, x.shape[1] // 2, 1)


def across(lhs, rhs):
    return lax.dot_general(lhs, rhs, (((1,), (1,)), ((), ())), preferred_element_type=F32)


def load_cotangent(cot, cots):
    col_count = cots.shape[0] - 1
    for c in range(0, col_count, 2):
        width = cots.shape[2]
        cots[c], cots[c + 1] = twice(cot[:, c * width // 2:(c + 2) * width // 2])
    cots[col_count] = jnp.zeros_like(cots[col_count])


def slots_kernel(first, n_parts, n_tensor, *refs):
    gathered, refs = refs[:n_parts], refs[n_parts:]
    if first:
        cot, (*outs, cots), (prod, blocks) = refs[0], refs[1:n_tensor + 2], refs[n_tensor + 2:]
        before = []
    else:
        cots, before, outs = refs[0], refs[1:n_tensor + 1], refs[n_tensor + 1:2 * n_tensor + 1]
        prod, blocks = refs[2 * n_tensor + 1:]
    pairs, side = gathered[0].shape[1:3]
    rows = cots.shape[1]
    share = rows // n_tensor
    if first:
        load_cotangent(cot, cots)
    low = low_half((rows, 2 * side))
    where = [(part, d) for part in gathered for d in range(part.shape[0])]
    heads = [part[d, pairs - 1, 0:16, :].astype(F32) for part, d in where]
    columns = [head.astype(I32) for head in heads]
    tiles = slot_tiles(len(where), pairs)[-prod.shape[0]:]
    for t, ((i, j), (m, l)) in enumerate(tiles):
        part, d = where[i]
        other, e = where[m]
        blocks[t] = diagonal(part[d, j]) if i == m else diagonal(part[d, j], other[e, l])
    for t, ((i, j), (m, l)) in enumerate(tiles):
        lhs = jnp.where(low, cots[columns[i][1, side + j]], cots[columns[m][1, side + l]])
        prod[t] = across(lhs, blocks[t])
    me = lax.axis_index("tensor")
    begin = 0
    if not first:
        begin = before[0].shape[0]
        rows_of_slots = jnp.concatenate([head[0:1] for head in heads], axis=0).astype(BF16)
        for k in range(n_tensor):
            outs[k][:begin, :] = before[k][...]
            outs[k][begin + len(tiles) * share:, :] = rows_of_slots
    for k in range(n_tensor):
        start = pl.multiple_of(lax.rem(me + k, n_tensor) * share, share)
        for t in range(0, len(tiles), 2):
            two = [prod[t, pl.ds(start, share), :], prod[t + 1, pl.ds(start, share), :]]
            here = slice(begin + t * share, begin + (t + 2) * share)
            outs[k][here, :] = jnp.concatenate(two, axis=0).astype(BF16)


def slot_tiles(n, pairs):
    tiles = []
    for i in range(0, n, 4):
        tiles += [((m, j), (m, j + pairs)) for m in range(i, i + 4) for j in range(pairs - 1)]
        tiles += [((m, pairs - 1), (m + 1, pairs - 1)) for m in range(i, i + 4, 2)]
    return tiles


def rows_kernel(count, n_parts, n_tensor, *refs):
    gathered, cot, outs = refs[:n_parts], refs[n_parts], refs[n_parts + 1:n_parts + 1 + n_tensor]
    ids_vmem, ids, cots, acc, sem = refs[n_parts + 1 + n_tensor:]
    pairs, side = gathered[0].shape[1:3]
    row_count = acc.shape[0] - 1
    rows = cot.shape[0]
    copy = load_ids(gathered, ids_vmem, ids, sem)
    acc[...] = jnp.zeros_like(acc)
    load_cotangent(cot, cots)
    low = low_half((rows, 2 * side))
    copy.wait()

    def add(part, d, i):
        for k in range(pairs):
            left, right = ids[1, i, side + k], ids[1, i, side + k + pairs]
            lhs = cots[left]
            if k + pairs >= count:
                prod = across(lhs[:, :side], part[d, k][:, :side])
                acc[ids[0, i, side + k], :, :side] += prod
            else:
                prod = across(jnp.where(low, lhs, cots[right]), diagonal(part[d, k]))
                acc[ids[0, i, side + k]] += jnp.where(low, prod, 0.0)
                acc[ids[0, i, side + k + pairs]] += jnp.where(low, 0.0, prod)

    over(gathered, add)
    me = lax.axis_index("tensor")
    share = rows // n_tensor
    for k in range(n_tensor):
        start = pl.multiple_of(lax.rem(me + k, n_tensor) * share, share)
        half = low_half((share, 2 * side))
        for r in range(0, row_count, 2):
            pair = [fold(acc[r + u, pl.ds(start, share), :]) for u in range(2)]
            outs[k][:, r * side:(r + 2) * side] = jnp.where(half, *pair).astype(BF16)


def load_tokens(token_parts, blocks):
    tokens = [part.at[i] for part in token_parts for i in range(part.shape[0])]
    row_count, width = blocks.shape[0] - 1, blocks.shape[2]
    for r in range(0, row_count, 2):
        parts = [value[:, r * width // 2:(r + 2) * width // 2].astype(F32) for value in tokens]
        blocks[r], blocks[r + 1] = twice(jnp.concatenate(parts, axis=0).astype(BF16))
    blocks[row_count] = jnp.zeros_like(blocks[row_count])


def multiply_tokens(count, gathered, ids, blocks, prod):
    pairs, side = gathered[0].shape[1:3]
    low = low_half(blocks.shape[1:])

    def multiply(part, d, i):
        for k in range(pairs):
            lhs = blocks[ids(0, i, side + k)]
            if k + pairs < count:
                lhs = jnp.where(low, lhs, blocks[ids(0, i, side + k + pairs)])
                tile = diagonal(part[d, k])
            else:
                lhs, tile = lhs[:, :side], part[d, k]
            prod[i * pairs + k] = jnp.dot(lhs, tile, preferred_element_type=F32)

    over(gathered, multiply)


def add_tokens(count, gathered, ids, prod, left_acc, right_acc):
    pairs, side = gathered[0].shape[1:3]

    def add(part, d, i):
        for k in range(pairs):
            value, left = prod[i * pairs + k], ids(1, i, side + k)
            left_sum = left_acc[left] + value
            if k + pairs < count:
                right = ids(1, i, side + k + pairs)
                right_sum = right_acc[right] + value
                right_acc[right] = right_sum
            left_acc[left] = left_sum

    over(gathered, add)


def place_outputs(n_tensor, left_acc, right_acc, stage):
    col_count, rows, width = left_acc.shape[0] - 1, left_acc.shape[1], left_acc.shape[2]
    share = rows // n_tensor
    me = lax.axis_index("tensor")
    half = low_half((share, width))
    for i, k in enumerate(peer_order(n_tensor)):
        start = pl.multiple_of(lax.bitwise_xor(me, k) * share, share)
        mine = slice(i * share, (i + 1) * share)
        for c in range(0, col_count, 2):
            sums = [fold(jnp.where(half, left_acc[c + u, mine, :], right_acc[c + u, mine, :])) for u in range(2)]
            stage[pl.ds(start, share), c * width // 2:(c + 2) * width // 2] = jnp.where(half, *sums)


def forward_kernel(count, few, n_parts, n_token_parts, n_tensor, *refs):
    gathered, token_parts = refs[:n_parts], refs[n_parts:n_parts + n_token_parts]
    out, blocks, prod, left_acc, right_acc, stage = refs[n_parts + n_token_parts:][:6]
    if few:
        heads = [part[d, part.shape[1] - 1, 0:16, :].astype(F32) for part in gathered for d in range(part.shape[0])]
        heads = [head.astype(I32) for head in heads]
        ids = lambda line, i, lane: heads[i][line, lane]
    else:
        ids_vmem, scalars, sem = refs[-3:]
        copy = load_ids(gathered, ids_vmem, scalars, sem)
        ids = lambda line, i, lane: scalars[line, i, lane]
    left_acc[...] = jnp.zeros_like(left_acc)
    right_acc[...] = jnp.zeros_like(right_acc)
    load_tokens(token_parts, blocks)
    if not few:
        copy.wait()
    multiply_tokens(count, gathered, ids, blocks, prod)
    add_tokens(count, gathered, ids, prod, left_acc, right_acc)
    place_outputs(n_tensor, left_acc, right_acc, stage)
    out[...] = stage[...].astype(BF16)


def sum_kernel(sizes, pairs, n_dp, *refs):
    groups = []
    for size in sizes:
        groups, refs = groups + [refs[:size]], refs[size:]
    n_tensor = len(groups)
    (grad, grad_vmem, grad_sems), accs = refs[:3], refs[3:]
    share, width = grad.shape
    side = groups[0][0].shape[1] // 2
    tiles = slot_tiles(n_dp, pairs)
    end = len(tiles) * share

    def load(group, start, stop):
        value = group[0][start:stop, :].astype(F32)
        for message in group[1:]:
            value = value + message[start:stop, :].astype(F32)
        return value

    places = [load(group, end, end + n_dp).astype(I32) for group in groups]
    for acc in accs:
        acc[...] = jnp.zeros_like(acc)
    low = low_half((share, 2 * side))
    for t in range(0, len(tiles), 2):
        both = [load(group, t * share, (t + 2) * share) for group in groups]
        for u in range(2):
            values = [two[u * share:(u + 1) * share] for two in both]
            for h, (i, j) in enumerate(tiles[t + u]):
                rows = [place[i, side + j] for place in places]
                halves = [jnp.where(low, 0.0, value) if h else jnp.where(low, value, 0.0) for value in values]
                sums = [acc[row] + half for acc, row, half in zip(accs, rows, halves)]
                for acc, row, value in zip(accs, rows, sums):
                    acc[row] = value

    def total(r):
        value = accs[0][r]
        for acc in accs[1:]:
            value = value + acc[r]
        return fold(value)

    copies = []
    chunk = width // grad_sems.shape[0]
    for c in range(grad_sems.shape[0]):
        for r in range(c * chunk // side, (c + 1) * chunk // side, 2):
            grad_vmem[:, r * side:(r + 2) * side] = jnp.where(low, total(r), total(r + 1)).astype(BF16)
        here = slice(c * chunk, (c + 1) * chunk)
        copies.append(pltpu.make_async_copy(grad_vmem.at[:, here], grad.at[:, here], grad_sems.at[c]))
        copies[-1].start()
    for copy in copies:
        copy.wait()


def steps(n):
    return [n >> i for i in range(1, n.bit_length())]


def peer_order(n):
    order = [0]
    for k in steps(n):
        order = order + [i ^ k for i in order]
    return order


def swap(value, axis, n, k):
    return lax.ppermute(value, axis, [(i, i ^ k) for i in range(n)])


def shift(value, axis, n, k):
    return lax.ppermute(value, axis, [(i, (i + k) % n) for i in range(n)])


def gather_all(packed, inputs, n_dp, n_tensor):
    if (n_dp, n_tensor) != (8, 4):
        tokens = [inputs[None]]
        for k in steps(n_tensor):
            tokens = tokens + [swap(value, "tensor", n_tensor, k) for value in tokens]
        return [lax.all_gather(packed, "dp", axis=0, tiled=True)], tokens
    far_tokens = swap(inputs, "tensor", n_tensor, 2)
    near, second, last = [swap(packed, "dp", n_dp, k) for k in (2, 4, 6)]
    joined, tokens = pl.pallas_call(
        join_kernel,
        out_shape=[
            pltpu.VMEM((2, *packed.shape[1:]), packed.dtype),
            pltpu.VMEM((2, *inputs.shape), inputs.dtype),
        ],
        in_specs=[VMEM] * 4,
        out_specs=[VMEM] * 2,
        compiler_params=pltpu.CompilerParams(vmem_limit_bytes=4 * MIB),
    )(packed, near, inputs, far_tokens)
    same_core = [joined, second, last]
    parts = same_core + [swap(part, "dp", n_dp, 1) for part in same_core]
    return parts, [tokens, swap(tokens, "tensor", n_tensor, 1)]


def on_device(n_dp, n_tensor, inputs, block_values, block_slot, grad_out):
    share, width = inputs.shape
    rows, hidden = grad_out.shape
    _, count, side, _ = block_values.shape
    row_count, col_count = width // side, hidden // side
    pairs = count // 2 + 1
    small = (n_dp, n_tensor) == (8, 4)
    per_slot = small and n_dp * count < row_count and count == 2 * pairs - 1
    params = pltpu.CompilerParams(vmem_limit_bytes=(12 if small else 48) * MIB)

    packed = pl.pallas_call(
        functools.partial(pack_kernel, count, row_count, col_count),
        out_shape=pltpu.VMEM((1, pairs, side, 2 * side), BF16),
        in_specs=[HBM, HBM],
        out_specs=VMEM,
        scratch_shapes=[
            pltpu.VMEM(block_slot.shape, I32),
            pltpu.VMEM(block_values.shape, BF16),
            pltpu.SemaphoreType.DMA((count + 1,)),
        ],
        compiler_params=pltpu.CompilerParams(vmem_limit_bytes=4 * MIB),
    )(
        pltpu.with_memory_space_constraint(block_slot, pltpu.HBM),
        pltpu.with_memory_space_constraint(block_values, pltpu.HBM),
    )
    gathered, tokens = gather_all(packed, inputs, n_dp, n_tensor)
    n_parts = len(gathered)
    ids = [pltpu.VMEM((2, n_dp, 2 * side), I32), pltpu.SMEM((2, n_dp, 2 * side), I32)]
    cots = (col_count + 1, rows, 2 * side)
    if per_slot:
        half, tiles = n_parts // 2, len(slot_tiles(n_dp, pairs)) // 2
        scratch = [
            pltpu.VMEM((tiles, rows, 2 * side), F32),
            pltpu.VMEM((tiles, 2 * side, 2 * side), BF16),
        ]
        *first_slots, cotangent = pl.pallas_call(
            functools.partial(slots_kernel, True, half, n_tensor),
            out_shape=[pltpu.VMEM((tiles * share, 2 * side), BF16)] * n_tensor + [pltpu.VMEM(cots, BF16)],
            in_specs=[VMEM] * (half + 1),
            out_specs=[VMEM] * (n_tensor + 1),
            scratch_shapes=scratch,
            compiler_params=params,
        )(*gathered[:half], grad_out)
        partial_sums = pl.pallas_call(
            functools.partial(slots_kernel, False, n_parts, n_tensor),
            out_shape=[pltpu.VMEM((2 * tiles * share + n_dp, 2 * side), BF16)] * n_tensor,
            in_specs=[VMEM] * (n_parts + 1 + n_tensor),
            out_specs=[VMEM] * n_tensor,
            scratch_shapes=scratch,
            compiler_params=params,
        )(*gathered, cotangent, *first_slots)
        groups = [[partial_sums[0]]] + [[shift(partial_sums[k], "tensor", n_tensor, k)] for k in (2, 1, 3)]
    else:
        partial_sums = pl.pallas_call(
            functools.partial(rows_kernel, count, n_parts, n_tensor),
            out_shape=[jax.ShapeDtypeStruct((share, width), BF16)] * n_tensor,
            in_specs=[VMEM] * (n_parts + 1),
            out_specs=[VMEM] * n_tensor,
            scratch_shapes=ids + [
                pltpu.VMEM(cots, BF16),
                pltpu.VMEM((row_count + 1, rows, 2 * side), F32),
                pltpu.SemaphoreType.DMA,
            ],
            compiler_params=params,
        )(*gathered, grad_out)
        arrived = [partial_sums[0]] + [shift(partial_sums[k], "tensor", n_tensor, k) for k in range(1, n_tensor)]
    outputs = pl.pallas_call(
        functools.partial(forward_kernel, count, per_slot, n_parts, len(tokens), n_tensor),
        out_shape=jax.ShapeDtypeStruct((rows, hidden), BF16),
        in_specs=[VMEM] * (n_parts + len(tokens)),
        out_specs=VMEM,
        scratch_shapes=[
            pltpu.VMEM((row_count + 1, rows, 2 * side), BF16),
            pltpu.VMEM((n_dp * pairs, rows, 2 * side), F32),
            pltpu.VMEM((col_count + 1, rows, 2 * side), F32),
            pltpu.VMEM((col_count + 1, rows, 2 * side), F32),
            pltpu.VMEM((rows, hidden), F32),
        ] + ([] if per_slot else ids + [pltpu.SemaphoreType.DMA]),
        compiler_params=params,
    )(*gathered, *tokens)
    if per_slot:
        grad_in = pl.pallas_call(
            functools.partial(sum_kernel, tuple(map(len, groups)), pairs, n_dp),
            out_shape=jax.ShapeDtypeStruct((share, width), BF16),
            in_specs=[VMEM] * sum(map(len, groups)),
            out_specs=HBM,
            scratch_shapes=[
                pltpu.VMEM((share, width), BF16),
                pltpu.SemaphoreType.DMA((4,)),
            ] + [pltpu.VMEM((row_count + 1, share, 2 * side), F32)] * n_tensor,
            compiler_params=params,
        )(*(message for group in groups for message in group))
        return (outputs, grad_in)
    total = arrived[0].astype(F32)
    for value in arrived[1:]:
        total = total + value.astype(F32)
    return (outputs, total.astype(BF16))


def solution(mesh):
    placed = (
        P(("dp", "tensor"), None),
        P("tensor", "dp", None, None),
        P("tensor", "dp"),
        P("dp", "tensor"),
    )
    return jax.shard_map(
        functools.partial(on_device, mesh.shape["dp"], mesh.shape["tensor"]),
        mesh=mesh,
        in_specs=placed,
        out_specs=(P("dp", "tensor"), P(("dp", "tensor"), None)),
        check_vma=False,
    )
```

```python
import functools

import jax
import jax.numpy as jnp
from jax import lax
from jax.experimental import pallas as pl
from jax.experimental.pallas import tpu as pltpu
from jax.sharding import PartitionSpec as P

VMEM = pl.BlockSpec(memory_space=pltpu.VMEM)
HBM = pl.BlockSpec(memory_space=pltpu.HBM)
MIB = 1024 * 1024
BF16, F32, I32 = jnp.bfloat16, jnp.float32, jnp.int32


def pack_kernel(count, row_count, col_count, slots_hbm, values_hbm, packed, slots, values, sems):
    copies = [pltpu.make_async_copy(slots_hbm, slots, sems.at[count])]
    copies += [pltpu.make_async_copy(values_hbm.at[0, j], values.at[0, j], sems.at[j]) for j in range(count)]
    for copy in copies:
        copy.start()
    side = values.shape[2]
    pairs = packed.shape[1]
    copies[0].wait()
    position = jnp.concatenate([slots[...], jnp.full((1, side - count), -1, I32)], axis=1)
    exact = position.astype(F32)
    row = jnp.floor((exact + 0.5) * (1.0 / col_count))
    col = exact - row * col_count
    row = jnp.where(position >= 0, row, float(row_count))
    col = jnp.where(position >= 0, col, float(col_count))
    head = jnp.concatenate([row, col, jnp.zeros((side - 2, side), F32)], axis=0).astype(BF16)
    for copy in copies[1:]:
        copy.wait()
    for k in range(pairs):
        left = values[0, k]
        right = values[0, k + pairs] if k + pairs < count else head
        packed[0, k] = jnp.concatenate([left, right], axis=1)


def join_kernel(own, near, tokens, far_tokens, joined, joined_tokens):
    joined[0], joined[1] = own[0], near[0]
    joined_tokens[0], joined_tokens[1] = tokens[...], far_tokens[...]


def load_ids(gathered, ids_vmem, ids, sem):
    i = 0
    for part in gathered:
        n, pairs = part.shape[:2]
        for d in range(n):
            head = part[d, pairs - 1, 0:16, :].astype(F32).astype(I32)
            ids_vmem[0, i:i + 1, :] = head[0:1]
            ids_vmem[1, i:i + 1, :] = head[1:2]
            i += 1
    copy = pltpu.make_async_copy(ids_vmem, ids, sem)
    copy.start()
    return copy


def over(gathered, body):
    start = 0
    for part in gathered:
        n = part.shape[0]
        if n <= 8:
            for d in range(n):
                body(part, d, start + d)
        else:
            def step(d, carry, part=part, start=start):
                body(part, d, start + d)
                return carry
            lax.fori_loop(0, n, step, 0)
        start += n


def low_half(shape):
    return lax.broadcasted_iota(I32, shape, 1) < shape[1] // 2


def swap_halves(x):
    half = x.shape[1] // 2
    return jnp.concatenate([x[:, half:], x[:, :half]], axis=1)


def twice(x):
    low, y = low_half(x.shape), swap_halves(x)
    return jnp.where(low, x, y), jnp.where(low, y, x)


def diagonal(tile, other=None):
    low = low_half(tile.shape)
    zero = jnp.zeros_like(tile)
    top = jnp.where(low, tile, zero)
    bottom = jnp.where(low, zero, tile if other is None else swap_halves(other))
    return jnp.concatenate([top, bottom], axis=0)


def fold(x):
    return x + pltpu.roll(x, x.shape[1] // 2, 1)


def across(lhs, rhs):
    return lax.dot_general(lhs, rhs, (((1,), (1,)), ((), ())), preferred_element_type=F32)


def load_cotangent(cot, cots):
    col_count = cots.shape[0] - 1
    for c in range(0, col_count, 2):
        width = cots.shape[2]
        cots[c], cots[c + 1] = twice(cot[:, c * width // 2:(c + 2) * width // 2])
    cots[col_count] = jnp.zeros_like(cots[col_count])


def slots_kernel(first, n_parts, n_tensor, *refs):
    gathered, refs = refs[:n_parts], refs[n_parts:]
    if first:
        cot, (*outs, cots), (prod, blocks) = refs[0], refs[1:n_tensor + 2], refs[n_tensor + 2:]
        before = []
    else:
        cots, before, outs = refs[0], refs[1:n_tensor + 1], refs[n_tensor + 1:2 * n_tensor + 1]
        prod, blocks = refs[2 * n_tensor + 1:]
    pairs, side = gathered[0].shape[1:3]
    rows = cots.shape[1]
    share = rows // n_tensor
    if first:
        load_cotangent(cot, cots)
    low = low_half((rows, 2 * side))
    where = [(part, d) for part in gathered for d in range(part.shape[0])]
    heads = [part[d, pairs - 1, 0:16, :].astype(F32) for part, d in where]
    columns = [head.astype(I32) for head in heads]
    tiles = slot_tiles(len(where), pairs)[-prod.shape[0]:]
    for t, ((i, j), (m, l)) in enumerate(tiles):
        part, d = where[i]
        other, e = where[m]
        blocks[t] = diagonal(part[d, j]) if i == m else diagonal(part[d, j], other[e, l])
    for t, ((i, j), (m, l)) in enumerate(tiles):
        lhs = jnp.where(low, cots[columns[i][1, side + j]], cots[columns[m][1, side + l]])
        prod[t] = across(lhs, blocks[t])
    me = lax.axis_index("tensor")
    begin = 0
    if not first:
        begin = before[0].shape[0]
        rows_of_slots = jnp.concatenate([head[0:1] for head in heads], axis=0).astype(BF16)
        for k in range(n_tensor):
            outs[k][:begin, :] = before[k][...]
            outs[k][begin + len(tiles) * share:, :] = rows_of_slots
    for k in range(n_tensor):
        start = pl.multiple_of(lax.rem(me + k, n_tensor) * share, share)
        for t in range(0, len(tiles), 2):
            two = [prod[t, pl.ds(start, share), :], prod[t + 1, pl.ds(start, share), :]]
            here = slice(begin + t * share, begin + (t + 2) * share)
            outs[k][here, :] = jnp.concatenate(two, axis=0).astype(BF16)


def slot_tiles(n, pairs):
    tiles = []
    for i in range(0, n, 4):
        tiles += [((m, j), (m, j + pairs)) for m in range(i, i + 4) for j in range(pairs - 1)]
        tiles += [((m, pairs - 1), (m + 1, pairs - 1)) for m in range(i, i + 4, 2)]
    return tiles


def rows_kernel(count, n_parts, n_tensor, *refs):
    gathered, cot, outs = refs[:n_parts], refs[n_parts], refs[n_parts + 1:n_parts + 1 + n_tensor]
    ids_vmem, ids, cots, acc, sem = refs[n_parts + 1 + n_tensor:]
    pairs, side = gathered[0].shape[1:3]
    row_count = acc.shape[0] - 1
    rows = cot.shape[0]
    copy = load_ids(gathered, ids_vmem, ids, sem)
    acc[...] = jnp.zeros_like(acc)
    load_cotangent(cot, cots)
    low = low_half((rows, 2 * side))
    copy.wait()

    def add(part, d, i):
        for k in range(pairs):
            left, right = ids[1, i, side + k], ids[1, i, side + k + pairs]
            lhs = cots[left]
            if k + pairs >= count:
                prod = across(lhs[:, :side], part[d, k][:, :side])
                acc[ids[0, i, side + k], :, :side] += prod
            else:
                prod = across(jnp.where(low, lhs, cots[right]), diagonal(part[d, k]))
                acc[ids[0, i, side + k]] += jnp.where(low, prod, 0.0)
                acc[ids[0, i, side + k + pairs]] += jnp.where(low, 0.0, prod)

    over(gathered, add)
    me = lax.axis_index("tensor")
    share = rows // n_tensor
    for k in range(n_tensor):
        start = pl.multiple_of(lax.rem(me + k, n_tensor) * share, share)
        half = low_half((share, 2 * side))
        for r in range(0, row_count, 2):
            pair = [fold(acc[r + u, pl.ds(start, share), :]) for u in range(2)]
            outs[k][:, r * side:(r + 2) * side] = jnp.where(half, *pair).astype(BF16)


def load_tokens(token_parts, blocks):
    tokens = [part.at[i] for part in token_parts for i in range(part.shape[0])]
    row_count, width = blocks.shape[0] - 1, blocks.shape[2]
    for r in range(0, row_count, 2):
        parts = [value[:, r * width // 2:(r + 2) * width // 2].astype(F32) for value in tokens]
        blocks[r], blocks[r + 1] = twice(jnp.concatenate(parts, axis=0).astype(BF16))
    blocks[row_count] = jnp.zeros_like(blocks[row_count])


def multiply_tokens(count, gathered, ids, blocks, prod):
    pairs, side = gathered[0].shape[1:3]
    low = low_half(blocks.shape[1:])

    def multiply(part, d, i):
        for k in range(pairs):
            lhs = blocks[ids(0, i, side + k)]
            if k + pairs < count:
                lhs = jnp.where(low, lhs, blocks[ids(0, i, side + k + pairs)])
                tile = diagonal(part[d, k])
            else:
                lhs, tile = lhs[:, :side], part[d, k]
            prod[i * pairs + k] = jnp.dot(lhs, tile, preferred_element_type=F32)

    over(gathered, multiply)


def add_tokens(count, gathered, ids, prod, left_acc, right_acc):
    pairs, side = gathered[0].shape[1:3]

    def add(part, d, i):
        for k in range(pairs):
            value, left = prod[i * pairs + k], ids(1, i, side + k)
            left_sum = left_acc[left] + value
            if k + pairs < count:
                right = ids(1, i, side + k + pairs)
                right_sum = right_acc[right] + value
                right_acc[right] = right_sum
            left_acc[left] = left_sum

    over(gathered, add)


def place_outputs(n_tensor, left_acc, right_acc, stage):
    col_count, rows, width = left_acc.shape[0] - 1, left_acc.shape[1], left_acc.shape[2]
    share = rows // n_tensor
    me = lax.axis_index("tensor")
    half = low_half((share, width))
    for i, k in enumerate(peer_order(n_tensor)):
        start = pl.multiple_of(lax.bitwise_xor(me, k) * share, share)
        mine = slice(i * share, (i + 1) * share)
        for c in range(0, col_count, 2):
            sums = [fold(jnp.where(half, left_acc[c + u, mine, :], right_acc[c + u, mine, :])) for u in range(2)]
            stage[pl.ds(start, share), c * width // 2:(c + 2) * width // 2] = jnp.where(half, *sums)


def forward_kernel(count, few, n_parts, n_token_parts, n_tensor, *refs):
    gathered, token_parts = refs[:n_parts], refs[n_parts:n_parts + n_token_parts]
    out, blocks, prod, left_acc, right_acc, stage = refs[n_parts + n_token_parts:][:6]
    if few:
        heads = [part[d, part.shape[1] - 1, 0:16, :].astype(F32) for part in gathered for d in range(part.shape[0])]
        heads = [head.astype(I32) for head in heads]
        ids = lambda line, i, lane: heads[i][line, lane]
    else:
        ids_vmem, scalars, sem = refs[-3:]
        copy = load_ids(gathered, ids_vmem, scalars, sem)
        ids = lambda line, i, lane: scalars[line, i, lane]
    left_acc[...] = jnp.zeros_like(left_acc)
    right_acc[...] = jnp.zeros_like(right_acc)
    load_tokens(token_parts, blocks)
    if not few:
        copy.wait()
    multiply_tokens(count, gathered, ids, blocks, prod)
    add_tokens(count, gathered, ids, prod, left_acc, right_acc)
    place_outputs(n_tensor, left_acc, right_acc, stage)
    out[...] = stage[...].astype(BF16)


def sum_kernel(sizes, pairs, n_dp, *refs):
    groups = []
    for size in sizes:
        groups, refs = groups + [refs[:size]], refs[size:]
    n_tensor = len(groups)
    (grad, grad_vmem, grad_sems), accs = refs[:3], refs[3:]
    share, width = grad.shape
    side = groups[0][0].shape[1] // 2
    tiles = slot_tiles(n_dp, pairs)
    end = len(tiles) * share

    def load(group, start, stop):
        value = group[0][start:stop, :].astype(F32)
        for message in group[1:]:
            value = value + message[start:stop, :].astype(F32)
        return value

    places = [load(group, end, end + n_dp).astype(I32) for group in groups]
    for acc in accs:
        acc[...] = jnp.zeros_like(acc)
    low = low_half((share, 2 * side))
    for t in range(0, len(tiles), 2):
        both = [load(group, t * share, (t + 2) * share) for group in groups]
        for u in range(2):
            values = [two[u * share:(u + 1) * share] for two in both]
            for h, (i, j) in enumerate(tiles[t + u]):
                rows = [place[i, side + j] for place in places]
                halves = [jnp.where(low, 0.0, value) if h else jnp.where(low, value, 0.0) for value in values]
                sums = [acc[row] + half for acc, row, half in zip(accs, rows, halves)]
                for acc, row, value in zip(accs, rows, sums):
                    acc[row] = value

    def total(r):
        value = accs[0][r]
        for acc in accs[1:]:
            value = value + acc[r]
        return fold(value)

    copies = []
    chunk = width // grad_sems.shape[0]
    for c in range(grad_sems.shape[0]):
        for r in range(c * chunk // side, (c + 1) * chunk // side, 2):
            grad_vmem[:, r * side:(r + 2) * side] = jnp.where(low, total(r), total(r + 1)).astype(BF16)
        here = slice(c * chunk, (c + 1) * chunk)
        copies.append(pltpu.make_async_copy(grad_vmem.at[:, here], grad.at[:, here], grad_sems.at[c]))
        copies[-1].start()
    for copy in copies:
        copy.wait()


def steps(n):
    return [n >> i for i in range(1, n.bit_length())]


def peer_order(n):
    order = [0]
    for k in steps(n):
        order = order + [i ^ k for i in order]
    return order


def swap(value, axis, n, k):
    return lax.ppermute(value, axis, [(i, i ^ k) for i in range(n)])


def shift(value, axis, n, k):
    return lax.ppermute(value, axis, [(i, (i + k) % n) for i in range(n)])


def gather_all(packed, inputs, n_dp, n_tensor):
    if (n_dp, n_tensor) != (8, 4):
        tokens = [inputs[None]]
        for k in steps(n_tensor):
            tokens = tokens + [swap(value, "tensor", n_tensor, k) for value in tokens]
        return [lax.all_gather(packed, "dp", axis=0, tiled=True)], tokens
    far_tokens = swap(inputs, "tensor", n_tensor, 2)
    near, second, last = [swap(packed, "dp", n_dp, k) for k in (6, 2, 4)]
    joined, tokens = pl.pallas_call(
        join_kernel,
        out_shape=[
            pltpu.VMEM((2, *packed.shape[1:]), packed.dtype),
            pltpu.VMEM((2, *inputs.shape), inputs.dtype),
        ],
        in_specs=[VMEM] * 4,
        out_specs=[VMEM] * 2,
        compiler_params=pltpu.CompilerParams(vmem_limit_bytes=4 * MIB),
    )(packed, near, inputs, far_tokens)
    same_core = [joined, second, last]
    parts = same_core + [swap(part, "dp", n_dp, 1) for part in same_core]
    return parts, [tokens, swap(tokens, "tensor", n_tensor, 1)]


def on_device(n_dp, n_tensor, inputs, block_values, block_slot, grad_out):
    share, width = inputs.shape
    rows, hidden = grad_out.shape
    _, count, side, _ = block_values.shape
    row_count, col_count = width // side, hidden // side
    pairs = count // 2 + 1
    small = (n_dp, n_tensor) == (8, 4)
    per_slot = small and n_dp * count < row_count and count == 2 * pairs - 1
    params = pltpu.CompilerParams(vmem_limit_bytes=(12 if small else 48) * MIB)

    packed = pl.pallas_call(
        functools.partial(pack_kernel, count, row_count, col_count),
        out_shape=pltpu.VMEM((1, pairs, side, 2 * side), BF16),
        in_specs=[HBM, HBM],
        out_specs=VMEM,
        scratch_shapes=[
            pltpu.VMEM(block_slot.shape, I32),
            pltpu.VMEM(block_values.shape, BF16),
            pltpu.SemaphoreType.DMA((count + 1,)),
        ],
        compiler_params=pltpu.CompilerParams(vmem_limit_bytes=4 * MIB),
    )(
        pltpu.with_memory_space_constraint(block_slot, pltpu.HBM),
        pltpu.with_memory_space_constraint(block_values, pltpu.HBM),
    )
    gathered, tokens = gather_all(packed, inputs, n_dp, n_tensor)
    n_parts = len(gathered)
    ids = [pltpu.VMEM((2, n_dp, 2 * side), I32), pltpu.SMEM((2, n_dp, 2 * side), I32)]
    cots = (col_count + 1, rows, 2 * side)
    if per_slot:
        half, tiles = n_parts // 2, len(slot_tiles(n_dp, pairs)) // 2
        scratch = [
            pltpu.VMEM((tiles, rows, 2 * side), F32),
            pltpu.VMEM((tiles, 2 * side, 2 * side), BF16),
        ]
        *first_slots, cotangent = pl.pallas_call(
            functools.partial(slots_kernel, True, half, n_tensor),
            out_shape=[pltpu.VMEM((tiles * share, 2 * side), BF16)] * n_tensor + [pltpu.VMEM(cots, BF16)],
            in_specs=[VMEM] * (half + 1),
            out_specs=[VMEM] * (n_tensor + 1),
            scratch_shapes=scratch,
            compiler_params=params,
        )(*gathered[:half], grad_out)
        partial_sums = pl.pallas_call(
            functools.partial(slots_kernel, False, n_parts, n_tensor),
            out_shape=[pltpu.VMEM((2 * tiles * share + n_dp, 2 * side), BF16)] * n_tensor,
            in_specs=[VMEM] * (n_parts + 1 + n_tensor),
            out_specs=[VMEM] * n_tensor,
            scratch_shapes=scratch,
            compiler_params=params,
        )(*gathered, cotangent, *first_slots)
        groups = [[partial_sums[0]]] + [[shift(partial_sums[k], "tensor", n_tensor, k)] for k in (2, 1, 3)]
    else:
        partial_sums = pl.pallas_call(
            functools.partial(rows_kernel, count, n_parts, n_tensor),
            out_shape=[jax.ShapeDtypeStruct((share, width), BF16)] * n_tensor,
            in_specs=[VMEM] * (n_parts + 1),
            out_specs=[VMEM] * n_tensor,
            scratch_shapes=ids + [
                pltpu.VMEM(cots, BF16),
                pltpu.VMEM((row_count + 1, rows, 2 * side), F32),
                pltpu.SemaphoreType.DMA,
            ],
            compiler_params=params,
        )(*gathered, grad_out)
        arrived = [partial_sums[0]] + [shift(partial_sums[k], "tensor", n_tensor, k) for k in range(1, n_tensor)]
    outputs = pl.pallas_call(
        functools.partial(forward_kernel, count, per_slot, n_parts, len(tokens), n_tensor),
        out_shape=jax.ShapeDtypeStruct((rows, hidden), BF16),
        in_specs=[VMEM] * (n_parts + len(tokens)),
        out_specs=VMEM,
        scratch_shapes=[
            pltpu.VMEM((row_count + 1, rows, 2 * side), BF16),
            pltpu.VMEM((n_dp * pairs, rows, 2 * side), F32),
            pltpu.VMEM((col_count + 1, rows, 2 * side), F32),
            pltpu.VMEM((col_count + 1, rows, 2 * side), F32),
            pltpu.VMEM((rows, hidden), F32),
        ] + ([] if per_slot else ids + [pltpu.SemaphoreType.DMA]),
        compiler_params=params,
    )(*gathered, *tokens)
    if per_slot:
        grad_in = pl.pallas_call(
            functools.partial(sum_kernel, tuple(map(len, groups)), pairs, n_dp),
            out_shape=jax.ShapeDtypeStruct((share, width), BF16),
            in_specs=[VMEM] * sum(map(len, groups)),
            out_specs=HBM,
            scratch_shapes=[
                pltpu.VMEM((share, width), BF16),
                pltpu.SemaphoreType.DMA((4,)),
            ] + [pltpu.VMEM((row_count + 1, share, 2 * side), F32)] * n_tensor,
            compiler_params=params,
        )(*(message for group in groups for message in group))
        return (outputs, grad_in)
    total = arrived[0].astype(F32)
    for value in arrived[1:]:
        total = total + value.astype(F32)
    return (outputs, total.astype(BF16))


def solution(mesh):
    placed = (
        P(("dp", "tensor"), None),
        P("tensor", "dp", None, None),
        P("tensor", "dp"),
        P("dp", "tensor"),
    )
    return jax.shard_map(
        functools.partial(on_device, mesh.shape["dp"], mesh.shape["tensor"]),
        mesh=mesh,
        in_specs=placed,
        out_specs=(P("dp", "tensor"), P(("dp", "tensor"), None)),
        check_vma=False,
    )
```

```python
import functools

import jax
import jax.numpy as jnp
from jax import lax
from jax.experimental import pallas as pl
from jax.experimental.pallas import tpu as pltpu
from jax.sharding import PartitionSpec as P

VMEM = pl.BlockSpec(memory_space=pltpu.VMEM)
HBM = pl.BlockSpec(memory_space=pltpu.HBM)
MIB = 1024 * 1024
BF16, F32, I32 = jnp.bfloat16, jnp.float32, jnp.int32


def pack_kernel(count, row_count, col_count, slots_hbm, values_hbm, packed, slots, values, sems):
    copies = [pltpu.make_async_copy(slots_hbm, slots, sems.at[count])]
    copies += [pltpu.make_async_copy(values_hbm.at[0, j], values.at[0, j], sems.at[j]) for j in range(count)]
    for copy in copies:
        copy.start()
    side = values.shape[2]
    pairs = packed.shape[1]
    copies[0].wait()
    position = jnp.concatenate([slots[...], jnp.full((1, side - count), -1, I32)], axis=1)
    exact = position.astype(F32)
    row = jnp.floor((exact + 0.5) * (1.0 / col_count))
    col = exact - row * col_count
    row = jnp.where(position >= 0, row, float(row_count))
    col = jnp.where(position >= 0, col, float(col_count))
    head = jnp.concatenate([row, col, jnp.zeros((side - 2, side), F32)], axis=0).astype(BF16)
    for copy in copies[1:]:
        copy.wait()
    for k in range(pairs):
        left = values[0, k]
        right = values[0, k + pairs] if k + pairs < count else head
        packed[0, k] = jnp.concatenate([left, right], axis=1)


def join_kernel(own, near, tokens, far_tokens, joined, joined_tokens):
    joined[0], joined[1] = own[0], near[0]
    joined_tokens[0], joined_tokens[1] = tokens[...], far_tokens[...]


def load_ids(gathered, ids_vmem, ids, sem):
    i = 0
    for part in gathered:
        n, pairs = part.shape[:2]
        for d in range(n):
            head = part[d, pairs - 1, 0:16, :].astype(F32).astype(I32)
            ids_vmem[0, i:i + 1, :] = head[0:1]
            ids_vmem[1, i:i + 1, :] = head[1:2]
            i += 1
    copy = pltpu.make_async_copy(ids_vmem, ids, sem)
    copy.start()
    return copy


def over(gathered, body):
    start = 0
    for part in gathered:
        n = part.shape[0]
        if n <= 8:
            for d in range(n):
                body(part, d, start + d)
        else:
            def step(d, carry, part=part, start=start):
                body(part, d, start + d)
                return carry
            lax.fori_loop(0, n, step, 0)
        start += n


def low_half(shape):
    return lax.broadcasted_iota(I32, shape, 1) < shape[1] // 2


def swap_halves(x):
    half = x.shape[1] // 2
    return jnp.concatenate([x[:, half:], x[:, :half]], axis=1)


def twice(x):
    low, y = low_half(x.shape), swap_halves(x)
    return jnp.where(low, x, y), jnp.where(low, y, x)


def diagonal(tile, other=None):
    low = low_half(tile.shape)
    zero = jnp.zeros_like(tile)
    top = jnp.where(low, tile, zero)
    bottom = jnp.where(low, zero, tile if other is None else swap_halves(other))
    return jnp.concatenate([top, bottom], axis=0)


def fold(x):
    return x + pltpu.roll(x, x.shape[1] // 2, 1)


def across(lhs, rhs):
    return lax.dot_general(lhs, rhs, (((1,), (1,)), ((), ())), preferred_element_type=F32)


def load_cotangent(cot, cots):
    col_count = cots.shape[0] - 1
    for c in range(0, col_count, 2):
        width = cots.shape[2]
        cots[c], cots[c + 1] = twice(cot[:, c * width // 2:(c + 2) * width // 2])
    cots[col_count] = jnp.zeros_like(cots[col_count])


def slots_kernel(first, n_parts, n_tensor, *refs):
    gathered, refs = refs[:n_parts], refs[n_parts:]
    if first:
        cot, (*outs, cots), (prod, blocks) = refs[0], refs[1:n_tensor + 2], refs[n_tensor + 2:]
        before = []
    else:
        cots, before, outs = refs[0], refs[1:n_tensor + 1], refs[n_tensor + 1:2 * n_tensor + 1]
        prod, blocks = refs[2 * n_tensor + 1:]
    pairs, side = gathered[0].shape[1:3]
    rows = cots.shape[1]
    share = rows // n_tensor
    if first:
        load_cotangent(cot, cots)
    low = low_half((rows, 2 * side))
    where = [(part, d) for part in gathered for d in range(part.shape[0])]
    heads = [part[d, pairs - 1, 0:16, :].astype(F32) for part, d in where]
    columns = [head.astype(I32) for head in heads]
    tiles = slot_tiles(len(where), pairs)[-prod.shape[0]:]
    for t, ((i, j), (m, l)) in enumerate(tiles):
        part, d = where[i]
        other, e = where[m]
        blocks[t] = diagonal(part[d, j]) if i == m else diagonal(part[d, j], other[e, l])
    for t, ((i, j), (m, l)) in enumerate(tiles):
        lhs = jnp.where(low, cots[columns[i][1, side + j]], cots[columns[m][1, side + l]])
        prod[t] = across(lhs, blocks[t])
    me = lax.axis_index("tensor")
    begin = 0
    if not first:
        begin = before[0].shape[0]
        rows_of_slots = jnp.concatenate([head[0:1] for head in heads] * 2, axis=0).astype(BF16)
        for k in range(n_tensor):
            outs[k][:begin, :] = before[k][...]
            outs[k][begin + len(tiles) * share:, :] = rows_of_slots
    for k in range(n_tensor):
        start = pl.multiple_of(lax.rem(me + k, n_tensor) * share, share)
        for t in range(0, len(tiles), 2):
            two = [prod[t, pl.ds(start, share), :], prod[t + 1, pl.ds(start, share), :]]
            here = slice(begin + t * share, begin + (t + 2) * share)
            outs[k][here, :] = jnp.concatenate(two, axis=0).astype(BF16)


def slot_tiles(n, pairs):
    tiles = []
    for i in range(0, n, 4):
        tiles += [((m, j), (m, j + pairs)) for m in range(i, i + 4) for j in range(pairs - 1)]
        tiles += [((m, pairs - 1), (m + 1, pairs - 1)) for m in range(i, i + 4, 2)]
    return tiles


def rows_kernel(count, n_parts, n_tensor, *refs):
    gathered, cot, outs = refs[:n_parts], refs[n_parts], refs[n_parts + 1:n_parts + 1 + n_tensor]
    ids_vmem, ids, cots, acc, sem = refs[n_parts + 1 + n_tensor:]
    pairs, side = gathered[0].shape[1:3]
    row_count = acc.shape[0] - 1
    rows = cot.shape[0]
    copy = load_ids(gathered, ids_vmem, ids, sem)
    acc[...] = jnp.zeros_like(acc)
    load_cotangent(cot, cots)
    low = low_half((rows, 2 * side))
    copy.wait()

    def add(part, d, i):
        for k in range(pairs):
            left, right = ids[1, i, side + k], ids[1, i, side + k + pairs]
            lhs = cots[left]
            if k + pairs >= count:
                prod = across(lhs[:, :side], part[d, k][:, :side])
                acc[ids[0, i, side + k], :, :side] += prod
            else:
                prod = across(jnp.where(low, lhs, cots[right]), diagonal(part[d, k]))
                acc[ids[0, i, side + k]] += jnp.where(low, prod, 0.0)
                acc[ids[0, i, side + k + pairs]] += jnp.where(low, 0.0, prod)

    over(gathered, add)
    me = lax.axis_index("tensor")
    share = rows // n_tensor
    for k in range(n_tensor):
        start = pl.multiple_of(lax.rem(me + k, n_tensor) * share, share)
        half = low_half((share, 2 * side))
        for r in range(0, row_count, 2):
            pair = [fold(acc[r + u, pl.ds(start, share), :]) for u in range(2)]
            outs[k][:, r * side:(r + 2) * side] = jnp.where(half, *pair).astype(BF16)


def load_tokens(token_parts, blocks):
    tokens = [part.at[i] for part in token_parts for i in range(part.shape[0])]
    row_count, width = blocks.shape[0] - 1, blocks.shape[2]
    for r in range(0, row_count, 2):
        parts = [value[:, r * width // 2:(r + 2) * width // 2].astype(F32) for value in tokens]
        blocks[r], blocks[r + 1] = twice(jnp.concatenate(parts, axis=0).astype(BF16))
    blocks[row_count] = jnp.zeros_like(blocks[row_count])


def multiply_tokens(count, gathered, ids, blocks, prod):
    pairs, side = gathered[0].shape[1:3]
    low = low_half(blocks.shape[1:])

    def multiply(part, d, i):
        for k in range(pairs):
            lhs = blocks[ids(0, i, side + k)]
            if k + pairs < count:
                lhs = jnp.where(low, lhs, blocks[ids(0, i, side + k + pairs)])
                tile = diagonal(part[d, k])
            else:
                lhs, tile = lhs[:, :side], part[d, k]
            prod[i * pairs + k] = jnp.dot(lhs, tile, preferred_element_type=F32)

    over(gathered, multiply)


def add_tokens(count, gathered, ids, prod, left_acc, right_acc):
    pairs, side = gathered[0].shape[1:3]

    def add(part, d, i):
        for k in range(pairs):
            value, left = prod[i * pairs + k], ids(1, i, side + k)
            left_sum = left_acc[left] + value
            if k + pairs < count:
                right = ids(1, i, side + k + pairs)
                right_sum = right_acc[right] + value
                right_acc[right] = right_sum
            left_acc[left] = left_sum

    over(gathered, add)


def place_outputs(n_tensor, left_acc, right_acc, stage):
    col_count, rows, width = left_acc.shape[0] - 1, left_acc.shape[1], left_acc.shape[2]
    share = rows // n_tensor
    me = lax.axis_index("tensor")
    half = low_half((share, width))
    for i, k in enumerate(peer_order(n_tensor)):
        start = pl.multiple_of(lax.bitwise_xor(me, k) * share, share)
        mine = slice(i * share, (i + 1) * share)
        for c in range(0, col_count, 2):
            sums = [fold(jnp.where(half, left_acc[c + u, mine, :], right_acc[c + u, mine, :])) for u in range(2)]
            stage[pl.ds(start, share), c * width // 2:(c + 2) * width // 2] = jnp.where(half, *sums)


def forward_kernel(count, few, n_parts, n_token_parts, n_tensor, *refs):
    gathered, token_parts = refs[:n_parts], refs[n_parts:n_parts + n_token_parts]
    out, blocks, prod, left_acc, right_acc, stage = refs[n_parts + n_token_parts:][:6]
    if few:
        heads = [part[d, part.shape[1] - 1, 0:16, :].astype(F32) for part in gathered for d in range(part.shape[0])]
        heads = [head.astype(I32) for head in heads]
        ids = lambda line, i, lane: heads[i][line, lane]
    else:
        ids_vmem, scalars, sem = refs[-3:]
        copy = load_ids(gathered, ids_vmem, scalars, sem)
        ids = lambda line, i, lane: scalars[line, i, lane]
    left_acc[...] = jnp.zeros_like(left_acc)
    right_acc[...] = jnp.zeros_like(right_acc)
    load_tokens(token_parts, blocks)
    if not few:
        copy.wait()
    multiply_tokens(count, gathered, ids, blocks, prod)
    add_tokens(count, gathered, ids, prod, left_acc, right_acc)
    place_outputs(n_tensor, left_acc, right_acc, stage)
    out[...] = stage[...].astype(BF16)


def sum_kernel(sizes, pairs, n_dp, *refs):
    groups = []
    for size in sizes:
        groups, refs = groups + [refs[:size]], refs[size:]
    n_tensor = len(groups)
    grad, accs = refs[0], refs[1:]
    share, width = grad.shape
    side = groups[0][0].shape[1] // 2
    tiles = slot_tiles(n_dp, pairs)
    end = len(tiles) * share

    def load(group, start, stop):
        value = group[0][start:stop, :].astype(F32)
        for message in group[1:]:
            value = value + message[start:stop, :].astype(F32)
        return value

    places = [load(group, end, end + 2 * n_dp)[:n_dp].astype(I32) for group in groups]
    for acc in accs:
        acc[...] = jnp.zeros_like(acc)
    low = low_half((share, 2 * side))
    for t in range(0, len(tiles), 2):
        both = [load(group, t * share, (t + 2) * share) for group in groups]
        for u in range(2):
            values = [two[u * share:(u + 1) * share] for two in both]
            for h, (i, j) in enumerate(tiles[t + u]):
                rows = [place[i, side + j] for place in places]
                halves = [jnp.where(low, 0.0, value) if h else jnp.where(low, value, 0.0) for value in values]
                sums = [acc[row] + half for acc, row, half in zip(accs, rows, halves)]
                for acc, row, value in zip(accs, rows, sums):
                    acc[row] = value

    def total(r):
        value = accs[0][r]
        for acc in accs[1:]:
            value = value + acc[r]
        return fold(value)

    for r in range(0, width // side, 2):
        grad[:, r * side:(r + 2) * side] = jnp.where(low, total(r), total(r + 1)).astype(BF16)


def steps(n):
    return [n >> i for i in range(1, n.bit_length())]


def peer_order(n):
    order = [0]
    for k in steps(n):
        order = order + [i ^ k for i in order]
    return order


def swap(value, axis, n, k):
    return lax.ppermute(value, axis, [(i, i ^ k) for i in range(n)])


def shift(value, axis, n, k):
    return lax.ppermute(value, axis, [(i, (i + k) % n) for i in range(n)])


def gather_all(packed, inputs, n_dp, n_tensor):
    if (n_dp, n_tensor) != (8, 4):
        tokens = [inputs[None]]
        for k in steps(n_tensor):
            tokens = tokens + [swap(value, "tensor", n_tensor, k) for value in tokens]
        return [lax.all_gather(packed, "dp", axis=0, tiled=True)], tokens
    far_tokens = swap(inputs, "tensor", n_tensor, 2)
    near, second, last = [swap(packed, "dp", n_dp, k) for k in (6, 2, 4)]
    joined, tokens = pl.pallas_call(
        join_kernel,
        out_shape=[
            pltpu.VMEM((2, *packed.shape[1:]), packed.dtype),
            pltpu.VMEM((2, *inputs.shape), inputs.dtype),
        ],
        in_specs=[VMEM] * 4,
        out_specs=[VMEM] * 2,
        compiler_params=pltpu.CompilerParams(vmem_limit_bytes=4 * MIB),
    )(packed, near, inputs, far_tokens)
    same_core = [joined, second, last]
    parts = same_core + [swap(part, "dp", n_dp, 1) for part in same_core]
    return parts, [tokens, swap(tokens, "tensor", n_tensor, 1)]


def on_device(n_dp, n_tensor, inputs, block_values, block_slot, grad_out):
    share, width = inputs.shape
    rows, hidden = grad_out.shape
    _, count, side, _ = block_values.shape
    row_count, col_count = width // side, hidden // side
    pairs = count // 2 + 1
    small = (n_dp, n_tensor) == (8, 4)
    per_slot = small and n_dp * count < row_count and count == 2 * pairs - 1
    params = pltpu.CompilerParams(vmem_limit_bytes=(12 if small else 48) * MIB)

    packed = pl.pallas_call(
        functools.partial(pack_kernel, count, row_count, col_count),
        out_shape=pltpu.VMEM((1, pairs, side, 2 * side), BF16),
        in_specs=[HBM, HBM],
        out_specs=VMEM,
        scratch_shapes=[
            pltpu.VMEM(block_slot.shape, I32),
            pltpu.VMEM(block_values.shape, BF16),
            pltpu.SemaphoreType.DMA((count + 1,)),
        ],
        compiler_params=pltpu.CompilerParams(vmem_limit_bytes=4 * MIB),
    )(
        pltpu.with_memory_space_constraint(block_slot, pltpu.HBM),
        pltpu.with_memory_space_constraint(block_values, pltpu.HBM),
    )
    gathered, tokens = gather_all(packed, inputs, n_dp, n_tensor)
    n_parts = len(gathered)
    ids = [pltpu.VMEM((2, n_dp, 2 * side), I32), pltpu.SMEM((2, n_dp, 2 * side), I32)]
    cots = (col_count + 1, rows, 2 * side)
    if per_slot:
        half, tiles = n_parts // 2, len(slot_tiles(n_dp, pairs)) // 2
        scratch = [
            pltpu.VMEM((tiles, rows, 2 * side), F32),
            pltpu.VMEM((tiles, 2 * side, 2 * side), BF16),
        ]
        *first_slots, cotangent = pl.pallas_call(
            functools.partial(slots_kernel, True, half, n_tensor),
            out_shape=[pltpu.VMEM((tiles * share, 2 * side), BF16)] * n_tensor + [pltpu.VMEM(cots, BF16)],
            in_specs=[VMEM] * (half + 1),
            out_specs=[VMEM] * (n_tensor + 1),
            scratch_shapes=scratch,
            compiler_params=params,
        )(*gathered[:half], grad_out)
        partial_sums = pl.pallas_call(
            functools.partial(slots_kernel, False, n_parts, n_tensor),
            out_shape=[pltpu.VMEM((2 * tiles * share + 2 * n_dp, 2 * side), BF16)] * n_tensor,
            in_specs=[VMEM] * (n_parts + 1 + n_tensor),
            out_specs=[VMEM] * n_tensor,
            scratch_shapes=scratch,
            compiler_params=params,
        )(*gathered, cotangent, *first_slots)
        groups = [[partial_sums[0]]] + [[shift(partial_sums[k], "tensor", n_tensor, k)] for k in (2, 1, 3)]
    else:
        partial_sums = pl.pallas_call(
            functools.partial(rows_kernel, count, n_parts, n_tensor),
            out_shape=[jax.ShapeDtypeStruct((share, width), BF16)] * n_tensor,
            in_specs=[VMEM] * (n_parts + 1),
            out_specs=[VMEM] * n_tensor,
            scratch_shapes=ids + [
                pltpu.VMEM(cots, BF16),
                pltpu.VMEM((row_count + 1, rows, 2 * side), F32),
                pltpu.SemaphoreType.DMA,
            ],
            compiler_params=params,
        )(*gathered, grad_out)
        arrived = [partial_sums[0]] + [shift(partial_sums[k], "tensor", n_tensor, k) for k in range(1, n_tensor)]
    outputs = pl.pallas_call(
        functools.partial(forward_kernel, count, per_slot, n_parts, len(tokens), n_tensor),
        out_shape=jax.ShapeDtypeStruct((rows, hidden), BF16),
        in_specs=[VMEM] * (n_parts + len(tokens)),
        out_specs=VMEM,
        scratch_shapes=[
            pltpu.VMEM((row_count + 1, rows, 2 * side), BF16),
            pltpu.VMEM((n_dp * pairs, rows, 2 * side), F32),
            pltpu.VMEM((col_count + 1, rows, 2 * side), F32),
            pltpu.VMEM((col_count + 1, rows, 2 * side), F32),
            pltpu.VMEM((rows, hidden), F32),
        ] + ([] if per_slot else ids + [pltpu.SemaphoreType.DMA]),
        compiler_params=params,
    )(*gathered, *tokens)
    if per_slot:
        grad_in = pl.pallas_call(
            functools.partial(sum_kernel, tuple(map(len, groups)), pairs, n_dp),
            out_shape=jax.ShapeDtypeStruct((share, width), BF16),
            in_specs=[VMEM] * sum(map(len, groups)),
            out_specs=VMEM,
            scratch_shapes=[pltpu.VMEM((row_count + 1, share, 2 * side), F32)] * n_tensor,
            compiler_params=params,
        )(*(message for group in groups for message in group))
        return (outputs, grad_in)
    total = arrived[0].astype(F32)
    for value in arrived[1:]:
        total = total + value.astype(F32)
    return (outputs, total.astype(BF16))


def solution(mesh):
    placed = (
        P(("dp", "tensor"), None),
        P("tensor", "dp", None, None),
        P("tensor", "dp"),
        P("dp", "tensor"),
    )
    return jax.shard_map(
        functools.partial(on_device, mesh.shape["dp"], mesh.shape["tensor"]),
        mesh=mesh,
        in_specs=placed,
        out_specs=(P("dp", "tensor"), P(("dp", "tensor"), None)),
        check_vma=False,
    )
```

```python
import functools

import jax
import jax.numpy as jnp
from jax import lax
from jax.experimental import pallas as pl
from jax.experimental.pallas import tpu as pltpu
from jax.sharding import PartitionSpec as P

VMEM = pl.BlockSpec(memory_space=pltpu.VMEM)
HBM = pl.BlockSpec(memory_space=pltpu.HBM)
MIB = 1024 * 1024
BF16, F32, I32 = jnp.bfloat16, jnp.float32, jnp.int32


def pack_kernel(count, row_count, col_count, slots_hbm, values_hbm, packed, slots, values, sems):
    copies = [pltpu.make_async_copy(slots_hbm, slots, sems.at[count])]
    copies += [pltpu.make_async_copy(values_hbm.at[0, j], values.at[0, j], sems.at[j]) for j in range(count)]
    for copy in copies:
        copy.start()
    side = values.shape[2]
    pairs = packed.shape[1]
    copies[0].wait()
    position = jnp.concatenate([slots[...], jnp.full((1, side - count), -1, I32)], axis=1)
    exact = position.astype(F32)
    row = jnp.floor((exact + 0.5) * (1.0 / col_count))
    col = exact - row * col_count
    row = jnp.where(position >= 0, row, float(row_count))
    col = jnp.where(position >= 0, col, float(col_count))
    head = jnp.concatenate([row, col, jnp.zeros((side - 2, side), F32)], axis=0).astype(BF16)
    for copy in copies[1:]:
        copy.wait()
    for k in range(pairs):
        left = values[0, k]
        right = values[0, k + pairs] if k + pairs < count else head
        packed[0, k] = jnp.concatenate([left, right], axis=1)


def join_kernel(own, near, tokens, far_tokens, joined, joined_tokens):
    joined[0], joined[1] = own[0], near[0]
    joined_tokens[0], joined_tokens[1] = tokens[...], far_tokens[...]


def load_ids(gathered, ids_vmem, ids, sem):
    i = 0
    for part in gathered:
        n, pairs = part.shape[:2]
        for d in range(n):
            head = part[d, pairs - 1, 0:16, :].astype(F32).astype(I32)
            ids_vmem[0, i:i + 1, :] = head[0:1]
            ids_vmem[1, i:i + 1, :] = head[1:2]
            i += 1
    copy = pltpu.make_async_copy(ids_vmem, ids, sem)
    copy.start()
    return copy


def over(gathered, body):
    start = 0
    for part in gathered:
        n = part.shape[0]
        if n <= 8:
            for d in range(n):
                body(part, d, start + d)
        else:
            def step(d, carry, part=part, start=start):
                body(part, d, start + d)
                return carry
            lax.fori_loop(0, n, step, 0)
        start += n


def low_half(shape):
    return lax.broadcasted_iota(I32, shape, 1) < shape[1] // 2


def swap_halves(x):
    half = x.shape[1] // 2
    return jnp.concatenate([x[:, half:], x[:, :half]], axis=1)


def twice(x):
    low, y = low_half(x.shape), swap_halves(x)
    return jnp.where(low, x, y), jnp.where(low, y, x)


def diagonal(tile, other=None):
    low = low_half(tile.shape)
    zero = jnp.zeros_like(tile)
    top = jnp.where(low, tile, zero)
    bottom = jnp.where(low, zero, tile if other is None else swap_halves(other))
    return jnp.concatenate([top, bottom], axis=0)


def fold(x):
    return x + pltpu.roll(x, x.shape[1] // 2, 1)


def across(lhs, rhs):
    return lax.dot_general(lhs, rhs, (((1,), (1,)), ((), ())), preferred_element_type=F32)


def load_cotangent(cot, cots):
    col_count = cots.shape[0] - 1
    for c in range(0, col_count, 2):
        width = cots.shape[2]
        cots[c], cots[c + 1] = twice(cot[:, c * width // 2:(c + 2) * width // 2])
    cots[col_count] = jnp.zeros_like(cots[col_count])


def slots_kernel(first, n_parts, n_tensor, *refs):
    gathered, refs = refs[:n_parts], refs[n_parts:]
    if first:
        cot, (*outs, cots), (prod, blocks) = refs[0], refs[1:n_tensor + 2], refs[n_tensor + 2:]
        before = []
    else:
        cots, before, outs = refs[0], refs[1:n_tensor + 1], refs[n_tensor + 1:2 * n_tensor + 1]
        prod, blocks = refs[2 * n_tensor + 1:]
    pairs, side = gathered[0].shape[1:3]
    rows = cots.shape[1]
    share = rows // n_tensor
    if first:
        load_cotangent(cot, cots)
    low = low_half((rows, 2 * side))
    where = [(part, d) for part in gathered for d in range(part.shape[0])]
    heads = [part[d, pairs - 1, 0:16, :].astype(F32) for part, d in where]
    columns = [head.astype(I32) for head in heads]
    tiles = slot_tiles(len(where), pairs)[-prod.shape[0]:]
    for t, ((i, j), (m, l)) in enumerate(tiles):
        part, d = where[i]
        other, e = where[m]
        blocks[t] = diagonal(part[d, j]) if i == m else diagonal(part[d, j], other[e, l])
    for t, ((i, j), (m, l)) in enumerate(tiles):
        lhs = jnp.where(low, cots[columns[i][1, side + j]], cots[columns[m][1, side + l]])
        prod[t] = across(lhs, blocks[t])
    me = lax.axis_index("tensor")
    begin = 0
    if not first:
        begin = before[0].shape[0]
        rows_of_slots = jnp.concatenate([head[0:1] for head in heads] * 2, axis=0).astype(BF16)
        for k in range(n_tensor):
            outs[k][:begin, :] = before[k][...]
            outs[k][begin + len(tiles) * share:, :] = rows_of_slots
    for k in range(n_tensor):
        start = pl.multiple_of(lax.rem(me + k, n_tensor) * share, share)
        for t in range(0, len(tiles), 2):
            two = [prod[t, pl.ds(start, share), :], prod[t + 1, pl.ds(start, share), :]]
            here = slice(begin + t * share, begin + (t + 2) * share)
            outs[k][here, :] = jnp.concatenate(two, axis=0).astype(BF16)


def slot_tiles(n, pairs):
    tiles = []
    for i in range(0, n, 4):
        tiles += [((m, j), (m, j + pairs)) for m in range(i, i + 4) for j in range(pairs - 1)]
        tiles += [((m, pairs - 1), (m + 1, pairs - 1)) for m in range(i, i + 4, 2)]
    return tiles


def rows_kernel(count, n_parts, n_tensor, *refs):
    gathered, cot, outs = refs[:n_parts], refs[n_parts], refs[n_parts + 1:n_parts + 1 + n_tensor]
    ids_vmem, ids, cots, acc, sem = refs[n_parts + 1 + n_tensor:]
    pairs, side = gathered[0].shape[1:3]
    row_count = acc.shape[0] - 1
    rows = cot.shape[0]
    copy = load_ids(gathered, ids_vmem, ids, sem)
    acc[...] = jnp.zeros_like(acc)
    load_cotangent(cot, cots)
    low = low_half((rows, 2 * side))
    copy.wait()

    def add(part, d, i):
        for k in range(pairs):
            left, right = ids[1, i, side + k], ids[1, i, side + k + pairs]
            lhs = cots[left]
            if k + pairs >= count:
                prod = across(lhs[:, :side], part[d, k][:, :side])
                acc[ids[0, i, side + k], :, :side] += prod
            else:
                prod = across(jnp.where(low, lhs, cots[right]), diagonal(part[d, k]))
                acc[ids[0, i, side + k]] += jnp.where(low, prod, 0.0)
                acc[ids[0, i, side + k + pairs]] += jnp.where(low, 0.0, prod)

    over(gathered, add)
    me = lax.axis_index("tensor")
    share = rows // n_tensor
    for k in range(n_tensor):
        start = pl.multiple_of(lax.rem(me + k, n_tensor) * share, share)
        half = low_half((share, 2 * side))
        for r in range(0, row_count, 2):
            pair = [fold(acc[r + u, pl.ds(start, share), :]) for u in range(2)]
            outs[k][:, r * side:(r + 2) * side] = jnp.where(half, *pair).astype(BF16)


def load_tokens(token_parts, blocks):
    tokens = [part.at[i] for part in token_parts for i in range(part.shape[0])]
    row_count, width = blocks.shape[0] - 1, blocks.shape[2]
    for r in range(0, row_count, 2):
        parts = [value[:, r * width // 2:(r + 2) * width // 2].astype(F32) for value in tokens]
        blocks[r], blocks[r + 1] = twice(jnp.concatenate(parts, axis=0).astype(BF16))
    blocks[row_count] = jnp.zeros_like(blocks[row_count])


def multiply_tokens(count, gathered, ids, blocks, prod):
    pairs, side = gathered[0].shape[1:3]
    low = low_half(blocks.shape[1:])

    def multiply(part, d, i):
        for k in range(pairs):
            lhs = blocks[ids(0, i, side + k)]
            if k + pairs < count:
                lhs = jnp.where(low, lhs, blocks[ids(0, i, side + k + pairs)])
                tile = diagonal(part[d, k])
            else:
                lhs, tile = lhs[:, :side], part[d, k]
            prod[i * pairs + k] = jnp.dot(lhs, tile, preferred_element_type=F32)

    over(gathered, multiply)


def add_tokens(count, gathered, ids, prod, left_acc, right_acc):
    pairs, side = gathered[0].shape[1:3]

    def add(part, d, i):
        for k in range(pairs):
            value, left = prod[i * pairs + k], ids(1, i, side + k)
            left_sum = left_acc[left] + value
            if k + pairs < count:
                right = ids(1, i, side + k + pairs)
                right_sum = right_acc[right] + value
                right_acc[right] = right_sum
            left_acc[left] = left_sum

    over(gathered, add)


def place_outputs(n_tensor, left_acc, right_acc, stage):
    col_count, rows, width = left_acc.shape[0] - 1, left_acc.shape[1], left_acc.shape[2]
    share = rows // n_tensor
    me = lax.axis_index("tensor")
    half = low_half((share, width))
    for i, k in enumerate(peer_order(n_tensor)):
        start = pl.multiple_of(lax.bitwise_xor(me, k) * share, share)
        mine = slice(i * share, (i + 1) * share)
        for c in range(0, col_count, 2):
            sums = [fold(jnp.where(half, left_acc[c + u, mine, :], right_acc[c + u, mine, :])) for u in range(2)]
            stage[pl.ds(start, share), c * width // 2:(c + 2) * width // 2] = jnp.where(half, *sums)


def forward_kernel(count, few, n_parts, n_token_parts, n_tensor, *refs):
    gathered, token_parts = refs[:n_parts], refs[n_parts:n_parts + n_token_parts]
    out, blocks, prod, left_acc, right_acc, stage = refs[n_parts + n_token_parts:][:6]
    if few:
        heads = [part[d, part.shape[1] - 1, 0:16, :].astype(F32) for part in gathered for d in range(part.shape[0])]
        heads = [head.astype(I32) for head in heads]
        ids = lambda line, i, lane: heads[i][line, lane]
    else:
        ids_vmem, scalars, sem = refs[-3:]
        copy = load_ids(gathered, ids_vmem, scalars, sem)
        ids = lambda line, i, lane: scalars[line, i, lane]
    left_acc[...] = jnp.zeros_like(left_acc)
    right_acc[...] = jnp.zeros_like(right_acc)
    load_tokens(token_parts, blocks)
    if not few:
        copy.wait()
    multiply_tokens(count, gathered, ids, blocks, prod)
    add_tokens(count, gathered, ids, prod, left_acc, right_acc)
    place_outputs(n_tensor, left_acc, right_acc, stage)
    out[...] = stage[...].astype(BF16)


def sum_kernel(sizes, pairs, n_dp, *refs):
    groups = []
    for size in sizes:
        groups, refs = groups + [refs[:size]], refs[size:]
    n_tensor = len(groups)
    before, grad, accs = refs[:-1 - n_tensor], refs[-1 - n_tensor], refs[-n_tensor:]
    share, width = grad.shape
    side = groups[0][0].shape[1] // 2
    tiles = slot_tiles(n_dp, pairs)
    end = len(tiles) * share

    def load(group, start, stop):
        value = group[0][start:stop, :].astype(F32)
        for message in group[1:]:
            value = value + message[start:stop, :].astype(F32)
        return value

    places = [load(group, end, end + 2 * n_dp)[:n_dp].astype(I32) for group in groups]
    for acc in accs:
        acc[...] = jnp.zeros_like(acc)
    low = low_half((share, 2 * side))
    for t in range(0, len(tiles), 2):
        both = [load(group, t * share, (t + 2) * share) for group in groups]
        for u in range(2):
            values = [two[u * share:(u + 1) * share] for two in both]
            for h, (i, j) in enumerate(tiles[t + u]):
                rows = [place[i, side + j] for place in places]
                halves = [jnp.where(low, 0.0, value) if h else jnp.where(low, value, 0.0) for value in values]
                sums = [acc[row] + half for acc, row, half in zip(accs, rows, halves)]
                for acc, row, value in zip(accs, rows, sums):
                    acc[row] = value

    def total(r):
        value = accs[0][r]
        for acc in accs[1:]:
            value = value + acc[r]
        return fold(value)

    for r in range(0, width // side, 2):
        value = jnp.where(low, total(r), total(r + 1))
        for earlier in before:
            value = value + earlier[:, r * side:(r + 2) * side]
        grad[:, r * side:(r + 2) * side] = value.astype(grad.dtype)


def steps(n):
    return [n >> i for i in range(1, n.bit_length())]


def peer_order(n):
    order = [0]
    for k in steps(n):
        order = order + [i ^ k for i in order]
    return order


def swap(value, axis, n, k):
    return lax.ppermute(value, axis, [(i, i ^ k) for i in range(n)])


def shift(value, axis, n, k):
    return lax.ppermute(value, axis, [(i, (i + k) % n) for i in range(n)])


def gather_all(packed, inputs, n_dp, n_tensor):
    if (n_dp, n_tensor) != (8, 4):
        tokens = [inputs[None]]
        for k in steps(n_tensor):
            tokens = tokens + [swap(value, "tensor", n_tensor, k) for value in tokens]
        return [lax.all_gather(packed, "dp", axis=0, tiled=True)], tokens
    far_tokens = swap(inputs, "tensor", n_tensor, 2)
    near, second, last = [swap(packed, "dp", n_dp, k) for k in (6, 2, 4)]
    joined, tokens = pl.pallas_call(
        join_kernel,
        out_shape=[
            pltpu.VMEM((2, *packed.shape[1:]), packed.dtype),
            pltpu.VMEM((2, *inputs.shape), inputs.dtype),
        ],
        in_specs=[VMEM] * 4,
        out_specs=[VMEM] * 2,
        compiler_params=pltpu.CompilerParams(vmem_limit_bytes=4 * MIB),
    )(packed, near, inputs, far_tokens)
    same_core = [joined, second, last]
    parts = same_core + [swap(part, "dp", n_dp, 1) for part in same_core]
    return parts, [tokens, swap(tokens, "tensor", n_tensor, 1)]


def on_device(n_dp, n_tensor, inputs, block_values, block_slot, grad_out):
    share, width = inputs.shape
    rows, hidden = grad_out.shape
    _, count, side, _ = block_values.shape
    row_count, col_count = width // side, hidden // side
    pairs = count // 2 + 1
    small = (n_dp, n_tensor) == (8, 4)
    per_slot = small and n_dp * count < row_count and count == 2 * pairs - 1
    params = pltpu.CompilerParams(vmem_limit_bytes=(12 if small else 48) * MIB)

    packed = pl.pallas_call(
        functools.partial(pack_kernel, count, row_count, col_count),
        out_shape=pltpu.VMEM((1, pairs, side, 2 * side), BF16),
        in_specs=[HBM, HBM],
        out_specs=VMEM,
        scratch_shapes=[
            pltpu.VMEM(block_slot.shape, I32),
            pltpu.VMEM(block_values.shape, BF16),
            pltpu.SemaphoreType.DMA((count + 1,)),
        ],
        compiler_params=pltpu.CompilerParams(vmem_limit_bytes=4 * MIB),
    )(
        pltpu.with_memory_space_constraint(block_slot, pltpu.HBM),
        pltpu.with_memory_space_constraint(block_values, pltpu.HBM),
    )
    gathered, tokens = gather_all(packed, inputs, n_dp, n_tensor)
    n_parts = len(gathered)
    ids = [pltpu.VMEM((2, n_dp, 2 * side), I32), pltpu.SMEM((2, n_dp, 2 * side), I32)]
    cots = (col_count + 1, rows, 2 * side)
    if per_slot:
        half, tiles = n_parts // 2, len(slot_tiles(n_dp, pairs)) // 2
        scratch = [
            pltpu.VMEM((tiles, rows, 2 * side), F32),
            pltpu.VMEM((tiles, 2 * side, 2 * side), BF16),
        ]
        *first_slots, cotangent = pl.pallas_call(
            functools.partial(slots_kernel, True, half, n_tensor),
            out_shape=[pltpu.VMEM((tiles * share, 2 * side), BF16)] * n_tensor + [pltpu.VMEM(cots, BF16)],
            in_specs=[VMEM] * (half + 1),
            out_specs=[VMEM] * (n_tensor + 1),
            scratch_shapes=scratch,
            compiler_params=params,
        )(*gathered[:half], grad_out)
        partial_sums = pl.pallas_call(
            functools.partial(slots_kernel, False, n_parts, n_tensor),
            out_shape=[pltpu.VMEM((2 * tiles * share + 2 * n_dp, 2 * side), BF16)] * n_tensor,
            in_specs=[VMEM] * (n_parts + 1 + n_tensor),
            out_specs=[VMEM] * n_tensor,
            scratch_shapes=scratch,
            compiler_params=params,
        )(*gathered, cotangent, *first_slots)
        groups = [[partial_sums[0]]] + [[shift(partial_sums[k], "tensor", n_tensor, k)] for k in (2, 1, 3)]
    else:
        partial_sums = pl.pallas_call(
            functools.partial(rows_kernel, count, n_parts, n_tensor),
            out_shape=[jax.ShapeDtypeStruct((share, width), BF16)] * n_tensor,
            in_specs=[VMEM] * (n_parts + 1),
            out_specs=[VMEM] * n_tensor,
            scratch_shapes=ids + [
                pltpu.VMEM(cots, BF16),
                pltpu.VMEM((row_count + 1, rows, 2 * side), F32),
                pltpu.SemaphoreType.DMA,
            ],
            compiler_params=params,
        )(*gathered, grad_out)
        arrived = [partial_sums[0]] + [shift(partial_sums[k], "tensor", n_tensor, k) for k in range(1, n_tensor)]
    outputs = pl.pallas_call(
        functools.partial(forward_kernel, count, per_slot, n_parts, len(tokens), n_tensor),
        out_shape=jax.ShapeDtypeStruct((rows, hidden), BF16),
        in_specs=[VMEM] * (n_parts + len(tokens)),
        out_specs=VMEM,
        scratch_shapes=[
            pltpu.VMEM((row_count + 1, rows, 2 * side), BF16),
            pltpu.VMEM((n_dp * pairs, rows, 2 * side), F32),
            pltpu.VMEM((col_count + 1, rows, 2 * side), F32),
            pltpu.VMEM((col_count + 1, rows, 2 * side), F32),
            pltpu.VMEM((rows, hidden), F32),
        ] + ([] if per_slot else ids + [pltpu.SemaphoreType.DMA]),
        compiler_params=params,
    )(*gathered, *tokens)
    if per_slot:
        def add(groups, before, dtype):
            return pl.pallas_call(
                functools.partial(sum_kernel, tuple(map(len, groups)), pairs, n_dp),
                out_shape=jax.ShapeDtypeStruct((share, width), dtype),
                in_specs=[VMEM] * (sum(map(len, groups)) + len(before)),
                out_specs=VMEM,
                scratch_shapes=[pltpu.VMEM((row_count + 1, share, 2 * side), F32)] * len(groups),
                compiler_params=params,
            )(*(message for group in groups for message in group), *before)

        grad_in = add(groups[1:], [add(groups[:1], [], F32)], BF16)
        return (outputs, grad_in)
    total = arrived[0].astype(F32)
    for value in arrived[1:]:
        total = total + value.astype(F32)
    return (outputs, total.astype(BF16))


def solution(mesh):
    placed = (
        P(("dp", "tensor"), None),
        P("tensor", "dp", None, None),
        P("tensor", "dp"),
        P("dp", "tensor"),
    )
    return jax.shard_map(
        functools.partial(on_device, mesh.shape["dp"], mesh.shape["tensor"]),
        mesh=mesh,
        in_specs=placed,
        out_specs=(P("dp", "tensor"), P(("dp", "tensor"), None)),
        check_vma=False,
    )
```

```python
import functools

import jax
import jax.numpy as jnp
from jax import lax
from jax.experimental import pallas as pl
from jax.experimental.pallas import tpu as pltpu
from jax.sharding import PartitionSpec as P

VMEM = pl.BlockSpec(memory_space=pltpu.VMEM)
HBM = pl.BlockSpec(memory_space=pltpu.HBM)
MIB = 1024 * 1024
BF16, F32, I32 = jnp.bfloat16, jnp.float32, jnp.int32


def pack_kernel(count, row_count, col_count, slots_hbm, values_hbm, packed, slots, values, sems):
    copies = [pltpu.make_async_copy(slots_hbm, slots, sems.at[count])]
    copies += [pltpu.make_async_copy(values_hbm.at[0, j], values.at[0, j], sems.at[j]) for j in range(count)]
    for copy in copies:
        copy.start()
    side = values.shape[2]
    pairs = packed.shape[1]
    copies[0].wait()
    position = jnp.concatenate([slots[...], jnp.full((1, side - count), -1, I32)], axis=1)
    exact = position.astype(F32)
    row = jnp.floor((exact + 0.5) * (1.0 / col_count))
    col = exact - row * col_count
    row = jnp.where(position >= 0, row, float(row_count))
    col = jnp.where(position >= 0, col, float(col_count))
    head = jnp.concatenate([row, col, jnp.zeros((side - 2, side), F32)], axis=0).astype(BF16)
    for copy in copies[1:]:
        copy.wait()
    for k in range(pairs):
        left = values[0, k]
        right = values[0, k + pairs] if k + pairs < count else head
        packed[0, k] = jnp.concatenate([left, right], axis=1)


def join_kernel(own, near, tokens, far_tokens, joined, joined_tokens):
    joined[0], joined[1] = own[0], near[0]
    joined_tokens[0], joined_tokens[1] = tokens[...], far_tokens[...]


def load_ids(gathered, ids_vmem, ids, sem):
    i = 0
    for part in gathered:
        n, pairs = part.shape[:2]
        for d in range(n):
            head = part[d, pairs - 1, 0:16, :].astype(F32).astype(I32)
            ids_vmem[0, i:i + 1, :] = head[0:1]
            ids_vmem[1, i:i + 1, :] = head[1:2]
            i += 1
    copy = pltpu.make_async_copy(ids_vmem, ids, sem)
    copy.start()
    return copy


def over(gathered, body):
    start = 0
    for part in gathered:
        n = part.shape[0]
        if n <= 8:
            for d in range(n):
                body(part, d, start + d)
        else:
            def step(d, carry, part=part, start=start):
                body(part, d, start + d)
                return carry
            lax.fori_loop(0, n, step, 0)
        start += n


def low_half(shape):
    return lax.broadcasted_iota(I32, shape, 1) < shape[1] // 2


def swap_halves(x):
    half = x.shape[1] // 2
    return jnp.concatenate([x[:, half:], x[:, :half]], axis=1)


def twice(x):
    low, y = low_half(x.shape), swap_halves(x)
    return jnp.where(low, x, y), jnp.where(low, y, x)


def diagonal(tile, other=None):
    low = low_half(tile.shape)
    zero = jnp.zeros_like(tile)
    top = jnp.where(low, tile, zero)
    bottom = jnp.where(low, zero, tile if other is None else swap_halves(other))
    return jnp.concatenate([top, bottom], axis=0)


def fold(x):
    return x + pltpu.roll(x, x.shape[1] // 2, 1)


def across(lhs, rhs):
    return lax.dot_general(lhs, rhs, (((1,), (1,)), ((), ())), preferred_element_type=F32)


def load_cotangent(cot, cots):
    col_count = cots.shape[0] - 1
    for c in range(0, col_count, 2):
        width = cots.shape[2]
        cots[c], cots[c + 1] = twice(cot[:, c * width // 2:(c + 2) * width // 2])
    cots[col_count] = jnp.zeros_like(cots[col_count])


def slots_kernel(first, n_parts, n_tensor, *refs):
    gathered, refs = refs[:n_parts], refs[n_parts:]
    if first:
        cot, (*outs, cots), (prod, blocks) = refs[0], refs[1:n_tensor + 2], refs[n_tensor + 2:]
        before = []
    else:
        cots, before, outs = refs[0], refs[1:n_tensor + 1], refs[n_tensor + 1:2 * n_tensor + 1]
        prod, blocks = refs[2 * n_tensor + 1:]
    pairs, side = gathered[0].shape[1:3]
    rows = cots.shape[1]
    share = rows // n_tensor
    if first:
        load_cotangent(cot, cots)
    low = low_half((rows, 2 * side))
    where = [(part, d) for part in gathered for d in range(part.shape[0])]
    heads = [part[d, pairs - 1, 0:16, :].astype(F32) for part, d in where]
    columns = [head.astype(I32) for head in heads]
    tiles = slot_tiles(len(where), pairs)[-prod.shape[0]:]
    for t, ((i, j), (m, l)) in enumerate(tiles):
        part, d = where[i]
        other, e = where[m]
        blocks[t] = diagonal(part[d, j]) if i == m else diagonal(part[d, j], other[e, l])
    for t, ((i, j), (m, l)) in enumerate(tiles):
        lhs = jnp.where(low, cots[columns[i][1, side + j]], cots[columns[m][1, side + l]])
        prod[t] = across(lhs, blocks[t])
    me = lax.axis_index("tensor")
    begin = 0
    if not first:
        begin = before[0].shape[0]
        rows_of_slots = jnp.concatenate([head[0:1] for head in heads] * 2, axis=0).astype(BF16)
        for k in range(n_tensor):
            outs[k][:begin, :] = before[k][...]
            outs[k][begin + len(tiles) * share:, :] = rows_of_slots
    for k in range(n_tensor):
        start = pl.multiple_of(lax.rem(me + k, n_tensor) * share, share)
        for t in range(0, len(tiles), 2):
            two = [prod[t, pl.ds(start, share), :], prod[t + 1, pl.ds(start, share), :]]
            here = slice(begin + t * share, begin + (t + 2) * share)
            outs[k][here, :] = jnp.concatenate(two, axis=0).astype(BF16)


def slot_tiles(n, pairs):
    tiles = []
    for i in range(0, n, 4):
        tiles += [((m, j), (m, j + pairs)) for m in range(i, i + 4) for j in range(pairs - 1)]
        tiles += [((m, pairs - 1), (m + 1, pairs - 1)) for m in range(i, i + 4, 2)]
    return tiles


def rows_kernel(count, n_parts, n_tensor, *refs):
    gathered, cot, outs = refs[:n_parts], refs[n_parts], refs[n_parts + 1:n_parts + 1 + n_tensor]
    ids_vmem, ids, cots, acc, sem = refs[n_parts + 1 + n_tensor:]
    pairs, side = gathered[0].shape[1:3]
    row_count = acc.shape[0] - 1
    rows = cot.shape[0]
    copy = load_ids(gathered, ids_vmem, ids, sem)
    acc[...] = jnp.zeros_like(acc)
    load_cotangent(cot, cots)
    low = low_half((rows, 2 * side))
    copy.wait()

    def add(part, d, i):
        for k in range(pairs):
            left, right = ids[1, i, side + k], ids[1, i, side + k + pairs]
            lhs = cots[left]
            if k + pairs >= count:
                prod = across(lhs[:, :side], part[d, k][:, :side])
                acc[ids[0, i, side + k], :, :side] += prod
            else:
                prod = across(jnp.where(low, lhs, cots[right]), diagonal(part[d, k]))
                acc[ids[0, i, side + k]] += jnp.where(low, prod, 0.0)
                acc[ids[0, i, side + k + pairs]] += jnp.where(low, 0.0, prod)

    over(gathered, add)
    me = lax.axis_index("tensor")
    share = rows // n_tensor
    for k in range(n_tensor):
        start = pl.multiple_of(lax.rem(me + k, n_tensor) * share, share)
        half = low_half((share, 2 * side))
        for r in range(0, row_count, 2):
            pair = [fold(acc[r + u, pl.ds(start, share), :]) for u in range(2)]
            outs[k][:, r * side:(r + 2) * side] = jnp.where(half, *pair).astype(BF16)


def load_tokens(token_parts, blocks):
    tokens = [part.at[i] for part in token_parts for i in range(part.shape[0])]
    row_count, width = blocks.shape[0] - 1, blocks.shape[2]
    for r in range(0, row_count, 2):
        parts = [value[:, r * width // 2:(r + 2) * width // 2].astype(F32) for value in tokens]
        blocks[r], blocks[r + 1] = twice(jnp.concatenate(parts, axis=0).astype(BF16))
    blocks[row_count] = jnp.zeros_like(blocks[row_count])


def multiply_tokens(count, gathered, ids, blocks, prod):
    pairs, side = gathered[0].shape[1:3]
    low = low_half(blocks.shape[1:])

    def multiply(part, d, i):
        for k in range(pairs):
            lhs = blocks[ids(0, i, side + k)]
            if k + pairs < count:
                lhs = jnp.where(low, lhs, blocks[ids(0, i, side + k + pairs)])
                tile = diagonal(part[d, k])
            else:
                lhs, tile = lhs[:, :side], part[d, k]
            prod[i * pairs + k] = jnp.dot(lhs, tile, preferred_element_type=F32)

    over(gathered, multiply)


def add_tokens(count, gathered, ids, prod, left_acc, right_acc):
    pairs, side = gathered[0].shape[1:3]

    def add(part, d, i):
        for k in range(pairs):
            value, left = prod[i * pairs + k], ids(1, i, side + k)
            left_sum = left_acc[left] + value
            if k + pairs < count:
                right = ids(1, i, side + k + pairs)
                right_sum = right_acc[right] + value
                right_acc[right] = right_sum
            left_acc[left] = left_sum

    over(gathered, add)


def place_outputs(n_tensor, left_acc, right_acc, stage):
    col_count, rows, width = left_acc.shape[0] - 1, left_acc.shape[1], left_acc.shape[2]
    share = rows // n_tensor
    me = lax.axis_index("tensor")
    half = low_half((share, width))
    for i, k in enumerate(peer_order(n_tensor)):
        start = pl.multiple_of(lax.bitwise_xor(me, k) * share, share)
        mine = slice(i * share, (i + 1) * share)
        for c in range(0, col_count, 2):
            sums = [fold(jnp.where(half, left_acc[c + u, mine, :], right_acc[c + u, mine, :])) for u in range(2)]
            stage[pl.ds(start, share), c * width // 2:(c + 2) * width // 2] = jnp.where(half, *sums)


def forward_kernel(count, few, n_parts, n_token_parts, n_tensor, *refs):
    gathered, token_parts = refs[:n_parts], refs[n_parts:n_parts + n_token_parts]
    out, blocks, prod, left_acc, right_acc, stage = refs[n_parts + n_token_parts:][:6]
    if few:
        heads = [part[d, part.shape[1] - 1, 0:16, :].astype(F32) for part in gathered for d in range(part.shape[0])]
        heads = [head.astype(I32) for head in heads]
        ids = lambda line, i, lane: heads[i][line, lane]
    else:
        ids_vmem, scalars, sem = refs[-3:]
        copy = load_ids(gathered, ids_vmem, scalars, sem)
        ids = lambda line, i, lane: scalars[line, i, lane]
    left_acc[...] = jnp.zeros_like(left_acc)
    right_acc[...] = jnp.zeros_like(right_acc)
    load_tokens(token_parts, blocks)
    if not few:
        copy.wait()
    multiply_tokens(count, gathered, ids, blocks, prod)
    add_tokens(count, gathered, ids, prod, left_acc, right_acc)
    place_outputs(n_tensor, left_acc, right_acc, stage)
    out[...] = stage[...].astype(BF16)


def sum_kernel(sizes, pairs, n_dp, *refs):
    groups = []
    for size in sizes:
        groups, refs = groups + [refs[:size]], refs[size:]
    n_tensor = len(groups)
    grad, accs = refs[0], refs[1:]
    share, width = grad.shape
    side = groups[0][0].shape[1] // 2
    tiles = slot_tiles(n_dp, pairs)
    end = len(tiles) * share

    def load(group, start, stop):
        value = group[0][start:stop, :].astype(F32)
        for message in group[1:]:
            value = value + message[start:stop, :].astype(F32)
        return value

    places = [load(group, end, end + 2 * n_dp)[:n_dp].astype(I32) for group in groups]
    for acc in accs:
        acc[...] = jnp.zeros_like(acc)
    low = low_half((share, 2 * side))
    for t in range(0, len(tiles), 2):
        both = [load(group, t * share, (t + 2) * share) for group in groups]
        for u in range(2):
            values = [two[u * share:(u + 1) * share] for two in both]
            for h, (i, j) in enumerate(tiles[t + u]):
                rows = [place[i, side + j] for place in places]
                halves = [jnp.where(low, 0.0, value) if h else jnp.where(low, value, 0.0) for value in values]
                sums = [acc[row] + half for acc, row, half in zip(accs, rows, halves)]
                for acc, row, value in zip(accs, rows, sums):
                    acc[row] = value

    def total(r):
        value = accs[0][r]
        for acc in accs[1:]:
            value = value + acc[r]
        return fold(value)

    for r in range(0, width // side, 2):
        grad[:, r * side:(r + 2) * side] = jnp.where(low, total(r), total(r + 1)).astype(BF16)


def steps(n):
    return [n >> i for i in range(1, n.bit_length())]


def peer_order(n):
    order = [0]
    for k in steps(n):
        order = order + [i ^ k for i in order]
    return order


def swap(value, axis, n, k):
    return lax.ppermute(value, axis, [(i, i ^ k) for i in range(n)])


def shift(value, axis, n, k):
    return lax.ppermute(value, axis, [(i, (i + k) % n) for i in range(n)])


def gather_all(packed, inputs, n_dp, n_tensor):
    if (n_dp, n_tensor) != (8, 4):
        tokens = [inputs[None]]
        for k in steps(n_tensor):
            tokens = tokens + [swap(value, "tensor", n_tensor, k) for value in tokens]
        return [lax.all_gather(packed, "dp", axis=0, tiled=True)], tokens
    far_tokens = swap(inputs, "tensor", n_tensor, 2)
    near, second, last = [swap(packed, "dp", n_dp, k) for k in (4, 2, 6)]
    joined, tokens = pl.pallas_call(
        join_kernel,
        out_shape=[
            pltpu.VMEM((2, *packed.shape[1:]), packed.dtype),
            pltpu.VMEM((2, *inputs.shape), inputs.dtype),
        ],
        in_specs=[VMEM] * 4,
        out_specs=[VMEM] * 2,
        compiler_params=pltpu.CompilerParams(vmem_limit_bytes=4 * MIB),
    )(packed, near, inputs, far_tokens)
    same_core = [joined, second, last]
    parts = same_core + [swap(part, "dp", n_dp, 1) for part in same_core]
    return parts, [tokens, swap(tokens, "tensor", n_tensor, 1)]


def on_device(n_dp, n_tensor, inputs, block_values, block_slot, grad_out):
    share, width = inputs.shape
    rows, hidden = grad_out.shape
    _, count, side, _ = block_values.shape
    row_count, col_count = width // side, hidden // side
    pairs = count // 2 + 1
    small = (n_dp, n_tensor) == (8, 4)
    per_slot = small and n_dp * count < row_count and count == 2 * pairs - 1
    params = pltpu.CompilerParams(vmem_limit_bytes=(12 if small else 48) * MIB)

    packed = pl.pallas_call(
        functools.partial(pack_kernel, count, row_count, col_count),
        out_shape=pltpu.VMEM((1, pairs, side, 2 * side), BF16),
        in_specs=[HBM, HBM],
        out_specs=VMEM,
        scratch_shapes=[
            pltpu.VMEM(block_slot.shape, I32),
            pltpu.VMEM(block_values.shape, BF16),
            pltpu.SemaphoreType.DMA((count + 1,)),
        ],
        compiler_params=pltpu.CompilerParams(vmem_limit_bytes=4 * MIB),
    )(
        pltpu.with_memory_space_constraint(block_slot, pltpu.HBM),
        pltpu.with_memory_space_constraint(block_values, pltpu.HBM),
    )
    gathered, tokens = gather_all(packed, inputs, n_dp, n_tensor)
    n_parts = len(gathered)
    ids = [pltpu.VMEM((2, n_dp, 2 * side), I32), pltpu.SMEM((2, n_dp, 2 * side), I32)]
    cots = (col_count + 1, rows, 2 * side)
    if per_slot:
        half, tiles = n_parts // 2, len(slot_tiles(n_dp, pairs)) // 2
        scratch = [
            pltpu.VMEM((tiles, rows, 2 * side), F32),
            pltpu.VMEM((tiles, 2 * side, 2 * side), BF16),
        ]
        *first_slots, cotangent = pl.pallas_call(
            functools.partial(slots_kernel, True, half, n_tensor),
            out_shape=[pltpu.VMEM((tiles * share, 2 * side), BF16)] * n_tensor + [pltpu.VMEM(cots, BF16)],
            in_specs=[VMEM] * (half + 1),
            out_specs=[VMEM] * (n_tensor + 1),
            scratch_shapes=scratch,
            compiler_params=params,
        )(*gathered[:half], grad_out)
        partial_sums = pl.pallas_call(
            functools.partial(slots_kernel, False, n_parts, n_tensor),
            out_shape=[pltpu.VMEM((2 * tiles * share + 2 * n_dp, 2 * side), BF16)] * n_tensor,
            in_specs=[VMEM] * (n_parts + 1 + n_tensor),
            out_specs=[VMEM] * n_tensor,
            scratch_shapes=scratch,
            compiler_params=params,
        )(*gathered, cotangent, *first_slots)
        groups = [[partial_sums[0]]] + [[shift(partial_sums[k], "tensor", n_tensor, k)] for k in (2, 1, 3)]
    else:
        partial_sums = pl.pallas_call(
            functools.partial(rows_kernel, count, n_parts, n_tensor),
            out_shape=[jax.ShapeDtypeStruct((share, width), BF16)] * n_tensor,
            in_specs=[VMEM] * (n_parts + 1),
            out_specs=[VMEM] * n_tensor,
            scratch_shapes=ids + [
                pltpu.VMEM(cots, BF16),
                pltpu.VMEM((row_count + 1, rows, 2 * side), F32),
                pltpu.SemaphoreType.DMA,
            ],
            compiler_params=params,
        )(*gathered, grad_out)
        arrived = [partial_sums[0]] + [shift(partial_sums[k], "tensor", n_tensor, k) for k in range(1, n_tensor)]
    outputs = pl.pallas_call(
        functools.partial(forward_kernel, count, per_slot, n_parts, len(tokens), n_tensor),
        out_shape=jax.ShapeDtypeStruct((rows, hidden), BF16),
        in_specs=[VMEM] * (n_parts + len(tokens)),
        out_specs=VMEM,
        scratch_shapes=[
            pltpu.VMEM((row_count + 1, rows, 2 * side), BF16),
            pltpu.VMEM((n_dp * pairs, rows, 2 * side), F32),
            pltpu.VMEM((col_count + 1, rows, 2 * side), F32),
            pltpu.VMEM((col_count + 1, rows, 2 * side), F32),
            pltpu.VMEM((rows, hidden), F32),
        ] + ([] if per_slot else ids + [pltpu.SemaphoreType.DMA]),
        compiler_params=params,
    )(*gathered, *tokens)
    if per_slot:
        grad_in = pl.pallas_call(
            functools.partial(sum_kernel, tuple(map(len, groups)), pairs, n_dp),
            out_shape=jax.ShapeDtypeStruct((share, width), BF16),
            in_specs=[VMEM] * sum(map(len, groups)),
            out_specs=VMEM,
            scratch_shapes=[pltpu.VMEM((row_count + 1, share, 2 * side), F32)] * n_tensor,
            compiler_params=params,
        )(*(message for group in groups for message in group))
        return (outputs, grad_in)
    total = arrived[0].astype(F32)
    for value in arrived[1:]:
        total = total + value.astype(F32)
    return (outputs, total.astype(BF16))


def solution(mesh):
    placed = (
        P(("dp", "tensor"), None),
        P("tensor", "dp", None, None),
        P("tensor", "dp"),
        P("dp", "tensor"),
    )
    return jax.shard_map(
        functools.partial(on_device, mesh.shape["dp"], mesh.shape["tensor"]),
        mesh=mesh,
        in_specs=placed,
        out_specs=(P("dp", "tensor"), P(("dp", "tensor"), None)),
        check_vma=False,
    )
```
